32 devices in a mesh: seq: 4 (over z), dp: 8 (over y, x, core).
Axes of the slice: x: 2, y: 2, z: 4, core: 2. Of those that a mesh axis runs over, the one named last changes fastest.
Arguments:
- media: bfloat16 [8, 2048, 1536], P('dp', 'seq'), may hold values from -6 to 6
- latents: bfloat16 [8, 64, 1536], P('dp', 'seq'), may hold values from -6 to 6
- frame_counts: int32 [8], P('dp'), may hold values from 1 to 8, as said below
- media_mask: int32 [8, 2048], P('dp'), may hold values 0 or 1
- media_gain: float32 [1536], replicated, may hold values from 0.1 to 1.9
- latent_gain: float32 [1536], replicated, may hold values from 0.1 to 1.9
- ffn_gain: float32 [1536], replicated, may hold values from 0.1 to 1.9
- w_query: bfloat16 [1536, 1536], replicated, may hold values from -0.15625 to 0.15625
- w_key: bfloat16 [1536, 1536], replicated, may hold values from -0.15625 to 0.15625
- w_value: bfloat16 [1536, 1536], replicated, may hold values from -0.15625 to 0.15625
- w_out: bfloat16 [1536, 1536], replicated, may hold values from -4 to 4
- w_up: bfloat16 [1536, 6144], replicated, may hold values from -0.15625 to 0.15625
- w_down: bfloat16 [6144, 1536], replicated, may hold values from -0.078125 to 0.078125
- cotangent: bfloat16 [8, 64, 1536], P('dp', 'seq'), may hold values from -6 to 6
Outputs:
- new_latents: bfloat16 [8, 64, 1536], P('dp', 'seq')
- media_grad: bfloat16 [8, 2048, 1536], P('dp', 'seq')
- latent_grad: bfloat16 [8, 64, 1536], P('dp', 'seq')
- grad_query: float32 [1536, 1536], P(('seq', 'dp'))
- grad_key: float32 [1536, 1536], P(('seq', 'dp'))
- grad_value: float32 [1536, 1536], P(('seq', 'dp'))
- grad_out: float32 [1536, 1536], P(('seq', 'dp'))
- grad_up: float32 [1536, 6144], P(('seq', 'dp'))
- grad_down: float32 [6144, 1536], P(('seq', 'dp'))
- grad_media_gain: float32 [1536], P(('seq', 'dp'))
- grad_latent_gain: float32 [1536], P(('seq', 'dp'))
- grad_ffn_gain: float32 [1536], P(('seq', 'dp'))
The draws below stay inside these ranges and needn't reach their ends.
Inputs may be any that keep to these rules, and one draw needn't show every extreme that they name: `frame_counts`: each item has 1 to 8 true frames; among the 1 items of each index of dp, one has all 8.
All inputs are finite; a program needn't handle non-finite values. No bound on the sum of `media_mask` on one device may be relied on, other than what follows from the above.
Results may differ from the reference program's by a relative error of at most 0.015.
Values may be sent and summed in bfloat16 or wider, within the bound.
A program may use at most 384 MiB of HBM per device.

```python
import jax
import jax.numpy as jnp
from jax import lax

D = 1536
HEADS = 16
HEAD_DIM = 96
FF = 6144
LAT = 64
FRAMES = 8
PATCH = 256
ITEMS_G = 1
ITEMS = 8
ROWS = 2048


def draw_frame_counts(key, part):
    key = jax.random.fold_in(key, 11)
    count_key, image_key, full_key = jax.random.split(key, 3)
    clip_frames = jax.random.randint(count_key, (ITEMS,), 1, FRAMES + 1)
    is_image = jax.random.randint(image_key, (ITEMS,), 0, 2) == 0
    frames = jnp.where(is_image, 1, clip_frames)
    chosen = jax.random.randint(full_key, (ITEMS // ITEMS_G,), 0, ITEMS_G)
    slot_index = jnp.arange(ITEMS, dtype=jnp.int32) % ITEMS_G
    full_item = slot_index == jnp.repeat(chosen, ITEMS_G)
    return jnp.where(full_item, FRAMES, frames).astype(jnp.int32)


def plant(values, rng, least, high):
    extent = values.shape
    spot = [jax.random.randint(jax.random.fold_in(rng, axis), (), 0, extent[axis]) for axis in range(len(extent))]
    values = values.at[tuple(spot)].set(least)
    longest = extent.index(max(extent))
    spot[longest] = (spot[longest] + 1) % extent[longest]
    return values.at[tuple(spot)].set(high)


def raised(drawn, key, source, target, blocks, factor):
    def block_of(position):
        return (jnp.arange(drawn.shape[position]) // (drawn.shape[position] // blocks)).reshape((-1,) + (1,) * (drawn.ndim - 1 - position))

    near = jax.random.permutation(key, blocks)[block_of(target)]
    other_side = (block_of(target) + blocks // 2) % blocks
    return jnp.where((block_of(source) == near) | (block_of(source) == other_side), factor * drawn, drawn)


def level_of(stream_key, extent, cuts, low, high):
    def one(dim, parts):
        draws = jax.random.uniform(jax.random.fold_in(jax.random.fold_in(stream_key, 6), dim), (parts,), jnp.float32, low / len(cuts), high / len(cuts))
        return jnp.repeat(jnp.exp(draws), extent[dim] // parts).reshape((-1,) + (1,) * (len(extent) - dim - 1))

    level = one(*cuts[0])
    for cut in cuts[1:]:
        level = level * one(*cut)
    return level


def normal_values(stream_key, extent, scale, reach, cuts=(), kind=jnp.bfloat16):
    gain = level_of(stream_key, extent, cuts, -0.22, 0.18) if cuts else 1.0
    array = jax.random.normal(stream_key, extent, jnp.float32) * scale * gain
    return jnp.minimum(jnp.maximum(array, -reach), reach).astype(kind)


def heavy_noise(own_key, extent, scale, limit, cuts, heavy, kind=jnp.bfloat16):
    values = scale * jax.random.normal(own_key, extent, jnp.float32)
    if cuts:
        values = values * level_of(own_key, extent, cuts, -0.22, 0.18)
    return jnp.clip(raised(values, jax.random.fold_in(own_key, 3), *heavy), -limit, limit).astype(kind)


def setup_inputs(seed: int = 0) -> dict:
    keys = jax.random.split(jax.random.key(seed), 15)
    media = heavy_noise(keys[0], (ITEMS, ROWS, D), 1.0, 6.0, ((0, 8), (1, 4)), (0, 2, 8, 2.0))
    latents = normal_values(keys[1], (ITEMS, LAT, D), 1.0, 6.0, ((0, 8), (1, 4)))
    frame_counts = draw_frame_counts(jax.random.fold_in(keys[14], 71), 0)
    media_mask = plant((jax.random.randint(keys[3], (ITEMS, ROWS), 0, 8) < 7).astype(jnp.int32), jax.random.fold_in(keys[3], 1), 0, 1)
    media_gain = jnp.clip(1.0 + 0.18 * jax.random.normal(keys[4], (D,), jnp.float32), 0.1, 1.9)
    latent_gain = jnp.clip(1.0 + 0.18 * jax.random.normal(keys[5], (D,), jnp.float32), 0.1, 1.9)
    ffn_gain = jnp.clip(1.0 + 0.18 * jax.random.normal(keys[6], (D,), jnp.float32), 0.1, 1.9)
    w_query = normal_values(keys[7], (D, D), D ** -0.5, 0.15625)
    w_key = normal_values(keys[8], (D, D), D ** -0.5, 0.15625)
    w_value = normal_values(keys[9], (D, D), D ** -0.5, 0.15625)
    w_out = normal_values(keys[10], (D, D), 2 ** -0.5, 4.0)
    w_up = normal_values(keys[11], (D, FF), D ** -0.5, 0.15625)
    w_down = normal_values(keys[12], (FF, D), FF ** -0.5, 0.078125)
    cotangent = heavy_noise(keys[13], (ITEMS, LAT, D), 1.0, 6.0, ((0, 8), (1, 4)), (0, 2, 8, 2.0))
    return {"media": media, "latents": latents, "frame_counts": frame_counts, "media_mask": media_mask, "media_gain": media_gain, "latent_gain": latent_gain, "ffn_gain": ffn_gain, "w_query": w_query, "w_key": w_key, "w_value": w_value, "w_out": w_out, "w_up": w_up, "w_down": w_down, "cotangent": cotangent}


MASKED_SCORE = -1e+30
HIGHEST_PREC = lax.Precision.HIGHEST

@jax.custom_vjp
def low(v):
    return lax.optimization_barrier(v.astype(jnp.bfloat16)).astype(jnp.float32)

@jax.custom_vjp
def low_back(v):
    return v

def low_keep(v):
    return (low(v), None)

def low_pass(kept, grad):
    return (grad,)

def back_keep(v):
    return (v, None)

def back_low(kept, grad):
    return (low(grad),)
low.defvjp(low_keep, low_pass)
low_back.defvjp(back_keep, back_low)

def layer_norm(tensor, gain_vec):
    centered = tensor - lax.optimization_barrier(jnp.mean(tensor, axis=-1, keepdims=True))
    spread = lax.optimization_barrier(jnp.mean(centered * centered, axis=-1, keepdims=True))
    return centered * lax.rsqrt(spread + 1e-05) * gain_vec

def matmul(left_op, right_op):
    return jnp.dot(left_op, right_op, precision=HIGHEST_PREC, preferred_element_type=jnp.float32)

def item_layer(media_item, latent_item, valid_item, params):
    media_gain, latent_gain, ffn_gain, w_query, w_key, w_value, w_out, w_up, w_down = params
    media_normed = low(layer_norm(media_item, media_gain))
    media_keys = low_back(low(matmul(media_normed, w_key)))
    media_values = low_back(low(matmul(media_normed, w_value)))
    latent_normed = low(layer_norm(latent_item, latent_gain))
    queries = low_back(low(matmul(latent_normed, w_query) * HEAD_DIM ** (-0.5)))
    latent_keys = low_back(low(matmul(latent_normed, w_key)))
    latent_values = low_back(low(matmul(latent_normed, w_value)))
    key_rows = jnp.concatenate([media_keys, latent_keys], 0).reshape(-1, HEADS, HEAD_DIM)
    value_rows = jnp.concatenate([media_values, latent_values], 0).reshape(-1, HEADS, HEAD_DIM)
    query_heads = queries.reshape(LAT, HEADS, HEAD_DIM)
    scores = low_back(jnp.einsum('qhd,khd->hqk', query_heads, key_rows, precision=HIGHEST_PREC))
    kept_keys = jnp.concatenate([valid_item, jnp.ones((LAT,), jnp.int32)], 0) > 0
    scores = jnp.where(kept_keys[None, None, :], scores, MASKED_SCORE)
    largest = lax.optimization_barrier(jnp.max(scores, axis=-1, keepdims=True))
    expo = jnp.exp(scores - largest)
    probs = low(expo / lax.optimization_barrier(jnp.sum(expo, axis=-1, keepdims=True)))
    attended = jnp.einsum('hqk,khd->qhd', probs, value_rows, precision=HIGHEST_PREC).reshape(LAT, D)
    attended = low_back(low(attended))
    mid = latent_item + low_back(matmul(attended, w_out))
    ffn_in = low(layer_norm(mid, ffn_gain))
    pre = low_back(matmul(ffn_in, w_up))
    act = low(jax.nn.gelu(pre, approximate=False))
    return mid + low_back(matmul(act, w_down))

def reference(media, latents, frame_counts, media_mask, media_gain, latent_gain, ffn_gain, w_query, w_key, w_value, w_out, w_up, w_down, cotangent):
    frame_index = jnp.arange(FRAMES * PATCH, dtype=jnp.int32) // PATCH
    valid_rows = ((media_mask > 0) & (frame_index[None, :] < frame_counts[:, None])).astype(jnp.int32)
    weights_in = tuple((tensor.astype(jnp.float32) for tensor in (media_gain, latent_gain, ffn_gain, w_query, w_key, w_value, w_out, w_up, w_down)))

    def forward(media_in, latent_in, params):

        def per_item(item_data):
            return jax.checkpoint(item_layer)(item_data[0], item_data[1], item_data[2], params)
        return lax.map(per_item, (media_in, latent_in, valid_rows))
    result, pullback = jax.vjp(forward, media.astype(jnp.float32), latents.astype(jnp.float32), weights_in)
    media_grad, latent_grad, weight_grads = pullback(cotangent.astype(jnp.float32))
    return (result.astype(jnp.bfloat16), media_grad.astype(jnp.bfloat16), latent_grad.astype(jnp.bfloat16), weight_grads[3], weight_grads[4], weight_grads[5], weight_grads[6], weight_grads[7], weight_grads[8], weight_grads[0], weight_grads[1], weight_grads[2])
```

```python
import jax
import jax.numpy as jnp
from jax import lax
from jax.sharding import PartitionSpec as P

HEAD_DIM = 96
PATCH = 256


MASKED_SCORE = -1e30


def normalize(tensor):
    centered = tensor - jnp.mean(tensor, axis=-1, keepdims=True)
    inv = lax.rsqrt(jnp.mean(centered * centered, axis=-1, keepdims=True) + 1e-05)
    return centered * inv, inv


def norm_back(grad, gain_vec, unit, inv):
    scaled = grad * gain_vec
    inner = jnp.mean(scaled * unit, axis=-1, keepdims=True)
    input_grad = inv * (scaled - jnp.mean(scaled, axis=-1, keepdims=True) - unit * inner)
    return input_grad, jnp.sum(grad * unit, axis=0)


def gelu_exact(tensor):
    return jax.nn.gelu(tensor, approximate=False)


def dot(left_op, right_op):
    return jnp.dot(left_op, right_op, preferred_element_type=jnp.float32)


def dot_t(left_op, right_op):
    return lax.dot_general(
        left_op, right_op, (((1,), (1,)), ((), ())), preferred_element_type=jnp.float32
    )


def outer_sum(left_op, right_op):
    return lax.dot_general(
        left_op, right_op, (((0,), (0,)), ((), ())), preferred_element_type=jnp.float32
    )


def split_heads(tensor):
    return tensor.reshape(tensor.shape[0], -1, HEAD_DIM)


def head_products(left_op, right_op):
    return jnp.einsum(
        "qhd,khd->hqk",
        split_heads(left_op),
        split_heads(right_op),
        preferred_element_type=jnp.float32,
    )


def weighted(weights_tab, rows):
    result = jnp.einsum(
        "hqk,khd->qhd", weights_tab, split_heads(rows), preferred_element_type=jnp.float32
    )
    return result.reshape(result.shape[0], -1)


def transposed(weights_tab, rows):
    result = jnp.einsum(
        "hqk,qhd->khd", weights_tab, split_heads(rows), preferred_element_type=jnp.float32
    )
    return result.reshape(result.shape[0], -1)


def body(
    media,
    latents,
    frame_counts,
    media_mask,
    media_gain,
    latent_gain,
    ffn_gain,
    w_query,
    w_key,
    w_value,
    w_out,
    w_up,
    w_down,
    cotangent,
):
    _, own_rows, features = media.shape
    own_lat = latents.shape[1]
    seq_parts = lax.axis_size("seq")
    seq_index = lax.axis_index("seq")
    device_count = seq_parts * lax.axis_size("dp")
    both = ("seq", "dp")
    heads = features // HEAD_DIM
    score_scale = HEAD_DIM ** (-0.5)
    bf16 = jnp.bfloat16

    media, latents, cotangent = media[0], latents[0], cotangent[0]
    own_mask = lax.dynamic_slice_in_dim(media_mask[0], seq_index * own_rows, own_rows, 0)
    row_frame = (seq_index * own_rows + jnp.arange(own_rows, dtype=jnp.int32)) // PATCH
    own_valid = (own_mask > 0) & (row_frame < frame_counts[0])
    valid = jnp.concatenate([own_valid, jnp.ones((own_lat,), jnp.bool_)])[None, None, :]

    all_cotangent = lax.all_gather(cotangent, both, axis=0, tiled=True)

    latents_f = latents.astype(jnp.float32)
    latent_unit, latent_inv = normalize(latents_f)
    latent_normed = (latent_unit * latent_gain).astype(bf16)
    own_queries = (dot(latent_normed, w_query) * score_scale).astype(bf16)
    queries = lax.all_gather(own_queries, "seq", axis=0, tiled=True)

    media_unit, media_inv = normalize(media.astype(jnp.float32))
    media_normed = (media_unit * media_gain).astype(bf16)
    rows = jnp.concatenate([media_normed, latent_normed], axis=0)
    keys = dot(rows, w_key).astype(bf16)
    values = dot(rows, w_value).astype(bf16)

    scores = jnp.where(valid, head_products(queries, keys), MASKED_SCORE)
    largest = jnp.max(scores, axis=-1)
    expo = jnp.where(valid, jnp.exp(scores - largest[..., None]), 0.0)
    total = jnp.sum(expo, axis=-1)
    part = weighted(expo.astype(bf16), values)
    packed = jnp.concatenate([part, largest.T, total.T], axis=1)
    packed = lax.all_to_all(packed, "seq", split_axis=0, concat_axis=0, tiled=True)
    packed = packed.reshape(seq_parts, own_lat, -1)
    parts = packed[..., :features]
    maxima = packed[..., features : features + heads]
    totals = packed[..., features + heads :]
    top = jnp.max(maxima, axis=0)
    factor = jnp.exp(maxima - top)
    denominator = jnp.sum(factor * totals, axis=0)
    log_total = top + jnp.log(denominator)
    share = jnp.repeat(factor / denominator, HEAD_DIM, axis=-1)
    attended_f = jnp.sum(parts * share, axis=0)
    attended = attended_f.astype(bf16)

    mid = latents_f + dot(attended, w_out)
    mid_unit, mid_inv = normalize(mid)
    ffn_in = (mid_unit * ffn_gain).astype(bf16)
    pre = dot(ffn_in, w_up)
    act = gelu_exact(pre).astype(bf16)
    new_latents = (mid + dot(act, w_down)).astype(bf16)
    act_grad = dot_t(cotangent, w_down)
    pre_grad = jax.vjp(gelu_exact, pre)[1](act_grad)[0].astype(bf16)
    all_pre_grad = lax.all_gather(pre_grad, both, axis=0, tiled=True)
    ffn_in_grad = dot_t(pre_grad, w_up)
    mid_back, grad_ffn_gain = norm_back(ffn_in_grad, ffn_gain, mid_unit, mid_inv)
    mid_grad = cotangent.astype(jnp.float32) + mid_back
    branch_grad = mid_grad.astype(bf16)
    all_branch = lax.all_gather(branch_grad, both, axis=0, tiled=True)
    attended_grad = dot_t(branch_grad, w_out).astype(bf16)
    own_delta = jnp.sum(
        split_heads(attended_f * attended_grad.astype(jnp.float32)), axis=-1
    )
    out_grad = lax.all_gather(attended_grad, "seq", axis=0, tiled=True)
    stats = lax.all_gather(
        jnp.concatenate([log_total, own_delta], axis=1), "seq", axis=0, tiled=True
    )
    lse = stats[:, :heads].T[..., None]
    delta = stats[:, heads:].T[..., None]

    exact = jnp.where(valid, jnp.exp(scores - lse), 0.0)
    score_grad = (exact * (head_products(out_grad, values) - delta)).astype(bf16)
    value_grad = transposed(exact.astype(bf16), out_grad).astype(bf16)
    key_grad = transposed(score_grad, queries).astype(bf16)
    query_part = weighted(score_grad, keys)
    query_grad = lax.psum_scatter(
        query_part, "seq", scatter_dimension=0, tiled=True
    ).astype(bf16)
    all_query_grad = lax.all_gather(query_grad, both, axis=0, tiled=True)
    part_value = outer_sum(rows, value_grad).astype(bf16)
    part_key = outer_sum(rows, key_grad).astype(bf16)
    sum_value = lax.psum_scatter(part_value, both, scatter_dimension=0, tiled=True)
    sum_key = lax.psum_scatter(part_key, both, scatter_dimension=0, tiled=True)

    rows_grad = dot_t(key_grad, w_key) + dot_t(value_grad, w_value)
    media_back, grad_media_gain = norm_back(
        rows_grad[:own_rows], media_gain, media_unit, media_inv
    )
    media_grad = media_back.astype(bf16)
    latent_normed_grad = rows_grad[own_rows:] + dot_t(query_grad, w_query) * score_scale
    latent_back, grad_latent_gain = norm_back(
        latent_normed_grad, latent_gain, latent_unit, latent_inv
    )
    latent_grad = (mid_grad + latent_back).astype(bf16)

    def by_owner(tensor):
        return tensor.reshape(tensor.shape[0], device_count, -1)

    sent = jnp.concatenate(
        [by_owner(latent_normed), by_owner(attended), by_owner(ffn_in), by_owner(act)], axis=2
    )
    got = lax.all_to_all(sent, both, split_axis=1, concat_axis=0, tiled=True)
    got = got.reshape(-1, got.shape[-1])
    block = features // device_count
    grad_query = outer_sum(got[:, :block], all_query_grad) * score_scale
    grad_out = outer_sum(got[:, block : 2 * block], all_branch)
    grad_up = outer_sum(got[:, 2 * block : 3 * block], all_pre_grad)
    grad_down = outer_sum(got[:, 3 * block :], all_cotangent)

    gains = jnp.stack([grad_media_gain, grad_latent_gain, grad_ffn_gain])
    gains = by_owner(gains).transpose(1, 0, 2).reshape(device_count, -1)
    gains = lax.all_to_all(gains, both, split_axis=0, concat_axis=0, tiled=True)
    gains = jnp.sum(gains.reshape(device_count, 3, -1), axis=0)
    return (
        new_latents[None],
        media_grad[None],
        latent_grad[None],
        grad_query,
        sum_key.astype(jnp.float32),
        sum_value.astype(jnp.float32),
        grad_out,
        grad_up,
        grad_down,
        gains[0],
        gains[1],
        gains[2],
    )


def solution(mesh):
    return jax.shard_map(
        body,
        mesh=mesh,
        in_specs=(
            P("dp", "seq", None),
            P("dp", "seq", None),
            P("dp"),
            P("dp", None),
            P(),
            P(),
            P(),
            P(),
            P(),
            P(),
            P(),
            P(),
            P(),
            P("dp", "seq", None),
        ),
        out_specs=(
            P("dp", "seq", None),
            P("dp", "seq", None),
            P("dp", "seq", None),
            P(("seq", "dp"), None),
            P(("seq", "dp"), None),
            P(("seq", "dp"), None),
            P(("seq", "dp"), None),
            P(("seq", "dp"), None),
            P(("seq", "dp"), None),
            P(("seq", "dp")),
            P(("seq", "dp")),
            P(("seq", "dp")),
        ),
        check_vma=False,
    )
```

```python
import jax
import jax.numpy as jnp
from jax import lax
from jax.experimental import pallas as pl
from jax.experimental.pallas import tpu as pltpu
from jax.sharding import PartitionSpec as P

HEAD_DIM = 96
PATCH = 256


MASKED_SCORE = -1e30


def normalize(tensor):
    centered = tensor - jnp.mean(tensor, axis=-1, keepdims=True)
    inv = lax.rsqrt(jnp.mean(centered * centered, axis=-1, keepdims=True) + 1e-05)
    return centered * inv, inv


def norm_back(grad, gain_vec, unit, inv):
    scaled = grad * gain_vec
    inner = jnp.mean(scaled * unit, axis=-1, keepdims=True)
    input_grad = inv * (scaled - jnp.mean(scaled, axis=-1, keepdims=True) - unit * inner)
    return input_grad, jnp.sum(grad * unit, axis=0)


def gelu_exact(tensor):
    return jax.nn.gelu(tensor, approximate=False)


def dot(left_op, right_op):
    return jnp.dot(left_op, right_op, preferred_element_type=jnp.float32)


def dot_t(left_op, right_op):
    return lax.dot_general(
        left_op, right_op, (((1,), (1,)), ((), ())), preferred_element_type=jnp.float32
    )


def outer_sum(left_op, right_op):
    return lax.dot_general(
        left_op, right_op, (((0,), (0,)), ((), ())), preferred_element_type=jnp.float32
    )


def split_heads(tensor):
    return tensor.reshape(tensor.shape[0], -1, HEAD_DIM)


def head_products(left_op, right_op):
    return jnp.einsum(
        "qhd,khd->hqk",
        split_heads(left_op),
        split_heads(right_op),
        preferred_element_type=jnp.float32,
    )


def weighted(weights_tab, rows):
    result = jnp.einsum(
        "hqk,khd->qhd", weights_tab, split_heads(rows), preferred_element_type=jnp.float32
    )
    return result.reshape(result.shape[0], -1)


def transposed(weights_tab, rows):
    result = jnp.einsum(
        "hqk,qhd->khd", weights_tab, split_heads(rows), preferred_element_type=jnp.float32
    )
    return result.reshape(result.shape[0], -1)


MESH = pl.DeviceIdType.MESH
GROUP = 4
SPAN = GROUP * HEAD_DIM


def tail_kernel(
    rows_ref,
    keys_ref,
    values_ref,
    queries_ref,
    out_grad_ref,
    stats_ref,
    valid_ref,
    media_ref,
    media_gain_ref,
    latents_ref,
    latent_gain_ref,
    mid_grad_ref,
    ffn_gain_grad_ref,
    attended_ref,
    w_query_ref,
    w_key_ref,
    w_value_ref,
    media_grad_ref,
    latent_grad_ref,
    grad_query_ref,
    grad_key_ref,
    grad_value_ref,
    grad_out_ref,
    gains_ref,
    rows_t,
    lat_t,
    att_t,
    key_grad,
    value_grad,
    rows_grad,
    first_w,
    second_w,
    query_parts,
    pair_send,
    pair_recv,
    own,
    one_recv,
    two_recv,
    line_recv,
    line_own,
    lat_all,
    att_all,
    branch_parts,
    branch_send,
    query_send,
    query_recv,
    back_send,
    back_recv,
    gain_send,
    gain_recv,
    w_sems,
    pair_sems,
    one_sems,
    two_sems,
    line_sems,
    small_sems,
    gain_sems,
):
    bf16, f32 = jnp.bfloat16, jnp.float32
    z = lax.axis_index("seq")
    d = lax.axis_index("dp")
    y, x, c = d // 4, (d // 2) % 2, d % 2
    own_lat = latents_ref.shape[0]
    own_rows = media_ref.shape[0]
    features = media_ref.shape[1]
    groups = features // SPAN
    scale = HEAD_DIM ** (-0.5)
    pair_dev = (z, d + 1 - 2 * c)
    x_dev = (z, d + 2 * (1 - 2 * x))
    y_dev = (z, d + 4 * (1 - 2 * y))
    peers = [(z + k) % 4 for k in (1, 2, 3)]

    def copy_to(src, dst, sems, index, device):
        return pltpu.make_async_remote_copy(
            src_ref=src,
            dst_ref=dst,
            send_sem=sems.at[(0,) + index],
            recv_sem=sems.at[(1,) + index],
            device_id=device,
            device_id_type=MESH,
        )

    load_key = pltpu.make_async_copy(w_key_ref, first_w, w_sems.at[0])
    load_value = pltpu.make_async_copy(w_value_ref, second_w, w_sems.at[1])
    load_key.start()
    load_value.start()

    barrier = pltpu.get_barrier_semaphore()
    for device in [pair_dev, x_dev, y_dev] + [(p, d) for p in peers]:
        pl.semaphore_signal(barrier, inc=1, device_id=device, device_id_type=MESH)
    pl.semaphore_wait(barrier, 6)

    lat_all[z] = rows_ref[own_rows:, :]
    att_all[z] = attended_ref[...]
    branch = mid_grad_ref[...].astype(bf16)
    for quarter in range(4):
        branch_send[quarter] = branch[:, quarter * SPAN : (quarter + 1) * SPAN]
    branch_parts[z] = branch_send[z]
    spread = []
    for k, p in enumerate(peers):
        spread.append(copy_to(lat_all.at[z], lat_all.at[z], small_sems, (0, k), (p, d)))
        spread.append(copy_to(att_all.at[z], att_all.at[z], small_sems, (1, k), (p, d)))
        spread.append(
            copy_to(branch_send.at[p], branch_parts.at[z], small_sems, (2, k), (p, d))
        )
    for item in spread:
        item.start()

    def place_transposed(dest, tile, column):
        for piece in range(8):
            row = column + 16 * piece
            block, off = row // 48, row % 48
            bz, by, bx, bc = block // 8, (block // 4) % 2, (block // 2) % 2, block % 2
            at = bx * 384 + by * 192 + bz * 48 + off
            dest[bc, at : at + 16, :] = tile[16 * piece : 16 * piece + 16, :]

    for j in range(features // 128):
        tile = rows_ref[:, 128 * j : 128 * j + 128].astype(f32).T.astype(bf16)
        place_transposed(rows_t, tile, 128 * j)

    lane = lax.broadcasted_iota(jnp.int32, (64, SPAN), 1)
    head_masks = [(lane >= h * HEAD_DIM) & (lane < (h + 1) * HEAD_DIM) for h in range(GROUP)]

    def stacked(tensor):
        return jnp.concatenate(
            [jnp.where(mask, tensor, jnp.zeros_like(tensor)) for mask in head_masks], axis=0
        )

    def send_pair(ch, left, right, factor=None):
        for half in range(2):
            part = dot(left[1 - c, half * 384 : (half + 1) * 384, :], right)
            if factor is not None:
                part = part * factor
            pair_send[ch, half * 384 : (half + 1) * 384, :] = part.astype(bf16)
        copy = copy_to(pair_send.at[ch], pair_recv.at[ch], pair_sems, (ch,), pair_dev)
        copy.start()
        slot = ch % 6
        for half in range(2):
            part = dot(left[c, half * 384 : (half + 1) * 384, :], right)
            if factor is not None:
                part = part * factor
            own[slot, half] = part.reshape(2, 192, SPAN)
        return copy

    flights = {}

    def compute_group(g):
        cols = slice(g * SPAN, (g + 1) * SPAN)
        key_g = keys_ref[:, cols]
        value_g = values_ref[:, cols]
        q_stack = stacked(queries_ref[:, cols])
        o_stack = stacked(out_grad_ref[:, cols])
        scores = dot_t(key_g, q_stack)
        keep = valid_ref[...] > 0.0
        exact = jnp.where(keep, jnp.exp(scores - stats_ref[g : g + 1, :]), 0.0)
        prob_grad = dot_t(value_g, o_stack)
        score_grad = (exact * (prob_grad - stats_ref[4 + g : 5 + g, :])).astype(bf16)
        v_grad = dot(exact.astype(bf16), o_stack).astype(bf16)
        value_grad[:, cols] = v_grad
        flights["pair", 2 * g] = send_pair(2 * g, rows_t, v_grad)
        k_grad = dot(score_grad, q_stack).astype(bf16)
        key_grad[:, cols] = k_grad
        flights["pair", 2 * g + 1] = send_pair(2 * g + 1, rows_t, k_grad)
        q_part = outer_sum(score_grad, key_g)
        q_sum = jnp.zeros((64, SPAN), f32)
        for h in range(GROUP):
            q_sum = q_sum + jnp.where(head_masks[h], q_part[64 * h : 64 * h + 64], 0.0)
        query_parts[g] = q_sum
        query_send[g] = q_sum.astype(bf16)

    def pair_sum(k):
        for ch in (2 * k, 2 * k + 1):
            flights["pair", ch].wait()
            slot = ch % 6
            for bx in range(2):
                for by in range(2):
                    at = bx * 384 + by * 192
                    own[slot, bx, by] += pair_recv[ch, at : at + 192, :].astype(f32)
            if ch % 2 == 0:
                theirs, device = own[slot, 1 - x], x_dev
            else:
                theirs, device = own[slot, :, 1 - y], y_dev
            pair_send[ch, 0:384, :] = theirs.reshape(384, SPAN).astype(bf16)
            copy = copy_to(
                pair_send.at[ch, pl.ds(0, 384)], one_recv.at[ch], one_sems, (ch,), device
            )
            copy.start()
            flights["one", ch] = copy

    def one_sum(k):
        for ch in (2 * k, 2 * k + 1):
            flights["one", ch].wait()
            slot = ch % 6
            if ch % 2 == 0:
                for by in range(2):
                    own[slot, x, by] += one_recv[ch, by * 192 : by * 192 + 192, :].astype(f32)
                theirs, device = own[slot, x, 1 - y], y_dev
            else:
                for bx in range(2):
                    own[slot, bx, y] += one_recv[ch, bx * 192 : bx * 192 + 192, :].astype(f32)
                theirs, device = own[slot, 1 - x, y], x_dev
            pair_send[ch, 384:576, :] = theirs.astype(bf16)
            copy = copy_to(
                pair_send.at[ch, pl.ds(384, 192)], two_recv.at[ch], two_sems, (ch,), device
            )
            copy.start()
            flights["two", ch] = copy

    def two_sum(k):
        for ch in (2 * k, 2 * k + 1):
            flights["two", ch].wait()
            slot = ch % 6
            total = own[slot, x, y] + two_recv[ch].astype(f32)
            own[slot, x, y] = total
            pair_send[ch, 576:768, :] = total.astype(bf16)
            line_own[ch] = own[slot, x, y, pl.ds(pl.multiple_of(z * 48, 16), 48), :]
            copies = []
            for j, p in enumerate(peers):
                copies.append(
                    copy_to(
                        pair_send.at[ch, pl.ds(pl.multiple_of(576 + p * 48, 16), 48)],
                        line_recv.at[ch, z],
                        line_sems,
                        (ch, j),
                        (p, d),
                    )
                )
            for copy in copies:
                copy.start()
            flights["line", ch] = copies

    def line_sum(k):
        for ch in (2 * k, 2 * k + 1):
            for copy in flights["line", ch]:
                copy.wait()
            if k < groups:
                total = line_own[ch]
                for p in peers:
                    total = total + line_recv[ch, p].astype(f32)
                dest = grad_value_ref if ch % 2 == 0 else grad_key_ref
                dest[:, k * SPAN : (k + 1) * SPAN] = total
            else:
                dest = grad_out_ref if ch % 2 == 0 else grad_query_ref
                line_recv[ch, z] = line_own[ch].astype(bf16)
                for quarter in range(4):
                    dest[:, quarter * SPAN : (quarter + 1) * SPAN] = line_recv[
                        ch, quarter
                    ].astype(f32)

    compute_group(0)
    pair_sum(0)
    compute_group(1)
    pair_sum(1)
    one_sum(0)
    compute_group(2)
    pair_sum(2)
    one_sum(1)
    two_sum(0)
    compute_group(3)
    pair_sum(3)
    one_sum(2)
    two_sum(1)
    line_sum(0)

    to_quarter = [
        copy_to(query_send.at[p], query_recv.at[z], small_sems, (3, k), (p, d))
        for k, p in enumerate(peers)
    ]
    for item in to_quarter:
        item.start()
    for item in spread:
        item.wait()
    for j in range(features // 128):
        cols = slice(128 * j, 128 * j + 128)
        tile = lat_all[:, :, cols].reshape(64, 128).astype(f32).T.astype(bf16)
        place_transposed(lat_t, tile, 128 * j)
        tile = att_all[:, :, cols].reshape(64, 128).astype(f32).T.astype(bf16)
        place_transposed(att_t, tile, 128 * j)
    last = 2 * groups
    flights["pair", last] = send_pair(last, att_t, branch_parts[...].reshape(64, SPAN))
    for item in to_quarter:
        item.wait()
    query_quarter = query_parts[z]
    for p in peers:
        query_quarter = query_quarter + query_recv[p].astype(f32)
    query_quarter = query_quarter.astype(bf16)
    back_send[...] = query_quarter.reshape(4, own_lat, SPAN)
    back_recv[z] = back_send[z]
    to_rows = [
        copy_to(back_send.at[p], back_recv.at[z], small_sems, (4, k), (p, d))
        for k, p in enumerate(peers)
    ]
    for item in to_rows:
        item.start()
    flights["pair", last + 1] = send_pair(last + 1, lat_t, query_quarter, scale)
    pair_sum(4)
    one_sum(3)
    two_sum(2)
    line_sum(1)

    load_key.wait()
    load_value.wait()

    def back_step(n, carry):
        at = pl.ds(pl.multiple_of(n * SPAN, SPAN), SPAN)
        rows_grad[:, at] = dot_t(key_grad[...], first_w[at, :]) + dot_t(
            value_grad[...], second_w[at, :]
        )
        return carry

    lax.fori_loop(0, groups, back_step, 0)
    load_query = pltpu.make_async_copy(w_query_ref, first_w, w_sems.at[2])
    load_query.start()
    one_sum(4)
    two_sum(3)
    line_sum(2)

    def norm_parts(block):
        block = block.astype(f32)
        centered = block - jnp.mean(block, axis=-1, keepdims=True)
        inv = lax.rsqrt(jnp.mean(centered * centered, axis=-1, keepdims=True) + 1e-05)
        return centered * inv, inv

    def input_grad(grad, gain, unit, inv):
        scaled = grad * gain
        inner = jnp.mean(scaled * unit, axis=-1, keepdims=True)
        return inv * (scaled - jnp.mean(scaled, axis=-1, keepdims=True) - unit * inner)

    def norm_step(n, total):
        at = pl.ds(pl.multiple_of(n * 64, 64), 64)
        unit, inv = norm_parts(media_ref[at, :])
        grad = rows_grad[at, :]
        media_grad_ref[at, :] = input_grad(grad, media_gain_ref[...], unit, inv).astype(bf16)
        return total + jnp.sum(grad * unit, axis=0, keepdims=True)

    gain_total = lax.fori_loop(0, own_rows // 64, norm_step, jnp.zeros((1, features), f32))

    for item in to_rows:
        item.wait()
    load_query.wait()
    lat_grad = rows_grad[own_rows:, :]
    for quarter in range(4):
        lat_grad = lat_grad + scale * dot_t(
            back_recv[quarter], first_w[:, quarter * SPAN : (quarter + 1) * SPAN]
        )
    unit, inv = norm_parts(latents_ref[...])
    latent_grad_ref[...] = (
        mid_grad_ref[...] + input_grad(lat_grad, latent_gain_ref[...], unit, inv)
    ).astype(bf16)
    latent_total = jnp.sum(lat_grad * unit, axis=0, keepdims=True)
    gain_send[0] = jnp.concatenate(
        [gain_total, latent_total, ffn_gain_grad_ref[...], jnp.zeros((5, features), f32)], axis=0
    )
    hops = [pair_dev, x_dev, y_dev]

    def gain_hop(hop):
        return copy_to(
            gain_send.at[hop], gain_recv.at[hop], gain_sems, (hop,), hops[hop]
        )

    first_hop = gain_hop(0)
    first_hop.start()
    two_sum(4)
    line_sum(3)
    first_hop.wait()
    gain_send[1] = gain_send[0] + gain_recv[0]
    second_hop = gain_hop(1)
    second_hop.start()
    second_hop.wait()
    gain_send[2] = gain_send[1] + gain_recv[1]
    third_hop = gain_hop(2)
    third_hop.start()
    third_hop.wait()
    gain_send[3] = gain_send[2] + gain_recv[2]
    lines = [
        copy_to(gain_send.at[3], gain_recv.at[3 + z], gain_sems, (3 + k,), (p, d))
        for k, p in enumerate(peers)
    ]
    for item in lines:
        item.start()
    line_sum(4)
    for item in lines:
        item.wait()
    total = gain_send[3]
    for p in peers:
        total = total + gain_recv[3 + p]
    gains_ref[...] = total


def tail(operands, own_rows, own_lat, features):
    bf16, f32 = jnp.bfloat16, jnp.float32
    count = own_rows + own_lat
    chunks = 2 * (features // SPAN) + 2
    vmem = pl.BlockSpec(memory_space=pltpu.VMEM)
    anyway = pl.BlockSpec(memory_space=pl.ANY)
    share = features // 32
    return pl.pallas_call(
        tail_kernel,
        out_shape=(
            jax.ShapeDtypeStruct((own_rows, features), bf16),
            jax.ShapeDtypeStruct((own_lat, features), bf16),
            jax.ShapeDtypeStruct((share, features), f32),
            jax.ShapeDtypeStruct((share, features), f32),
            jax.ShapeDtypeStruct((share, features), f32),
            jax.ShapeDtypeStruct((share, features), f32),
            jax.ShapeDtypeStruct((8, features), f32),
        ),
        in_specs=[vmem] * 14 + [anyway] * 3,
        out_specs=(vmem,) * 7,
        scratch_shapes=[
            pltpu.VMEM((2, features // 2, count), bf16),
            pltpu.VMEM((2, features // 2, 64), bf16),
            pltpu.VMEM((2, features // 2, 64), bf16),
            pltpu.VMEM((count, features), bf16),
            pltpu.VMEM((count, features), bf16),
            pltpu.VMEM((count, features), f32),
            pltpu.VMEM((features, features), bf16),
            pltpu.VMEM((features, features), bf16),
            pltpu.VMEM((4, 64, SPAN), f32),
            pltpu.VMEM((chunks, 768, SPAN), bf16),
            pltpu.VMEM((chunks, 768, SPAN), bf16),
            pltpu.VMEM((6, 2, 2, 192, SPAN), f32),
            pltpu.VMEM((chunks, 384, SPAN), bf16),
            pltpu.VMEM((chunks, 192, SPAN), bf16),
            pltpu.VMEM((chunks, 4, 48, SPAN), bf16),
            pltpu.VMEM((chunks, 48, SPAN), f32),
            pltpu.VMEM((4, own_lat, features), bf16),
            pltpu.VMEM((4, own_lat, features), bf16),
            pltpu.VMEM((4, own_lat, SPAN), bf16),
            pltpu.VMEM((4, own_lat, SPAN), bf16),
            pltpu.VMEM((4, 64, SPAN), bf16),
            pltpu.VMEM((4, 64, SPAN), bf16),
            pltpu.VMEM((4, own_lat, SPAN), bf16),
            pltpu.VMEM((4, own_lat, SPAN), bf16),
            pltpu.VMEM((4, 8, features), f32),
            pltpu.VMEM((7, 8, features), f32),
            pltpu.SemaphoreType.DMA((3,)),
            pltpu.SemaphoreType.DMA((2, chunks)),
            pltpu.SemaphoreType.DMA((2, chunks)),
            pltpu.SemaphoreType.DMA((2, chunks)),
            pltpu.SemaphoreType.DMA((2, chunks, 3)),
            pltpu.SemaphoreType.DMA((2, 5, 3)),
            pltpu.SemaphoreType.DMA((2, 6)),
        ],
        compiler_params=pltpu.CompilerParams(
            collective_id=0, has_side_effects=True, vmem_limit_bytes=62 * 1024 * 1024
        ),
    )(*operands)


def body(
    media,
    latents,
    frame_counts,
    media_mask,
    media_gain,
    latent_gain,
    ffn_gain,
    w_query,
    w_key,
    w_value,
    w_out,
    w_up,
    w_down,
    cotangent,
):
    _, own_rows, features = media.shape
    own_lat = latents.shape[1]
    seq_parts = lax.axis_size("seq")
    seq_index = lax.axis_index("seq")
    device_count = seq_parts * lax.axis_size("dp")
    both = ("seq", "dp")
    heads = features // HEAD_DIM
    score_scale = HEAD_DIM ** (-0.5)
    bf16 = jnp.bfloat16

    media, latents, cotangent = media[0], latents[0], cotangent[0]
    own_mask = lax.dynamic_slice_in_dim(media_mask[0], seq_index * own_rows, own_rows, 0)
    row_frame = (seq_index * own_rows + jnp.arange(own_rows, dtype=jnp.int32)) // PATCH
    own_valid = (own_mask > 0) & (row_frame < frame_counts[0])
    valid = jnp.concatenate([own_valid, jnp.ones((own_lat,), jnp.bool_)])[None, None, :]

    all_cotangent = lax.all_gather(cotangent, both, axis=0, tiled=True)

    latents_f = latents.astype(jnp.float32)
    latent_unit, latent_inv = normalize(latents_f)
    latent_normed = (latent_unit * latent_gain).astype(bf16)
    own_queries = (dot(latent_normed, w_query) * score_scale).astype(bf16)
    queries = lax.all_gather(own_queries, "seq", axis=0, tiled=True)

    media_unit, media_inv = normalize(media.astype(jnp.float32))
    media_normed = (media_unit * media_gain).astype(bf16)
    rows = jnp.concatenate([media_normed, latent_normed], axis=0)
    keys = dot(rows, w_key).astype(bf16)
    values = dot(rows, w_value).astype(bf16)

    scores = jnp.where(valid, head_products(queries, keys), MASKED_SCORE)
    largest = jnp.max(scores, axis=-1)
    expo = jnp.where(valid, jnp.exp(scores - largest[..., None]), 0.0)
    total = jnp.sum(expo, axis=-1)
    part = weighted(expo.astype(bf16), values)
    packed = jnp.concatenate([part, largest.T, total.T], axis=1)
    packed = lax.all_to_all(packed, "seq", split_axis=0, concat_axis=0, tiled=True)
    packed = packed.reshape(seq_parts, own_lat, -1)
    parts = packed[..., :features]
    maxima = packed[..., features : features + heads]
    totals = packed[..., features + heads :]
    top = jnp.max(maxima, axis=0)
    factor = jnp.exp(maxima - top)
    denominator = jnp.sum(factor * totals, axis=0)
    log_total = top + jnp.log(denominator)
    share = jnp.repeat(factor / denominator, HEAD_DIM, axis=-1)
    attended_f = jnp.sum(parts * share, axis=0)
    attended = attended_f.astype(bf16)

    mid = latents_f + dot(attended, w_out)
    mid_unit, mid_inv = normalize(mid)
    ffn_in = (mid_unit * ffn_gain).astype(bf16)
    pre = dot(ffn_in, w_up)
    act = gelu_exact(pre).astype(bf16)
    new_latents = (mid + dot(act, w_down)).astype(bf16)
    act_grad = dot_t(cotangent, w_down)
    pre_grad = jax.vjp(gelu_exact, pre)[1](act_grad)[0].astype(bf16)
    all_pre_grad = lax.all_gather(pre_grad, both, axis=0, tiled=True)
    ffn_in_grad = dot_t(pre_grad, w_up)
    mid_back, grad_ffn_gain = norm_back(ffn_in_grad, ffn_gain, mid_unit, mid_inv)
    mid_grad = cotangent.astype(jnp.float32) + mid_back
    branch_grad = mid_grad.astype(bf16)
    attended_grad = dot_t(branch_grad, w_out).astype(bf16)
    own_delta = jnp.sum(
        split_heads(attended_f * attended_grad.astype(jnp.float32)), axis=-1
    )
    out_grad = lax.all_gather(attended_grad, "seq", axis=0, tiled=True)
    stats = lax.all_gather(
        jnp.concatenate([log_total, own_delta], axis=1), "seq", axis=0, tiled=True
    )
    lse = stats[:, :heads].T[..., None]
    delta = stats[:, heads:].T[..., None]

    fast = lax.axis_size("dp") == 8 and seq_parts == 4 and own_lat == 16 and features == 4 * SPAN
    if fast:
        operands = (
            rows,
            keys,
            values,
            queries,
            out_grad,
            jnp.concatenate([lse.reshape(4, -1), delta.reshape(4, -1)], axis=0),
            valid.reshape(-1, 1).astype(jnp.float32),
            media,
            media_gain[None],
            latents,
            latent_gain[None],
            mid_grad,
            grad_ffn_gain[None],
            attended,
            w_query,
            w_key,
            w_value,
        )
        media_grad, latent_grad, grad_query, sum_key, sum_value, grad_out, gain_sums = tail(
            operands, own_rows, own_lat, features
        )
    else:
        exact = jnp.where(valid, jnp.exp(scores - lse), 0.0)
        score_grad = (exact * (head_products(out_grad, values) - delta)).astype(bf16)
        value_grad = transposed(exact.astype(bf16), out_grad).astype(bf16)
        key_grad = transposed(score_grad, queries).astype(bf16)
        query_part = weighted(score_grad, keys)
        query_grad = lax.psum_scatter(
            query_part, "seq", scatter_dimension=0, tiled=True
        ).astype(bf16)
        all_branch = lax.all_gather(branch_grad, both, axis=0, tiled=True)
        all_query_grad = lax.all_gather(query_grad, both, axis=0, tiled=True)
        part_value = outer_sum(rows, value_grad).astype(bf16)
        part_key = outer_sum(rows, key_grad).astype(bf16)
        sum_value = lax.psum_scatter(part_value, both, scatter_dimension=0, tiled=True)
        sum_key = lax.psum_scatter(part_key, both, scatter_dimension=0, tiled=True)

        rows_grad = dot_t(key_grad, w_key) + dot_t(value_grad, w_value)
        media_back, grad_media_gain = norm_back(
            rows_grad[:own_rows], media_gain, media_unit, media_inv
        )
        media_grad = media_back.astype(bf16)
        latent_normed_grad = rows_grad[own_rows:] + dot_t(query_grad, w_query) * score_scale
        latent_back, grad_latent_gain = norm_back(
            latent_normed_grad, latent_gain, latent_unit, latent_inv
        )
        latent_grad = (mid_grad + latent_back).astype(bf16)

    def by_owner(tensor):
        return tensor.reshape(tensor.shape[0], device_count, -1)

    block = features // device_count
    if fast:
        sent = jnp.concatenate([by_owner(ffn_in), by_owner(act)], axis=2)
    else:
        sent = jnp.concatenate(
            [by_owner(ffn_in), by_owner(act), by_owner(latent_normed), by_owner(attended)], axis=2
        )
    got = lax.all_to_all(sent, both, split_axis=1, concat_axis=0, tiled=True)
    got = got.reshape(-1, got.shape[-1])
    grad_up = outer_sum(got[:, :block], all_pre_grad)
    ff_block = act.shape[1] // device_count
    grad_down = outer_sum(got[:, block : block + ff_block], all_cotangent)
    if fast:
        place = seq_index * lax.axis_size("dp") + lax.axis_index("dp")
        gains = lax.dynamic_slice_in_dim(gain_sums[:3], place * block, block, 1)
    else:
        at = block + ff_block
        grad_query = outer_sum(got[:, at : at + block], all_query_grad) * score_scale
        grad_out = outer_sum(got[:, at + block :], all_branch)
        gains = jnp.stack([grad_media_gain, grad_latent_gain, grad_ffn_gain])
        gains = by_owner(gains).transpose(1, 0, 2).reshape(device_count, -1)
        gains = lax.all_to_all(gains, both, split_axis=0, concat_axis=0, tiled=True)
        gains = jnp.sum(gains.reshape(device_count, 3, -1), axis=0)
    return (
        new_latents[None],
        media_grad[None],
        latent_grad[None],
        grad_query,
        sum_key.astype(jnp.float32),
        sum_value.astype(jnp.float32),
        grad_out,
        grad_up,
        grad_down,
        gains[0],
        gains[1],
        gains[2],
    )


def solution(mesh):
    return jax.shard_map(
        body,
        mesh=mesh,
        in_specs=(
            P("dp", "seq", None),
            P("dp", "seq", None),
            P("dp"),
            P("dp", None),
            P(),
            P(),
            P(),
            P(),
            P(),
            P(),
            P(),
            P(),
            P(),
            P("dp", "seq", None),
        ),
        out_specs=(
            P("dp", "seq", None),
            P("dp", "seq", None),
            P("dp", "seq", None),
            P(("seq", "dp"), None),
            P(("seq", "dp"), None),
            P(("seq", "dp"), None),
            P(("seq", "dp"), None),
            P(("seq", "dp"), None),
            P(("seq", "dp"), None),
            P(("seq", "dp")),
            P(("seq", "dp")),
            P(("seq", "dp")),
        ),
        check_vma=False,
    )
```

```python
import jax
import jax.numpy as jnp
from jax import lax
from jax.experimental import pallas as pl
from jax.experimental.pallas import tpu as pltpu
from jax.sharding import PartitionSpec as P

HEAD_DIM = 96
PATCH = 256


MASKED_SCORE = -1e30


def normalize(tensor):
    centered = tensor - jnp.mean(tensor, axis=-1, keepdims=True)
    inv = lax.rsqrt(jnp.mean(centered * centered, axis=-1, keepdims=True) + 1e-05)
    return centered * inv, inv


def norm_back(grad, gain_vec, unit, inv):
    scaled = grad * gain_vec
    inner = jnp.mean(scaled * unit, axis=-1, keepdims=True)
    input_grad = inv * (scaled - jnp.mean(scaled, axis=-1, keepdims=True) - unit * inner)
    return input_grad, jnp.sum(grad * unit, axis=0)


def gelu_exact(tensor):
    return jax.nn.gelu(tensor, approximate=False)


def dot(left_op, right_op):
    return jnp.dot(left_op, right_op, preferred_element_type=jnp.float32)


def dot_t(left_op, right_op):
    return lax.dot_general(
        left_op, right_op, (((1,), (1,)), ((), ())), preferred_element_type=jnp.float32
    )


def outer_sum(left_op, right_op):
    return lax.dot_general(
        left_op, right_op, (((0,), (0,)), ((), ())), preferred_element_type=jnp.float32
    )


def split_heads(tensor):
    return tensor.reshape(tensor.shape[0], -1, HEAD_DIM)


def head_products(left_op, right_op):
    return jnp.einsum(
        "qhd,khd->hqk",
        split_heads(left_op),
        split_heads(right_op),
        preferred_element_type=jnp.float32,
    )


def weighted(weights_tab, rows):
    result = jnp.einsum(
        "hqk,khd->qhd", weights_tab, split_heads(rows), preferred_element_type=jnp.float32
    )
    return result.reshape(result.shape[0], -1)


def transposed(weights_tab, rows):
    result = jnp.einsum(
        "hqk,qhd->khd", weights_tab, split_heads(rows), preferred_element_type=jnp.float32
    )
    return result.reshape(result.shape[0], -1)


MESH = pl.DeviceIdType.MESH
GROUP = 4
SPAN = GROUP * HEAD_DIM


def norm_parts(block):
    block = block.astype(jnp.float32)
    centered = block - jnp.mean(block, axis=-1, keepdims=True)
    inv = lax.rsqrt(jnp.mean(centered * centered, axis=-1, keepdims=True) + 1e-05)
    return centered * inv, inv


def input_grad(grad, gain, unit, inv):
    scaled = grad * gain
    inner = jnp.mean(scaled * unit, axis=-1, keepdims=True)
    return inv * (scaled - jnp.mean(scaled, axis=-1, keepdims=True) - unit * inner)


def head_masks(count):
    lane = lax.broadcasted_iota(jnp.int32, (count, SPAN), 1)
    return [(lane >= h * HEAD_DIM) & (lane < (h + 1) * HEAD_DIM) for h in range(GROUP)]


def stacked(tensor, masks):
    return jnp.concatenate(
        [jnp.where(mask, tensor, jnp.zeros_like(tensor)) for mask in masks], axis=0
    )


def copy_to(src, dst, sems, index, device):
    return pltpu.make_async_remote_copy(
        src_ref=src,
        dst_ref=dst,
        send_sem=sems.at[(0,) + index],
        recv_sem=sems.at[(1,) + index],
        device_id=device,
        device_id_type=MESH,
    )


def spans(count):
    return [slice(n * SPAN, (n + 1) * SPAN) for n in range(count)]


def head_kernel(
    media_ref,
    latents_ref,
    cotangent_ref,
    mask_ref,
    frames_ref,
    media_gain_ref,
    latent_gain_ref,
    ffn_gain_ref,
    w_query_ref,
    w_key_ref,
    w_value_ref,
    w_out_ref,
    w_up_ref,
    w_down_ref,
    rows_ref,
    keys_ref,
    values_ref,
    queries_ref,
    out_grad_ref,
    stats_ref,
    valid_ref,
    mid_grad_ref,
    ffn_gain_grad_ref,
    att_all_ref,
    lat_normed_ref,
    up_part_ref,
    new_latents_ref,
    grad_down_ref,
    wq,
    wk,
    wv,
    wo,
    wu,
    wd,
    lat_all,
    cot_all,
    part_send,
    part_recv,
    stat_send,
    stat_recv,
    attended_f,
    log_total,
    mid_all,
    act_grad,
    pre_f,
    act_all,
    pre_all,
    ffn_all,
    fig_f,
    fig_send,
    fig_recv,
    new_f,
    new_send,
    new_recv,
    rhs_all,
    lhs_send,
    lhs_recv,
    og_all,
    st_all,
    w_sems,
    line_sems,
    spread_sems,
    block_sems,
):
    bf16, f32 = jnp.bfloat16, jnp.float32
    z = lax.axis_index("seq")
    d = lax.axis_index("dp")
    y, x, c = d // 4, (d // 2) % 2, d % 2
    own_lat = latents_ref.shape[0]
    own_rows, features = media_ref.shape
    groups = features // SPAN
    scale = HEAD_DIM ** (-0.5)
    pair = d + 1 - 2 * c
    x_peer = d + 2 * (1 - 2 * x)
    y_peer = d + 4 * (1 - 2 * y)
    xy_peer = 4 * (1 - y) + 2 * (1 - x) + c
    peers = [(z + k) % 4 for k in (1, 2, 3)]
    others = [(d + k) % 8 for k in range(1, 8)]

    quarter = pl.ds(pl.multiple_of(z * features, 128), features)
    loads = [
        pltpu.make_async_copy(src, dst, w_sems.at[n])
        for n, (src, dst) in enumerate(
            [
                (w_key_ref, wk),
                (w_value_ref, wv),
                (w_query_ref, wq),
                (w_down_ref.at[quarter], wd),
                (w_out_ref, wo),
                (w_up_ref.at[:, quarter], wu),
            ]
        )
    ]
    for load in loads:
        load.start()

    barrier = pltpu.get_barrier_semaphore()
    for device in [(p, d) for p in peers] + [(z, p) for p in others]:
        pl.semaphore_signal(barrier, inc=1, device_id=device, device_id_type=MESH)
    pl.semaphore_wait(barrier, 10)

    def to_line(src_of, dst, number):
        copies = [
            copy_to(src_of(p), dst, line_sems, (number, k), (p, d)) for k, p in enumerate(peers)
        ]
        for copy in copies:
            copy.start()
        return copies

    def settle(copies):
        for copy in copies:
            copy.wait()

    lat_all[z] = latents_ref[...]
    cot_all[z] = cotangent_ref[...]
    lat_flight = to_line(lambda p: lat_all.at[z], lat_all.at[z], 0)
    cot_flight = to_line(lambda p: cot_all.at[z], cot_all.at[z], 1)

    frame = (
        z * own_rows + lax.broadcasted_iota(jnp.int32, (1, own_rows), 1)
    ) // PATCH
    kept = (mask_ref[pl.ds(z, 1), :] > 0) & (frame < frames_ref[...])
    kept = jnp.where(kept, 1.0, 0.0)
    valid_ref[0:own_rows, :] = jnp.broadcast_to(kept, (128, own_rows)).T
    valid_ref[own_rows:, :] = jnp.ones((own_lat, 128), f32)
    keep_row = jnp.concatenate([kept, jnp.ones((1, own_lat), f32)], axis=1) > 0.0

    def norm_step(n, carry):
        at = pl.ds(pl.multiple_of(n * 64, 64), 64)
        unit, _ = norm_parts(media_ref[at, :])
        rows_ref[at, :] = (unit * media_gain_ref[...]).astype(bf16)
        return carry

    lax.fori_loop(0, own_rows // 64, norm_step, 0)
    unit, _ = norm_parts(latents_ref[...])
    rows_ref[own_rows:, :] = (unit * latent_gain_ref[...]).astype(bf16)

    loads[0].wait()
    loads[1].wait()

    def project_step(n, carry):
        at = pl.ds(pl.multiple_of(n * SPAN, SPAN), SPAN)
        keys_ref[:, at] = dot(rows_ref[...], wk[:, at]).astype(bf16)
        values_ref[:, at] = dot(rows_ref[...], wv[:, at]).astype(bf16)
        return carry

    lax.fori_loop(0, groups, project_step, 0)

    settle(lat_flight)
    unit, _ = norm_parts(lat_all[...].reshape(4 * own_lat, features))
    lat_normed_ref[...] = (unit * latent_gain_ref[...]).astype(bf16)
    loads[2].wait()
    for cols in spans(groups):
        queries_ref[:, cols] = (dot(lat_normed_ref[...], wq[:, cols]) * scale).astype(bf16)

    settle(cot_flight)
    own_cot = pl.ds(pl.multiple_of(d * 128, 128), 64)
    own_pre = pl.ds(pl.multiple_of(d * 128 + 64, 64), 64)
    rhs_all[own_cot, :] = cot_all[...].reshape(4 * own_lat, features)

    def to_plane(at, number):
        copies = [
            copy_to(rhs_all.at[at], rhs_all.at[at], spread_sems, (number, k), (z, p))
            for k, p in enumerate((x_peer, y_peer, xy_peer, pair))
        ]
        for copy in copies:
            copy.start()
        return copies

    def to_pair(low, number):
        copies = []
        for k, p in enumerate((x_peer, y_peer, xy_peer)):
            at = pl.ds(pl.multiple_of(p * 128 + low, 64), 64)
            copies.append(
                copy_to(rhs_all.at[at], rhs_all.at[at], spread_sems, (number, 4 + k), (z, pair))
            )
        for copy in copies:
            copy.start()
        return copies

    cot_plane = to_plane(own_cot, 0)

    masks = head_masks(4 * own_lat)
    lane = lax.broadcasted_iota(jnp.int32, (4 * own_lat, 128), 1)
    top_tile = jnp.zeros((4 * own_lat, 128), f32)
    sum_tile = jnp.ones((4 * own_lat, 128), f32)
    for g, cols in enumerate(spans(groups)):
        scores = dot_t(stacked(queries_ref[:, cols], masks), keys_ref[:, cols])
        scores = jnp.where(keep_row, scores, MASKED_SCORE)
        largest = jnp.max(scores, axis=-1, keepdims=True)
        expo = jnp.where(keep_row, jnp.exp(scores - largest), 0.0)
        total = jnp.sum(expo, axis=-1, keepdims=True)
        part = dot(expo.astype(bf16), values_ref[:, cols])
        mixed = jnp.zeros((64, SPAN), f32)
        for h in range(GROUP):
            at = slice(64 * h, 64 * h + 64)
            mixed = mixed + jnp.where(masks[h], part[at], 0.0)
            top_tile = jnp.where(lane == GROUP * g + h, largest[at], top_tile)
            sum_tile = jnp.where(lane == GROUP * g + h, total[at], sum_tile)
        part_send[:, :, cols] = mixed.astype(bf16).reshape(4, own_lat, SPAN)
    stat_send[:, 0] = top_tile.reshape(4, own_lat, 128)
    stat_send[:, 1] = sum_tile.reshape(4, own_lat, 128)
    part_flight = to_line(lambda p: part_send.at[p], part_recv.at[z], 2)
    stat_flight = to_line(lambda p: stat_send.at[p], stat_recv.at[z], 3)
    part_recv[z] = part_send[z]
    stat_recv[z] = stat_send[z]

    loads[3].wait()
    for cols in spans(groups):
        act_grad[:, cols] = dot_t(cot_all[...].reshape(64, features), wd[cols, :])

    settle(stat_flight)
    tops = stat_recv[:, 0]
    top = jnp.max(tops, axis=0)
    factor = jnp.exp(tops - top[None])
    denominator = jnp.sum(factor * stat_recv[:, 1], axis=0)
    log_total[...] = top + jnp.log(denominator)
    share = factor / denominator[None]
    settle(part_flight)
    own_masks = head_masks(own_lat)
    att_own = att_all_ref.at[pl.ds(pl.multiple_of(z * own_lat, 16), own_lat)]
    for g, cols in enumerate(spans(groups)):
        merged = jnp.zeros((own_lat, SPAN), f32)
        for j in range(4):
            spread = jnp.zeros((own_lat, SPAN), f32)
            for h in range(GROUP):
                n = GROUP * g + h
                spread = jnp.where(own_masks[h], share[j, :, n : n + 1], spread)
            merged = merged + spread * part_recv[j, :, cols].astype(f32)
        attended_f[:, cols] = merged
        att_own[:, cols] = merged.astype(bf16)
    att_flight = to_line(lambda p: att_own, att_own, 4)

    settle(cot_plane)
    cot_pair = to_pair(0, 0)
    loads[4].wait()
    loads[5].wait()
    settle(att_flight)

    latents_64 = lat_all[...].reshape(64, features).astype(f32)
    for cols in spans(groups):
        mid_all[:, cols] = latents_64[:, cols] + dot(att_all_ref[...], wo[:, cols])
    unit, _ = norm_parts(mid_all[...])
    ffn_all[...] = (unit * ffn_gain_ref[...]).astype(bf16)

    for cols in spans(groups):
        pre = dot(ffn_all[...], wu[:, cols])
        cdf = 0.5 * (1.0 + lax.erf(pre * (0.5**0.5)))
        act_all[:, cols] = (pre * cdf).astype(bf16)
        density = jnp.exp(-0.5 * pre * pre) * (0.5 / jnp.pi) ** 0.5
        pre_all[:, cols] = (act_grad[:, cols] * (cdf + pre * density)).astype(bf16)
    for cols in spans(groups):
        part = dot_t(pre_all[...], wu[cols, :])
        fig_f[:, :, cols] = part.reshape(4, own_lat, SPAN)
        fig_send[:, :, cols] = part.astype(bf16).reshape(4, own_lat, SPAN)
    fig_flight = to_line(lambda p: fig_send.at[p], fig_recv.at[z], 5)
    rhs_all[own_pre, :] = pre_all[...]
    pre_plane = to_plane(own_pre, 1)
    for cols in spans(groups):
        part = dot(act_all[...], wd[:, cols])
        new_f[:, :, cols] = part.reshape(4, own_lat, SPAN)
        new_send[:, :, cols] = part.astype(bf16).reshape(4, own_lat, SPAN)
    new_flight = to_line(lambda p: new_send.at[p], new_recv.at[z], 6)

    settle(fig_flight)
    fig = fig_f[z]
    for p in peers:
        fig = fig + fig_recv[p].astype(f32)
    mid = mid_all[pl.ds(pl.multiple_of(z * own_lat, 16), own_lat), :]
    unit, inv = norm_parts(mid)
    ffn_gain_grad_ref[...] = jnp.sum(fig * unit, axis=0, keepdims=True)
    mid_grad = cotangent_ref[...].astype(f32) + input_grad(fig, ffn_gain_ref[...], unit, inv)
    mid_grad_ref[...] = mid_grad
    branch_grad = mid_grad.astype(bf16)
    own_lane = lax.broadcasted_iota(jnp.int32, (own_lat, 128), 1)
    delta = jnp.zeros((own_lat, 128), f32)
    for g, cols in enumerate(spans(groups)):
        grad = dot_t(branch_grad, wo[cols, :]).astype(bf16)
        og_all[z, :, cols] = grad
        product = grad.astype(f32) * attended_f[:, cols]
        for h in range(GROUP):
            summed = jnp.sum(jnp.where(own_masks[h], product, 0.0), axis=-1, keepdims=True)
            delta = jnp.where(own_lane == GROUP * g + h, summed, delta)
    st_all[z, 0] = log_total[...]
    st_all[z, 1] = delta
    og_flight = to_line(lambda p: og_all.at[z], og_all.at[z], 7)
    st_flight = to_line(lambda p: st_all.at[z], st_all.at[z], 8)

    blank = jnp.zeros((64, 128), f32)
    for j in range(features // 128):
        cols = slice(128 * j, 128 * j + 128)
        tile = jnp.concatenate([act_all[:, cols].astype(f32), blank], axis=0).T.astype(bf16)
        for piece in range(8):
            row = 128 * j + 16 * piece
            lhs_send[row // 192, row % 192 : row % 192 + 16, :] = tile[
                16 * piece : 16 * piece + 16, :
            ]
    for j in range(features // 128):
        cols = slice(128 * j, 128 * j + 128)
        tile = jnp.concatenate([blank, ffn_all[:, cols].astype(f32)], axis=0).T.astype(bf16)
        for piece in range(8):
            row = 128 * j + 16 * piece
            block, off = row // 48, row % 48
            at = (block // 8) * 48 + off
            lhs_send[block % 8, at : at + 16, :] += tile[16 * piece : 16 * piece + 16, :]
    own_slot = pl.ds(pl.multiple_of(d * 128, 128), 128)
    lhs_flight = [
        copy_to(lhs_send.at[p], lhs_recv.at[:, own_slot], block_sems, (k,), (z, p))
        for k, p in enumerate(others)
    ]
    for item in lhs_flight:
        item.start()
    lhs_recv[:, own_slot] = lhs_send[d]

    settle(cot_pair)
    settle(pre_plane)
    pre_pair = to_pair(64, 1)

    settle(new_flight)
    new = mid + new_f[z]
    for p in peers:
        new = new + new_recv[p].astype(f32)
    new_latents_ref[...] = new.astype(bf16)

    settle(st_flight)
    lane = lax.broadcasted_iota(jnp.int32, (64, 256), 1)
    row = lax.broadcasted_iota(jnp.int32, (64, 256), 0)
    for kind in range(2):
        tile = st_all[:, kind].reshape(64, 128)
        for g in range(groups):
            wide = jnp.zeros((64, 256), f32)
            for h in range(GROUP):
                n = GROUP * g + h
                wide = jnp.where(lane == row + 64 * h, tile[:, n : n + 1], wide)
            at = kind * groups + g
            stats_ref[at : at + 1, :] = jnp.sum(wide, axis=0, keepdims=True)
    settle(og_flight)
    out_grad_ref[...] = og_all[...].reshape(64, features)

    settle(lhs_flight)
    settle(pre_pair)
    depth = lhs_recv.shape[1]
    lane = lax.broadcasted_iota(jnp.int32, lhs_recv.shape, 1) % 128
    left = lhs_recv[...]
    act_left = jnp.where(lane < 64, left, jnp.zeros_like(left))
    ffn_left = jnp.where(lane >= 64, left, jnp.zeros_like(left))
    for cols in spans(groups):
        grad_down_ref[:, cols] = dot(act_left, rhs_all[:, cols])
        up_part_ref[:, :, cols] = (
            dot(ffn_left, rhs_all[:, cols]).astype(bf16).reshape(4, depth * 48 // 1024, SPAN)
        )


def head(operands, own_rows, own_lat, features):
    bf16, f32 = jnp.bfloat16, jnp.float32
    count = own_rows + own_lat
    lat_rows = 4 * own_lat
    share = features // 32
    vmem = pl.BlockSpec(memory_space=pltpu.VMEM)
    anyway = pl.BlockSpec(memory_space=pl.ANY)

    def array(kind, *shape):
        return jax.ShapeDtypeStruct(shape, kind)

    outs = (
        array(bf16, count, features),
        array(bf16, count, features),
        array(bf16, count, features),
        array(bf16, lat_rows, features),
        array(bf16, lat_rows, features),
        array(f32, 8, 256),
        array(f32, count, 128),
        array(f32, own_lat, features),
        array(f32, 1, features),
        array(bf16, lat_rows, features),
        array(bf16, lat_rows, features),
        array(bf16, 4, share, features),
        array(bf16, own_lat, features),
        array(f32, 4 * share, features),
    )
    square = pltpu.VMEM((features, features), bf16)
    quads = pltpu.VMEM((4, own_lat, features), bf16)
    quads_f = pltpu.VMEM((4, own_lat, features), f32)
    stat = pltpu.VMEM((4, 2, own_lat, 128), f32)
    wide_f = pltpu.VMEM((lat_rows, features), f32)
    wide = pltpu.VMEM((lat_rows, features), bf16)
    return pl.pallas_call(
        head_kernel,
        out_shape=outs,
        in_specs=[vmem] * 8 + [anyway] * 6,
        out_specs=(vmem,) * len(outs),
        scratch_shapes=[square] * 6
        + [quads, quads, quads, quads, stat, stat]
        + [
            pltpu.VMEM((own_lat, features), f32),
            pltpu.VMEM((own_lat, 128), f32),
            wide_f,
            wide_f,
            wide_f,
            wide,
            wide,
            wide,
            quads_f,
            quads,
            quads,
            quads_f,
            quads,
            quads,
            pltpu.VMEM((1024, features), bf16),
            pltpu.VMEM((8, 4 * share, 128), bf16),
            pltpu.VMEM((4 * share, 1024), bf16),
            quads,
            stat,
            pltpu.SemaphoreType.DMA((6,)),
            pltpu.SemaphoreType.DMA((2, 9, 3)),
            pltpu.SemaphoreType.DMA((2, 2, 7)),
            pltpu.SemaphoreType.DMA((2, 7)),
        ],
        compiler_params=pltpu.CompilerParams(
            collective_id=1, has_side_effects=True, vmem_limit_bytes=62 * 1024 * 1024
        ),
    )(*operands)


def tail_kernel(
    rows_ref,
    keys_ref,
    values_ref,
    queries_ref,
    out_grad_ref,
    stats_ref,
    valid_ref,
    media_ref,
    media_gain_ref,
    latents_ref,
    latent_gain_ref,
    mid_grad_ref,
    ffn_gain_grad_ref,
    att_all_ref,
    lat_normed_ref,
    up_part_ref,
    w_query_ref,
    w_key_ref,
    w_value_ref,
    media_grad_ref,
    latent_grad_ref,
    grad_query_ref,
    grad_key_ref,
    grad_value_ref,
    grad_out_ref,
    grad_up_ref,
    gains_ref,
    rows_t,
    lat_t,
    att_t,
    key_grad,
    value_grad,
    rows_grad,
    first_w,
    second_w,
    query_parts,
    pair_send,
    pair_recv,
    own,
    one_recv,
    two_recv,
    line_recv,
    line_own,
    up_recv,
    branch_parts,
    branch_send,
    query_send,
    query_recv,
    back_send,
    back_recv,
    gain_send,
    gain_recv,
    w_sems,
    pair_sems,
    one_sems,
    two_sems,
    line_sems,
    small_sems,
    gain_sems,
):
    bf16, f32 = jnp.bfloat16, jnp.float32
    z = lax.axis_index("seq")
    d = lax.axis_index("dp")
    y, x, c = d // 4, (d // 2) % 2, d % 2
    own_lat = latents_ref.shape[0]
    own_rows = media_ref.shape[0]
    features = media_ref.shape[1]
    groups = features // SPAN
    scale = HEAD_DIM ** (-0.5)
    pair_dev = (z, d + 1 - 2 * c)
    x_dev = (z, d + 2 * (1 - 2 * x))
    y_dev = (z, d + 4 * (1 - 2 * y))
    peers = [(z + k) % 4 for k in (1, 2, 3)]

    load_key = pltpu.make_async_copy(w_key_ref, first_w, w_sems.at[0])
    load_value = pltpu.make_async_copy(w_value_ref, second_w, w_sems.at[1])
    load_key.start()
    load_value.start()

    barrier = pltpu.get_barrier_semaphore()
    for device in [pair_dev, x_dev, y_dev] + [(p, d) for p in peers]:
        pl.semaphore_signal(barrier, inc=1, device_id=device, device_id_type=MESH)
    pl.semaphore_wait(barrier, 6)

    branch = mid_grad_ref[...].astype(bf16)
    for quarter in range(4):
        branch_send[quarter] = branch[:, quarter * SPAN : (quarter + 1) * SPAN]
    branch_parts[z] = branch_send[z]
    spread = []
    for k, p in enumerate(peers):
        spread.append(copy_to(up_part_ref.at[p], up_recv.at[z], small_sems, (0, k), (p, d)))
        spread.append(
            copy_to(branch_send.at[p], branch_parts.at[z], small_sems, (2, k), (p, d))
        )
    for item in spread:
        item.start()

    def place_transposed(dest, tile, column):
        for piece in range(8):
            row = column + 16 * piece
            block, off = row // 48, row % 48
            bz, by, bx, bc = block // 8, (block // 4) % 2, (block // 2) % 2, block % 2
            at = bx * 384 + by * 192 + bz * 48 + off
            dest[bc, at : at + 16, :] = tile[16 * piece : 16 * piece + 16, :]

    for j in range(features // 128):
        tile = rows_ref[:, 128 * j : 128 * j + 128].astype(f32).T.astype(bf16)
        place_transposed(rows_t, tile, 128 * j)

    masks = head_masks(64)

    def send_pair(ch, left, right, factor=None):
        for half in range(2):
            part = dot(left[1 - c, half * 384 : (half + 1) * 384, :], right)
            if factor is not None:
                part = part * factor
            pair_send[ch, half * 384 : (half + 1) * 384, :] = part.astype(bf16)
        copy = copy_to(pair_send.at[ch], pair_recv.at[ch], pair_sems, (ch,), pair_dev)
        copy.start()
        slot = ch % 6
        for half in range(2):
            part = dot(left[c, half * 384 : (half + 1) * 384, :], right)
            if factor is not None:
                part = part * factor
            own[slot, half] = part.reshape(2, 192, SPAN)
        return copy

    flights = {}

    def compute_group(g):
        cols = slice(g * SPAN, (g + 1) * SPAN)
        key_g = keys_ref[:, cols]
        value_g = values_ref[:, cols]
        q_stack = stacked(queries_ref[:, cols], masks)
        o_stack = stacked(out_grad_ref[:, cols], masks)
        scores = dot_t(key_g, q_stack)
        keep = valid_ref[:, 0:1] > 0.0
        exact = jnp.where(keep, jnp.exp(scores - stats_ref[g : g + 1, :]), 0.0)
        prob_grad = dot_t(value_g, o_stack)
        score_grad = (exact * (prob_grad - stats_ref[4 + g : 5 + g, :])).astype(bf16)
        v_grad = dot(exact.astype(bf16), o_stack).astype(bf16)
        value_grad[:, cols] = v_grad
        flights["pair", 2 * g] = send_pair(2 * g, rows_t, v_grad)
        k_grad = dot(score_grad, q_stack).astype(bf16)
        key_grad[:, cols] = k_grad
        flights["pair", 2 * g + 1] = send_pair(2 * g + 1, rows_t, k_grad)
        q_part = outer_sum(score_grad, key_g)
        q_sum = jnp.zeros((64, SPAN), f32)
        for h in range(GROUP):
            q_sum = q_sum + jnp.where(masks[h], q_part[64 * h : 64 * h + 64], 0.0)
        query_parts[g] = q_sum
        query_send[g] = q_sum.astype(bf16)

    def pair_sum(k):
        for ch in (2 * k, 2 * k + 1):
            flights["pair", ch].wait()
            slot = ch % 6
            for bx in range(2):
                for by in range(2):
                    at = bx * 384 + by * 192
                    own[slot, bx, by] += pair_recv[ch, at : at + 192, :].astype(f32)
            if ch % 2 == 0:
                theirs, device = own[slot, 1 - x], x_dev
            else:
                theirs, device = own[slot, :, 1 - y], y_dev
            pair_send[ch, 0:384, :] = theirs.reshape(384, SPAN).astype(bf16)
            copy = copy_to(
                pair_send.at[ch, pl.ds(0, 384)], one_recv.at[ch], one_sems, (ch,), device
            )
            copy.start()
            flights["one", ch] = copy

    def one_sum(k):
        for ch in (2 * k, 2 * k + 1):
            flights["one", ch].wait()
            slot = ch % 6
            if ch % 2 == 0:
                for by in range(2):
                    own[slot, x, by] += one_recv[ch, by * 192 : by * 192 + 192, :].astype(f32)
                theirs, device = own[slot, x, 1 - y], y_dev
            else:
                for bx in range(2):
                    own[slot, bx, y] += one_recv[ch, bx * 192 : bx * 192 + 192, :].astype(f32)
                theirs, device = own[slot, 1 - x, y], x_dev
            pair_send[ch, 384:576, :] = theirs.astype(bf16)
            copy = copy_to(
                pair_send.at[ch, pl.ds(384, 192)], two_recv.at[ch], two_sems, (ch,), device
            )
            copy.start()
            flights["two", ch] = copy

    def two_sum(k):
        for ch in (2 * k, 2 * k + 1):
            flights["two", ch].wait()
            slot = ch % 6
            total = own[slot, x, y] + two_recv[ch].astype(f32)
            own[slot, x, y] = total
            pair_send[ch, 576:768, :] = total.astype(bf16)
            line_own[ch] = own[slot, x, y, pl.ds(pl.multiple_of(z * 48, 16), 48), :]
            copies = []
            for j, p in enumerate(peers):
                copies.append(
                    copy_to(
                        pair_send.at[ch, pl.ds(pl.multiple_of(576 + p * 48, 16), 48)],
                        line_recv.at[ch, z],
                        line_sems,
                        (ch, j),
                        (p, d),
                    )
                )
            for copy in copies:
                copy.start()
            flights["line", ch] = copies

    def line_sum(k):
        for ch in (2 * k, 2 * k + 1):
            for copy in flights["line", ch]:
                copy.wait()
            if k < groups:
                total = line_own[ch]
                for p in peers:
                    total = total + line_recv[ch, p].astype(f32)
                dest = grad_value_ref if ch % 2 == 0 else grad_key_ref
                dest[:, k * SPAN : (k + 1) * SPAN] = total
            else:
                dest = grad_out_ref if ch % 2 == 0 else grad_query_ref
                line_recv[ch, z] = line_own[ch].astype(bf16)
                for quarter in range(4):
                    dest[:, quarter * SPAN : (quarter + 1) * SPAN] = line_recv[
                        ch, quarter
                    ].astype(f32)

    compute_group(0)
    pair_sum(0)
    compute_group(1)
    pair_sum(1)
    one_sum(0)
    compute_group(2)
    pair_sum(2)
    one_sum(1)
    two_sum(0)
    compute_group(3)
    pair_sum(3)
    one_sum(2)
    two_sum(1)
    line_sum(0)

    to_quarter = [
        copy_to(query_send.at[p], query_recv.at[z], small_sems, (3, k), (p, d))
        for k, p in enumerate(peers)
    ]
    for item in to_quarter:
        item.start()
    for item in spread:
        item.wait()
    up_recv[z] = up_part_ref[z]
    for quarter in range(4):
        at = slice(quarter * features, (quarter + 1) * features)
        grad_up_ref[:, at] = up_recv[quarter].astype(f32)
    for j in range(features // 128):
        cols = slice(128 * j, 128 * j + 128)
        tile = lat_normed_ref[:, cols].astype(f32).T.astype(bf16)
        place_transposed(lat_t, tile, 128 * j)
        tile = att_all_ref[:, cols].astype(f32).T.astype(bf16)
        place_transposed(att_t, tile, 128 * j)
    last = 2 * groups
    flights["pair", last] = send_pair(last, att_t, branch_parts[...].reshape(64, SPAN))
    for item in to_quarter:
        item.wait()
    query_quarter = query_parts[z]
    for p in peers:
        query_quarter = query_quarter + query_recv[p].astype(f32)
    query_quarter = query_quarter.astype(bf16)
    back_send[...] = query_quarter.reshape(4, own_lat, SPAN)
    back_recv[z] = back_send[z]
    to_rows = [
        copy_to(back_send.at[p], back_recv.at[z], small_sems, (4, k), (p, d))
        for k, p in enumerate(peers)
    ]
    for item in to_rows:
        item.start()
    flights["pair", last + 1] = send_pair(last + 1, lat_t, query_quarter, scale)
    pair_sum(4)
    one_sum(3)
    two_sum(2)
    line_sum(1)

    load_key.wait()
    load_value.wait()

    def back_step(n, carry):
        at = pl.ds(pl.multiple_of(n * SPAN, SPAN), SPAN)
        rows_grad[:, at] = dot_t(key_grad[...], first_w[at, :]) + dot_t(
            value_grad[...], second_w[at, :]
        )
        return carry

    lax.fori_loop(0, groups, back_step, 0)
    load_query = pltpu.make_async_copy(w_query_ref, first_w, w_sems.at[2])
    load_query.start()
    one_sum(4)
    two_sum(3)
    line_sum(2)

    def norm_step(n, total):
        at = pl.ds(pl.multiple_of(n * 64, 64), 64)
        unit, inv = norm_parts(media_ref[at, :])
        grad = rows_grad[at, :]
        media_grad_ref[at, :] = input_grad(grad, media_gain_ref[...], unit, inv).astype(bf16)
        return total + jnp.sum(grad * unit, axis=0, keepdims=True)

    gain_total = lax.fori_loop(0, own_rows // 64, norm_step, jnp.zeros((1, features), f32))

    for item in to_rows:
        item.wait()
    load_query.wait()
    lat_grad = rows_grad[own_rows:, :]
    for quarter in range(4):
        lat_grad = lat_grad + scale * dot_t(
            back_recv[quarter], first_w[:, quarter * SPAN : (quarter + 1) * SPAN]
        )
    unit, inv = norm_parts(latents_ref[...])
    latent_grad_ref[...] = (
        mid_grad_ref[...] + input_grad(lat_grad, latent_gain_ref[...], unit, inv)
    ).astype(bf16)
    latent_total = jnp.sum(lat_grad * unit, axis=0, keepdims=True)
    gain_send[0] = jnp.concatenate(
        [gain_total, latent_total, ffn_gain_grad_ref[...], jnp.zeros((5, features), f32)], axis=0
    )
    hops = [pair_dev, x_dev, y_dev]

    def gain_hop(hop):
        return copy_to(
            gain_send.at[hop], gain_recv.at[hop], gain_sems, (hop,), hops[hop]
        )

    first_hop = gain_hop(0)
    first_hop.start()
    two_sum(4)
    line_sum(3)
    first_hop.wait()
    gain_send[1] = gain_send[0] + gain_recv[0]
    second_hop = gain_hop(1)
    second_hop.start()
    second_hop.wait()
    gain_send[2] = gain_send[1] + gain_recv[1]
    third_hop = gain_hop(2)
    third_hop.start()
    third_hop.wait()
    gain_send[3] = gain_send[2] + gain_recv[2]
    lines = [
        copy_to(gain_send.at[3], gain_recv.at[3 + z], gain_sems, (3 + k,), (p, d))
        for k, p in enumerate(peers)
    ]
    for item in lines:
        item.start()
    line_sum(4)
    for item in lines:
        item.wait()
    total = gain_send[3]
    for p in peers:
        total = total + gain_recv[3 + p]
    gains_ref[...] = total


def tail(operands, own_rows, own_lat, features):
    bf16, f32 = jnp.bfloat16, jnp.float32
    count = own_rows + own_lat
    chunks = 2 * (features // SPAN) + 2
    vmem = pl.BlockSpec(memory_space=pltpu.VMEM)
    anyway = pl.BlockSpec(memory_space=pl.ANY)
    share = features // 32
    return pl.pallas_call(
        tail_kernel,
        out_shape=(
            jax.ShapeDtypeStruct((own_rows, features), bf16),
            jax.ShapeDtypeStruct((own_lat, features), bf16),
            jax.ShapeDtypeStruct((share, features), f32),
            jax.ShapeDtypeStruct((share, features), f32),
            jax.ShapeDtypeStruct((share, features), f32),
            jax.ShapeDtypeStruct((share, features), f32),
            jax.ShapeDtypeStruct((share, 4 * features), f32),
            jax.ShapeDtypeStruct((8, features), f32),
        ),
        in_specs=[vmem] * 16 + [anyway] * 3,
        out_specs=(vmem,) * 8,
        scratch_shapes=[
            pltpu.VMEM((2, features // 2, count), bf16),
            pltpu.VMEM((2, features // 2, 64), bf16),
            pltpu.VMEM((2, features // 2, 64), bf16),
            pltpu.VMEM((count, features), bf16),
            pltpu.VMEM((count, features), bf16),
            pltpu.VMEM((count, features), f32),
            pltpu.VMEM((features, features), bf16),
            pltpu.VMEM((features, features), bf16),
            pltpu.VMEM((4, 64, SPAN), f32),
            pltpu.VMEM((chunks, 768, SPAN), bf16),
            pltpu.VMEM((chunks, 768, SPAN), bf16),
            pltpu.VMEM((6, 2, 2, 192, SPAN), f32),
            pltpu.VMEM((chunks, 384, SPAN), bf16),
            pltpu.VMEM((chunks, 192, SPAN), bf16),
            pltpu.VMEM((chunks, 4, 48, SPAN), bf16),
            pltpu.VMEM((chunks, 48, SPAN), f32),
            pltpu.VMEM((4, share, features), bf16),
            pltpu.VMEM((4, own_lat, SPAN), bf16),
            pltpu.VMEM((4, own_lat, SPAN), bf16),
            pltpu.VMEM((4, 64, SPAN), bf16),
            pltpu.VMEM((4, 64, SPAN), bf16),
            pltpu.VMEM((4, own_lat, SPAN), bf16),
            pltpu.VMEM((4, own_lat, SPAN), bf16),
            pltpu.VMEM((4, 8, features), f32),
            pltpu.VMEM((7, 8, features), f32),
            pltpu.SemaphoreType.DMA((3,)),
            pltpu.SemaphoreType.DMA((2, chunks)),
            pltpu.SemaphoreType.DMA((2, chunks)),
            pltpu.SemaphoreType.DMA((2, chunks)),
            pltpu.SemaphoreType.DMA((2, chunks, 3)),
            pltpu.SemaphoreType.DMA((2, 5, 3)),
            pltpu.SemaphoreType.DMA((2, 6)),
        ],
        compiler_params=pltpu.CompilerParams(
            collective_id=0, has_side_effects=True, vmem_limit_bytes=62 * 1024 * 1024
        ),
    )(*operands)


def spread_body(
    media,
    latents,
    frame_counts,
    media_mask,
    media_gain,
    latent_gain,
    ffn_gain,
    w_query,
    w_key,
    w_value,
    w_out,
    w_up,
    w_down,
    cotangent,
):
    _, own_rows, features = media.shape
    own_lat = latents.shape[1]
    seq_parts = lax.axis_size("seq")
    seq_index = lax.axis_index("seq")
    device_count = seq_parts * lax.axis_size("dp")
    both = ("seq", "dp")
    heads = features // HEAD_DIM
    score_scale = HEAD_DIM ** (-0.5)
    bf16 = jnp.bfloat16

    media, latents, cotangent = media[0], latents[0], cotangent[0]
    own_mask = lax.dynamic_slice_in_dim(media_mask[0], seq_index * own_rows, own_rows, 0)
    row_frame = (seq_index * own_rows + jnp.arange(own_rows, dtype=jnp.int32)) // PATCH
    own_valid = (own_mask > 0) & (row_frame < frame_counts[0])
    valid = jnp.concatenate([own_valid, jnp.ones((own_lat,), jnp.bool_)])[None, None, :]

    all_cotangent = lax.all_gather(cotangent, both, axis=0, tiled=True)

    latents_f = latents.astype(jnp.float32)
    latent_unit, latent_inv = normalize(latents_f)
    latent_normed = (latent_unit * latent_gain).astype(bf16)
    own_queries = (dot(latent_normed, w_query) * score_scale).astype(bf16)
    queries = lax.all_gather(own_queries, "seq", axis=0, tiled=True)

    media_unit, media_inv = normalize(media.astype(jnp.float32))
    media_normed = (media_unit * media_gain).astype(bf16)
    rows = jnp.concatenate([media_normed, latent_normed], axis=0)
    keys = dot(rows, w_key).astype(bf16)
    values = dot(rows, w_value).astype(bf16)

    scores = jnp.where(valid, head_products(queries, keys), MASKED_SCORE)
    largest = jnp.max(scores, axis=-1)
    expo = jnp.where(valid, jnp.exp(scores - largest[..., None]), 0.0)
    total = jnp.sum(expo, axis=-1)
    part = weighted(expo.astype(bf16), values)
    packed = jnp.concatenate([part, largest.T, total.T], axis=1)
    packed = lax.all_to_all(packed, "seq", split_axis=0, concat_axis=0, tiled=True)
    packed = packed.reshape(seq_parts, own_lat, -1)
    parts = packed[..., :features]
    maxima = packed[..., features : features + heads]
    totals = packed[..., features + heads :]
    top = jnp.max(maxima, axis=0)
    factor = jnp.exp(maxima - top)
    denominator = jnp.sum(factor * totals, axis=0)
    log_total = top + jnp.log(denominator)
    share = jnp.repeat(factor / denominator, HEAD_DIM, axis=-1)
    attended_f = jnp.sum(parts * share, axis=0)
    attended = attended_f.astype(bf16)

    mid = latents_f + dot(attended, w_out)
    mid_unit, mid_inv = normalize(mid)
    ffn_in = (mid_unit * ffn_gain).astype(bf16)
    pre = dot(ffn_in, w_up)
    act = gelu_exact(pre).astype(bf16)
    new_latents = (mid + dot(act, w_down)).astype(bf16)
    act_grad = dot_t(cotangent, w_down)
    pre_grad = jax.vjp(gelu_exact, pre)[1](act_grad)[0].astype(bf16)
    all_pre_grad = lax.all_gather(pre_grad, both, axis=0, tiled=True)
    ffn_in_grad = dot_t(pre_grad, w_up)
    mid_back, grad_ffn_gain = norm_back(ffn_in_grad, ffn_gain, mid_unit, mid_inv)
    mid_grad = cotangent.astype(jnp.float32) + mid_back
    branch_grad = mid_grad.astype(bf16)
    all_branch = lax.all_gather(branch_grad, both, axis=0, tiled=True)
    attended_grad = dot_t(branch_grad, w_out).astype(bf16)
    own_delta = jnp.sum(
        split_heads(attended_f * attended_grad.astype(jnp.float32)), axis=-1
    )
    out_grad = lax.all_gather(attended_grad, "seq", axis=0, tiled=True)
    stats = lax.all_gather(
        jnp.concatenate([log_total, own_delta], axis=1), "seq", axis=0, tiled=True
    )
    lse = stats[:, :heads].T[..., None]
    delta = stats[:, heads:].T[..., None]

    exact = jnp.where(valid, jnp.exp(scores - lse), 0.0)
    score_grad = (exact * (head_products(out_grad, values) - delta)).astype(bf16)
    value_grad = transposed(exact.astype(bf16), out_grad).astype(bf16)
    key_grad = transposed(score_grad, queries).astype(bf16)
    query_part = weighted(score_grad, keys)
    query_grad = lax.psum_scatter(
        query_part, "seq", scatter_dimension=0, tiled=True
    ).astype(bf16)
    all_query_grad = lax.all_gather(query_grad, both, axis=0, tiled=True)
    part_value = outer_sum(rows, value_grad).astype(bf16)
    part_key = outer_sum(rows, key_grad).astype(bf16)
    sum_value = lax.psum_scatter(part_value, both, scatter_dimension=0, tiled=True)
    sum_key = lax.psum_scatter(part_key, both, scatter_dimension=0, tiled=True)

    rows_grad = dot_t(key_grad, w_key) + dot_t(value_grad, w_value)
    media_back, grad_media_gain = norm_back(
        rows_grad[:own_rows], media_gain, media_unit, media_inv
    )
    media_grad = media_back.astype(bf16)
    latent_normed_grad = rows_grad[own_rows:] + dot_t(query_grad, w_query) * score_scale
    latent_back, grad_latent_gain = norm_back(
        latent_normed_grad, latent_gain, latent_unit, latent_inv
    )
    latent_grad = (mid_grad + latent_back).astype(bf16)

    def by_owner(tensor):
        return tensor.reshape(tensor.shape[0], device_count, -1)

    sent = jnp.concatenate(
        [by_owner(latent_normed), by_owner(attended), by_owner(ffn_in), by_owner(act)], axis=2
    )
    got = lax.all_to_all(sent, both, split_axis=1, concat_axis=0, tiled=True)
    got = got.reshape(-1, got.shape[-1])
    block = features // device_count
    grad_query = outer_sum(got[:, :block], all_query_grad) * score_scale
    grad_out = outer_sum(got[:, block : 2 * block], all_branch)
    grad_up = outer_sum(got[:, 2 * block : 3 * block], all_pre_grad)
    grad_down = outer_sum(got[:, 3 * block :], all_cotangent)

    gains = jnp.stack([grad_media_gain, grad_latent_gain, grad_ffn_gain])
    gains = by_owner(gains).transpose(1, 0, 2).reshape(device_count, -1)
    gains = lax.all_to_all(gains, both, split_axis=0, concat_axis=0, tiled=True)
    gains = jnp.sum(gains.reshape(device_count, 3, -1), axis=0)
    return (
        new_latents[None],
        media_grad[None],
        latent_grad[None],
        grad_query,
        sum_key.astype(jnp.float32),
        sum_value.astype(jnp.float32),
        grad_out,
        grad_up,
        grad_down,
        gains[0],
        gains[1],
        gains[2],
    )


def body(
    media,
    latents,
    frame_counts,
    media_mask,
    media_gain,
    latent_gain,
    ffn_gain,
    w_query,
    w_key,
    w_value,
    w_out,
    w_up,
    w_down,
    cotangent,
):
    _, own_rows, features = media.shape
    own_lat = latents.shape[1]
    seq_parts, dp_parts = lax.axis_size("seq"), lax.axis_size("dp")
    if (seq_parts, dp_parts, own_lat, features) != (4, 8, 16, 4 * SPAN):
        return spread_body(
            media,
            latents,
            frame_counts,
            media_mask,
            media_gain,
            latent_gain,
            ffn_gain,
            w_query,
            w_key,
            w_value,
            w_out,
            w_up,
            w_down,
            cotangent,
        )
    (
        rows,
        keys,
        values,
        queries,
        out_grad,
        stats,
        valid,
        mid_grad,
        grad_ffn_gain,
        attended,
        lat_normed,
        up_part,
        new_latents,
        grad_down,
    ) = head(
        (
            media[0],
            latents[0],
            cotangent[0],
            media_mask.reshape(seq_parts, own_rows),
            frame_counts[None],
            media_gain[None],
            latent_gain[None],
            ffn_gain[None],
            w_query,
            w_key,
            w_value,
            w_out,
            w_up,
            w_down,
        ),
        own_rows,
        own_lat,
        features,
    )
    media_grad, latent_grad, grad_query, grad_key, grad_value, grad_out, grad_up, gain_sums = tail(
        (
            rows,
            keys,
            values,
            queries,
            out_grad,
            stats,
            valid,
            media[0],
            media_gain[None],
            latents[0],
            latent_gain[None],
            mid_grad,
            grad_ffn_gain,
            attended,
            lat_normed,
            up_part,
            w_query,
            w_key,
            w_value,
        ),
        own_rows,
        own_lat,
        features,
    )
    block = features // (seq_parts * dp_parts)
    place = lax.axis_index("seq") * dp_parts + lax.axis_index("dp")
    gains = lax.dynamic_slice_in_dim(gain_sums[:3], place * block, block, 1)
    return (
        new_latents[None],
        media_grad[None],
        latent_grad[None],
        grad_query,
        grad_key,
        grad_value,
        grad_out,
        grad_up,
        grad_down,
        gains[0],
        gains[1],
        gains[2],
    )


def solution(mesh):
    return jax.shard_map(
        body,
        mesh=mesh,
        in_specs=(
            P("dp", "seq", None),
            P("dp", "seq", None),
            P("dp"),
            P("dp", None),
            P(),
            P(),
            P(),
            P(),
            P(),
            P(),
            P(),
            P(),
            P(),
            P("dp", "seq", None),
        ),
        out_specs=(
            P("dp", "seq", None),
            P("dp", "seq", None),
            P("dp", "seq", None),
            P(("seq", "dp"), None),
            P(("seq", "dp"), None),
            P(("seq", "dp"), None),
            P(("seq", "dp"), None),
            P(("seq", "dp"), None),
            P(("seq", "dp"), None),
            P(("seq", "dp")),
            P(("seq", "dp")),
            P(("seq", "dp")),
        ),
        check_vma=False,
    )
```

```python
import jax
import jax.numpy as jnp
from jax import lax
from jax.experimental import pallas as pl
from jax.experimental.pallas import tpu as pltpu
from jax.sharding import PartitionSpec as P

HEAD_DIM = 96
PATCH = 256


MASKED_SCORE = -1e30


def normalize(tensor):
    centered = tensor - jnp.mean(tensor, axis=-1, keepdims=True)
    inv = lax.rsqrt(jnp.mean(centered * centered, axis=-1, keepdims=True) + 1e-05)
    return centered * inv, inv


def norm_back(grad, gain_vec, unit, inv):
    scaled = grad * gain_vec
    inner = jnp.mean(scaled * unit, axis=-1, keepdims=True)
    input_grad = inv * (scaled - jnp.mean(scaled, axis=-1, keepdims=True) - unit * inner)
    return input_grad, jnp.sum(grad * unit, axis=0)


def gelu_exact(tensor):
    return jax.nn.gelu(tensor, approximate=False)


def dot(left_op, right_op):
    return jnp.dot(left_op, right_op, preferred_element_type=jnp.float32)


def dot_t(left_op, right_op):
    return lax.dot_general(
        left_op, right_op, (((1,), (1,)), ((), ())), preferred_element_type=jnp.float32
    )


def outer_sum(left_op, right_op):
    return lax.dot_general(
        left_op, right_op, (((0,), (0,)), ((), ())), preferred_element_type=jnp.float32
    )


def split_heads(tensor):
    return tensor.reshape(tensor.shape[0], -1, HEAD_DIM)


def head_products(left_op, right_op):
    return jnp.einsum(
        "qhd,khd->hqk",
        split_heads(left_op),
        split_heads(right_op),
        preferred_element_type=jnp.float32,
    )


def weighted(weights_tab, rows):
    result = jnp.einsum(
        "hqk,khd->qhd", weights_tab, split_heads(rows), preferred_element_type=jnp.float32
    )
    return result.reshape(result.shape[0], -1)


def transposed(weights_tab, rows):
    result = jnp.einsum(
        "hqk,qhd->khd", weights_tab, split_heads(rows), preferred_element_type=jnp.float32
    )
    return result.reshape(result.shape[0], -1)


MESH = pl.DeviceIdType.MESH
GROUP = 4
SPAN = GROUP * HEAD_DIM


def norm_parts(block):
    block = block.astype(jnp.float32)
    centered = block - jnp.mean(block, axis=-1, keepdims=True)
    inv = lax.rsqrt(jnp.mean(centered * centered, axis=-1, keepdims=True) + 1e-05)
    return centered * inv, inv


def input_grad(grad, gain, unit, inv):
    scaled = grad * gain
    inner = jnp.mean(scaled * unit, axis=-1, keepdims=True)
    return inv * (scaled - jnp.mean(scaled, axis=-1, keepdims=True) - unit * inner)


def head_masks(count):
    lane = lax.broadcasted_iota(jnp.int32, (count, SPAN), 1)
    return [(lane >= h * HEAD_DIM) & (lane < (h + 1) * HEAD_DIM) for h in range(GROUP)]


def stacked(tensor, masks):
    return jnp.concatenate(
        [jnp.where(mask, tensor, jnp.zeros_like(tensor)) for mask in masks], axis=0
    )


def copy_to(src, dst, sems, index, device):
    return pltpu.make_async_remote_copy(
        src_ref=src,
        dst_ref=dst,
        send_sem=sems.at[(0,) + index],
        recv_sem=sems.at[(1,) + index],
        device_id=device,
        device_id_type=MESH,
    )


def spans(count):
    return [slice(n * SPAN, (n + 1) * SPAN) for n in range(count)]


def halves(features):
    return [slice(0, features // 2), slice(features // 2, features)]


def settle(copies):
    for copy in copies:
        copy.wait()


def place_transposed(dest, tile, column):
    for piece in range(8):
        row = column + 16 * piece
        block, off = row // 48, row % 48
        bz, by, bx, bc = block // 8, (block // 4) % 2, (block // 2) % 2, block % 2
        at = bx * 384 + by * 192 + bz * 48 + off
        dest[bc, at : at + 16, :] = tile[16 * piece : 16 * piece + 16, :]


def layer_kernel(
    media_ref,
    latents_ref,
    cotangent_ref,
    mask_ref,
    frames_ref,
    media_gain_ref,
    latent_gain_ref,
    ffn_gain_ref,
    w_query_ref,
    w_key_ref,
    w_value_ref,
    w_out_ref,
    w_up_ref,
    w_down_ref,
    new_latents_out,
    media_grad_out,
    latent_grad_out,
    line_out,
    up_out,
    down_out,
    gains_out,
    gains,
    w_a,
    w_b,
    w_c,
    rows,
    keys,
    values,
    queries,
    stats,
    valid,
    lat_normed,
    lat_all,
    cot_all,
    att_all,
    part_send,
    part_recv,
    stat_send,
    stat_recv,
    attended_f,
    log_total,
    mid_all,
    act_grad,
    act_all,
    pre_all,
    ffn_all,
    fig_f,
    fig_send,
    fig_recv,
    new_f,
    new_send,
    new_recv,
    mid_grad_own,
    rhs_all,
    lhs_send,
    lhs_recv,
    og_all,
    st_all,
    branch_send,
    branch_parts,
    small_out,
    down_part,
    up_part,
    up_recv,
    rows_t,
    lat_t,
    att_t,
    key_grad,
    value_grad,
    rows_grad,
    query_parts,
    query_send,
    query_recv,
    back_send,
    back_recv,
    pair_send,
    pair_recv,
    own,
    one_recv,
    two_recv,
    line_recv,
    gain_part,
    gain_recv,
    gain_sum,
    gain_all,
    load_sems,
    store_sems,
    line_sems,
    spread_sems,
    block_sems,
    pair_sems,
    one_sems,
    two_sems,
    last_sems,
):
    bf16, f32 = jnp.bfloat16, jnp.float32
    z = lax.axis_index("seq")
    d = lax.axis_index("dp")
    y, x, c = d // 4, (d // 2) % 2, d % 2
    own_lat = latents_ref.shape[0]
    own_rows, features = media_ref.shape
    groups = features // SPAN
    scale = HEAD_DIM ** (-0.5)
    pair = d + 1 - 2 * c
    x_peer = d + 2 * (1 - 2 * x)
    y_peer = d + 4 * (1 - 2 * y)
    xy_peer = 4 * (1 - y) + 2 * (1 - x) + c
    peers = [(z + k) % 4 for k in (1, 2, 3)]
    others = [(d + k) % 8 for k in range(1, 8)]

    quarter = pl.ds(pl.multiple_of(z * features, 128), features)

    def load(src, dst, number):
        copy = pltpu.make_async_copy(src, dst, load_sems.at[number])
        copy.start()
        return copy

    gain_loads = [
        load(media_gain_ref, gains.at[0], 0),
        load(latent_gain_ref, gains.at[1], 1),
        load(ffn_gain_ref, gains.at[2], 2),
    ]
    load_a = load(w_key_ref, w_a, 3)
    load_b = load(w_value_ref, w_b, 4)
    load_c = load(w_query_ref, w_c, 5)

    stores = []

    def store(src, dst):
        copy = pltpu.make_async_copy(src, dst, store_sems.at[len(stores)])
        copy.start()
        stores.append(copy)

    barrier = pltpu.get_barrier_semaphore()
    for device in [(p, d) for p in peers] + [(z, p) for p in others]:
        pl.semaphore_signal(barrier, inc=1, device_id=device, device_id_type=MESH)

    lines = []

    def to_line(src_of, dst):
        number = len(lines)
        lines.append(number)
        copies = [
            copy_to(src_of(p), dst, line_sems, (number, k), (p, d)) for k, p in enumerate(peers)
        ]
        for copy in copies:
            copy.start()
        return copies

    frame = (z * own_rows + lax.broadcasted_iota(jnp.int32, (1, own_rows), 1)) // PATCH
    own_mask = mask_ref[:, pl.ds(pl.multiple_of(z * own_rows, 128), own_rows)]
    kept = jnp.where((own_mask > 0) & (frame < frames_ref[0]), 1.0, 0.0)
    valid[0:own_rows, :] = jnp.broadcast_to(kept, (128, own_rows)).T
    valid[own_rows:, :] = jnp.ones((own_lat, 128), f32)
    keep_row = jnp.concatenate([kept, jnp.ones((1, own_lat), f32)], axis=1) > 0.0

    settle(gain_loads)
    media_gain, latent_gain, ffn_gain = gains[0:1, :], gains[1:2, :], gains[2:3, :]

    def norm_step(n, carry):
        at = pl.ds(pl.multiple_of(n * 64, 64), 64)
        unit, _ = norm_parts(media_ref[at, :])
        rows[at, :] = (unit * gains[0:1, :]).astype(bf16)
        return carry

    lax.fori_loop(0, own_rows // 64, norm_step, 0)
    pl.semaphore_wait(barrier, 10)
    lat_all[z] = latents_ref[...]
    cot_all[z] = cotangent_ref[...]
    lat_flight = to_line(lambda p: lat_all.at[z], lat_all.at[z])
    cot_flight = to_line(lambda p: cot_all.at[z], cot_all.at[z])

    unit, _ = norm_parts(latents_ref[...])
    rows[own_rows:, :] = (unit * latent_gain).astype(bf16)

    load_a.wait()
    load_b.wait()

    def project_step(n, carry):
        at = pl.ds(pl.multiple_of(n * SPAN, SPAN), SPAN)
        keys[:, at] = dot(rows[...], w_a[:, at]).astype(bf16)
        values[:, at] = dot(rows[...], w_b[:, at]).astype(bf16)
        return carry

    lax.fori_loop(0, groups, project_step, 0)
    load_b = load(w_down_ref.at[quarter], w_b, 6)
    load_a = load(w_up_ref.at[:, quarter], w_a, 7)

    settle(lat_flight)
    unit, _ = norm_parts(lat_all[...].reshape(4 * own_lat, features))
    lat_normed[...] = (unit * latent_gain).astype(bf16)
    load_c.wait()
    for cols in spans(groups):
        queries[:, cols] = (dot(lat_normed[...], w_c[:, cols]) * scale).astype(bf16)
    load_c = load(w_out_ref, w_c, 8)

    settle(cot_flight)
    own_cot = pl.ds(pl.multiple_of(d * 128, 128), 64)
    own_pre = pl.ds(pl.multiple_of(d * 128 + 64, 64), 64)
    rhs_all[own_cot, :] = cot_all[...].reshape(4 * own_lat, features)

    def to_plane(at, number):
        copies = [
            copy_to(rhs_all.at[at], rhs_all.at[at], spread_sems, (number, k), (z, p))
            for k, p in enumerate((x_peer, y_peer, xy_peer, pair))
        ]
        for copy in copies:
            copy.start()
        return copies

    def to_pair(low, number):
        copies = []
        for k, p in enumerate((x_peer, y_peer, xy_peer)):
            at = pl.ds(pl.multiple_of(p * 128 + low, 64), 64)
            copies.append(
                copy_to(rhs_all.at[at], rhs_all.at[at], spread_sems, (number, 4 + k), (z, pair))
            )
        for copy in copies:
            copy.start()
        return copies

    cot_plane = to_plane(own_cot, 0)

    masks = head_masks(4 * own_lat)
    lane = lax.broadcasted_iota(jnp.int32, (4 * own_lat, 128), 1)
    top_tile = jnp.zeros((4 * own_lat, 128), f32)
    sum_tile = jnp.ones((4 * own_lat, 128), f32)
    part_flight = []
    for g, cols in enumerate(spans(groups)):
        scores = dot_t(stacked(queries[:, cols], masks), keys[:, cols])
        scores = jnp.where(keep_row, scores, MASKED_SCORE)
        largest = jnp.max(scores, axis=-1, keepdims=True)
        expo = jnp.where(keep_row, jnp.exp(scores - largest), 0.0)
        total = jnp.sum(expo, axis=-1, keepdims=True)
        part = dot(expo.astype(bf16), values[:, cols])
        mixed = jnp.zeros((64, SPAN), f32)
        for h in range(GROUP):
            at = slice(64 * h, 64 * h + 64)
            mixed = mixed + jnp.where(masks[h], part[at], 0.0)
            top_tile = jnp.where(lane == GROUP * g + h, largest[at], top_tile)
            sum_tile = jnp.where(lane == GROUP * g + h, total[at], sum_tile)
        part_send[:, :, cols] = mixed.astype(bf16).reshape(4, own_lat, SPAN)
        if g % 2 == 1:
            wide = halves(features)[g // 2]
            part_flight += to_line(
                lambda p: part_send.at[p, :, wide], part_recv.at[z, :, wide]
            )
    stat_send[:, 0] = top_tile.reshape(4, own_lat, 128)
    stat_send[:, 1] = sum_tile.reshape(4, own_lat, 128)
    stat_flight = to_line(lambda p: stat_send.at[p], stat_recv.at[z])
    part_recv[z] = part_send[z]
    stat_recv[z] = stat_send[z]

    load_b.wait()
    for cols in spans(groups):
        act_grad[:, cols] = dot_t(cot_all[...].reshape(64, features), w_b[cols, :])
    for j in range(features // 128):
        place_transposed(
            rows_t, rows[:, 128 * j : 128 * j + 128].astype(f32).T.astype(bf16), 128 * j
        )

    settle(stat_flight)
    tops = stat_recv[:, 0]
    top = jnp.max(tops, axis=0)
    factor = jnp.exp(tops - top[None])
    denominator = jnp.sum(factor * stat_recv[:, 1], axis=0)
    log_total[...] = top + jnp.log(denominator)
    share = factor / denominator[None]
    settle(part_flight)
    own_masks = head_masks(own_lat)
    own_at = pl.ds(pl.multiple_of(z * own_lat, 16), own_lat)
    att_own = att_all.at[own_at]
    att_flight = []
    for g, cols in enumerate(spans(groups)):
        merged = jnp.zeros((own_lat, SPAN), f32)
        for j in range(4):
            spread = jnp.zeros((own_lat, SPAN), f32)
            for h in range(GROUP):
                n = GROUP * g + h
                spread = jnp.where(own_masks[h], share[j, :, n : n + 1], spread)
            merged = merged + spread * part_recv[j, :, cols].astype(f32)
        attended_f[:, cols] = merged
        att_own[:, cols] = merged.astype(bf16)
        if g % 2 == 1:
            wide = halves(features)[g // 2]
            att_flight.append(to_line(lambda p: att_own.at[:, wide], att_own.at[:, wide]))

    settle(cot_plane)
    cot_pair = to_pair(0, 0)
    for j in range(features // 128):
        place_transposed(
            lat_t, lat_normed[:, 128 * j : 128 * j + 128].astype(f32).T.astype(bf16), 128 * j
        )
    load_c.wait()
    load_a.wait()

    mid_all[...] = lat_all[...].reshape(64, features).astype(f32)
    for flight, deep in zip(att_flight, halves(features)):
        settle(flight)
        for cols in spans(groups):
            mid_all[:, cols] += dot(att_all[:, deep], w_c[deep, cols])
    unit, _ = norm_parts(mid_all[...])
    ffn_all[...] = (unit * ffn_gain).astype(bf16)

    for cols in spans(groups):
        pre = dot(ffn_all[...], w_a[:, cols])
        cdf = 0.5 * (1.0 + lax.erf(pre * (0.5**0.5)))
        act_all[:, cols] = (pre * cdf).astype(bf16)
        density = jnp.exp(-0.5 * pre * pre) * (0.5 / jnp.pi) ** 0.5
        pre_all[:, cols] = (act_grad[:, cols] * (cdf + pre * density)).astype(bf16)
    fig_flight = []
    for g, cols in enumerate(spans(groups)):
        part = dot_t(pre_all[...], w_a[cols, :])
        fig_f[:, :, cols] = part.reshape(4, own_lat, SPAN)
        fig_send[:, :, cols] = part.astype(bf16).reshape(4, own_lat, SPAN)
        if g % 2 == 1:
            wide = halves(features)[g // 2]
            fig_flight += to_line(
                lambda p: fig_send.at[p, :, wide], fig_recv.at[z, :, wide]
            )
    load_a = load(w_key_ref, w_a, 9)
    rhs_all[own_pre, :] = pre_all[...]
    pre_plane = to_plane(own_pre, 1)
    for cols in spans(groups):
        part = dot(act_all[...], w_b[:, cols])
        new_f[:, :, cols] = part.reshape(4, own_lat, SPAN)
        new_send[:, :, cols] = part.astype(bf16).reshape(4, own_lat, SPAN)
    load_b = load(w_value_ref, w_b, 10)
    for j in range(features // 128):
        place_transposed(
            att_t, att_all[:, 128 * j : 128 * j + 128].astype(f32).T.astype(bf16), 128 * j
        )

    settle(fig_flight)
    fig = fig_f[z]
    for p in peers:
        fig = fig + fig_recv[p].astype(f32)
    mid = mid_all[own_at, :]
    unit, inv = norm_parts(mid)
    gain_part[...] = jnp.zeros_like(gain_part)
    gain_part[2:3, :] = jnp.sum(fig * unit, axis=0, keepdims=True)
    mid_grad = cotangent_ref[...].astype(f32) + input_grad(fig, ffn_gain, unit, inv)
    mid_grad_own[...] = mid_grad
    branch_grad = mid_grad.astype(bf16)
    for n, cols in enumerate(spans(groups)):
        branch_send[n] = branch_grad[:, cols]
    branch_parts[z] = branch_send[z]
    own_lane = lax.broadcasted_iota(jnp.int32, (own_lat, 128), 1)
    delta = jnp.zeros((own_lat, 128), f32)
    for g, cols in enumerate(spans(groups)):
        grad = dot_t(branch_grad, w_c[cols, :]).astype(bf16)
        og_all[g, z] = grad
        product = grad.astype(f32) * attended_f[:, cols]
        for h in range(GROUP):
            summed = jnp.sum(jnp.where(own_masks[h], product, 0.0), axis=-1, keepdims=True)
            delta = jnp.where(own_lane == GROUP * g + h, summed, delta)
    st_all[z, 0] = log_total[...]
    st_all[z, 1] = delta
    st_flight = to_line(lambda p: st_all.at[z], st_all.at[z])
    branch_flight = to_line(lambda p: branch_send.at[p], branch_parts.at[z])
    og_flight = [to_line(lambda p: og_all.at[g, z], og_all.at[g, z]) for g in range(groups)]
    new_flight = to_line(lambda p: new_send.at[p], new_recv.at[z])
    load_c = load(w_query_ref, w_c, 11)

    order = [8, 0, 1, 2, 3, 9, 4, 5, 6, 7]
    slots = {ch: n % 6 for n, ch in enumerate(order)}
    flights = {}

    def send_pair(ch, left, right, factor=None):
        def product(core, half):
            part = dot(left[core, half * 384 : (half + 1) * 384, :], right)
            return part if factor is None else part * factor

        slot = slots[ch]
        for half in range(2):
            pair_send[slot, half * 384 : (half + 1) * 384, :] = product(1 - c, half).astype(bf16)
        copy = copy_to(pair_send.at[slot], pair_recv.at[slot], pair_sems, (ch,), (z, pair))
        copy.start()
        flights["pair", ch] = copy
        for half in range(2):
            own[ch, half] = product(c, half).astype(bf16).reshape(2, 192, SPAN)

    def add_to(view, block):
        view[...] = (view[...].astype(f32) + block.astype(f32)).astype(bf16)

    def pair_sum(ch):
        flights["pair", ch].wait()
        for bx in range(2):
            for by in range(2):
                at = bx * 384 + by * 192
                add_to(own.at[ch, bx, by], pair_recv[slots[ch], at : at + 192, :])
        if ch % 2 == 0:
            theirs, device = own.at[ch, 1 - x], x_peer
        else:
            theirs, device = own.at[ch, :, 1 - y], y_peer
        copy = copy_to(theirs, one_recv.at[ch], one_sems, (ch,), (z, device))
        copy.start()
        flights["one", ch] = copy

    def one_sum(ch):
        flights["one", ch].wait()
        for n in range(2):
            add_to(own.at[ch, x, n] if ch % 2 == 0 else own.at[ch, n, y], one_recv[ch, n])
        if ch % 2 == 0:
            theirs, device = own.at[ch, x, 1 - y], y_peer
        else:
            theirs, device = own.at[ch, 1 - x, y], x_peer
        copy = copy_to(theirs, two_recv.at[ch], two_sems, (ch,), (z, device))
        copy.start()
        flights["two", ch] = copy

    def two_sum(ch):
        flights["two", ch].wait()
        add_to(own.at[ch, x, y], two_recv[ch])
        copies = [
            copy_to(
                own.at[ch, x, y, pl.ds(pl.multiple_of(p * 48, 16), 48)],
                line_recv.at[ch, z],
                last_sems,
                (ch, k),
                (p, d),
            )
            for k, p in enumerate(peers)
        ]
        for copy in copies:
            copy.start()
        flights["line", ch] = copies
        line_recv[ch, z] = own[ch, x, y, pl.ds(pl.multiple_of(z * 48, 16), 48), :]

    def line_end(ch):
        settle(flights["line", ch])
        store(line_recv.at[ch], line_out.at[ch])

    def each(step, *chunks):
        for ch in chunks:
            step(ch)

    blank = jnp.zeros((64, 128), f32)
    for j in range(features // 128):
        cols = slice(128 * j, 128 * j + 128)
        tile = jnp.concatenate([act_all[:, cols].astype(f32), blank], axis=0).T.astype(bf16)
        for piece in range(8):
            row = 128 * j + 16 * piece
            lhs_send[row // 192, row % 192 : row % 192 + 16, :] = tile[
                16 * piece : 16 * piece + 16, :
            ]
    for j in range(features // 128):
        cols = slice(128 * j, 128 * j + 128)
        tile = jnp.concatenate([blank, ffn_all[:, cols].astype(f32)], axis=0).T.astype(bf16)
        for piece in range(8):
            row = 128 * j + 16 * piece
            block, off = row // 48, row % 48
            at = (block // 8) * 48 + off
            lhs_send[block % 8, at : at + 16, :] += tile[16 * piece : 16 * piece + 16, :]
    own_slot = pl.ds(pl.multiple_of(d * 128, 128), 128)
    lhs_flight = [
        copy_to(lhs_send.at[p], lhs_recv.at[:, own_slot], block_sems, (k,), (z, p))
        for k, p in enumerate(others)
    ]
    for item in lhs_flight:
        item.start()
    lhs_recv[:, own_slot] = lhs_send[d]

    settle(branch_flight)
    send_pair(8, att_t, branch_parts[...].reshape(64, SPAN))

    settle(st_flight)
    lane = lax.broadcasted_iota(jnp.int32, (64, 256), 1)
    row = lax.broadcasted_iota(jnp.int32, (64, 256), 0)
    for kind in range(2):
        tile = st_all[:, kind].reshape(64, 128)
        for g in range(groups):
            wide = jnp.zeros((64, 256), f32)
            for h in range(GROUP):
                n = GROUP * g + h
                wide = jnp.where(lane == row + 64 * h, tile[:, n : n + 1], wide)
            at = kind * groups + g
            stats[at : at + 1, :] = jnp.sum(wide, axis=0, keepdims=True)

    def attend_back(g):
        cols = spans(groups)[g]
        settle(og_flight[g])
        q_stack = stacked(queries[:, cols], masks)
        o_stack = stacked(og_all[g].reshape(64, SPAN), masks)
        scores = dot_t(keys[:, cols], q_stack)
        keep = valid[:, 0:1] > 0.0
        exact = jnp.where(keep, jnp.exp(scores - stats[g : g + 1, :]), 0.0)
        prob_grad = dot_t(values[:, cols], o_stack)
        score_grad = (exact * (prob_grad - stats[4 + g : 5 + g, :])).astype(bf16)
        value_grad[:, cols] = dot(exact.astype(bf16), o_stack).astype(bf16)
        key_grad[:, cols] = dot(score_grad, q_stack).astype(bf16)
        q_part = outer_sum(score_grad, keys[:, cols])
        q_sum = jnp.zeros((64, SPAN), f32)
        for h in range(GROUP):
            q_sum = q_sum + jnp.where(masks[h], q_part[64 * h : 64 * h + 64], 0.0)
        query_parts[g] = q_sum
        query_send[g] = q_sum.astype(bf16)

    def weigh(g):
        cols = spans(groups)[g]
        send_pair(2 * g, rows_t, value_grad[:, cols])
        send_pair(2 * g + 1, rows_t, key_grad[:, cols])

    pair_sum(8)
    attend_back(0)
    weigh(0)
    settle(cot_pair)
    settle(pre_plane)
    pre_pair = to_pair(64, 1)
    attend_back(1)
    each(pair_sum, 0, 1)
    attend_back(2)
    attend_back(3)
    query_flight = to_line(lambda p: query_send.at[p], query_recv.at[z])
    weigh(1)
    each(pair_sum, 2, 3)
    one_sum(8)

    settle(new_flight)
    new = mid_all[own_at, :] + new_f[z]
    for p in peers:
        new = new + new_recv[p].astype(f32)
    small_out[0] = new.astype(bf16)
    store(small_out.at[0], new_latents_out)

    settle(query_flight)
    total = query_parts[z]
    for p in peers:
        total = total + query_recv[p].astype(f32)
    total = total.astype(bf16)
    back_send[...] = total.reshape(4, own_lat, SPAN)
    back_recv[z] = back_send[z]
    back_flight = to_line(lambda p: back_send.at[p], back_recv.at[z])
    send_pair(9, lat_t, total, scale)
    each(one_sum, 1, 0)
    pair_sum(9)
    weigh(2)
    each(pair_sum, 4, 5)

    settle(lhs_flight)
    settle(pre_pair)
    lane = lax.broadcasted_iota(jnp.int32, lhs_recv.shape, 1) % 128
    left = lhs_recv[...]
    act_left = jnp.where(lane < 64, left, jnp.zeros_like(left))
    ffn_left = jnp.where(lane >= 64, left, jnp.zeros_like(left))
    for cols in spans(groups):
        up_part[:, :, cols] = dot(ffn_left, rhs_all[:, cols]).astype(bf16).reshape(4, 48, SPAN)
    up_flight = to_line(lambda p: up_part.at[p], up_recv.at[z])
    up_recv[z] = up_part[z]
    for cols in spans(groups):
        down_part[:, cols] = dot(act_left, rhs_all[:, cols])
    store(down_part, down_out)
    each(one_sum, 3, 2)
    each(two_sum, 8)

    load_a.wait()
    load_b.wait()

    def back_step(n, carry):
        at = pl.ds(pl.multiple_of(n * SPAN, SPAN), SPAN)
        rows_grad[:, at] = dot_t(key_grad[...], w_a[at, :]) + dot_t(value_grad[...], w_b[at, :])
        return carry

    lax.fori_loop(0, groups // 2, back_step, 0)
    one_sum(9)
    each(two_sum, 1, 0)
    weigh(3)
    each(pair_sum, 6, 7)
    lax.fori_loop(groups // 2, groups, back_step, 0)
    each(one_sum, 5, 4)
    each(two_sum, 3, 2)

    def back_norm_step(n, total):
        at = pl.ds(pl.multiple_of(n * 64, 64), 64)
        unit, inv = norm_parts(media_ref[at, :])
        grad = rows_grad[at, :]
        rows[at, :] = input_grad(grad, gains[0:1, :], unit, inv).astype(bf16)
        return total + jnp.sum(grad * unit, axis=0, keepdims=True)

    gain_part[0:1, :] = lax.fori_loop(
        0, own_rows // 64, back_norm_step, jnp.zeros((1, features), f32)
    )
    store(rows.at[pl.ds(0, own_rows)], media_grad_out)
    two_sum(9)

    settle(back_flight)
    load_c.wait()
    lat_grad = rows_grad[own_rows:, :]
    for n, cols in enumerate(spans(groups)):
        lat_grad = lat_grad + scale * dot_t(back_recv[n], w_c[:, cols])
    unit, inv = norm_parts(latents_ref[...])
    small_out[1] = (
        mid_grad_own[...] + input_grad(lat_grad, latent_gain, unit, inv)
    ).astype(bf16)
    store(small_out.at[1], latent_grad_out)
    gain_part[1:2, :] = jnp.sum(lat_grad * unit, axis=0, keepdims=True)
    for n, cols in enumerate(spans(groups)):
        gain_sum[n] = gain_part[:, cols]
    gain_flight = to_line(lambda p: gain_sum.at[p], gain_recv.at[z])
    each(one_sum, 7, 6)
    each(line_end, 8, 1, 0, 3, 2)
    settle(up_flight)
    store(up_recv, up_out)
    each(two_sum, 5, 4)
    settle(gain_flight)
    total = gain_sum[z]
    for p in peers:
        total = total + gain_recv[p]
    gain_all[d] = total
    gain_spread = [
        copy_to(gain_all.at[d], gain_all.at[d], spread_sems, (2, k), (z, p))
        for k, p in enumerate(others)
    ]
    for item in gain_spread:
        item.start()
    each(two_sum, 7, 6)
    settle(gain_spread)
    gain_part[:, 0:SPAN] = jnp.sum(gain_all[...], axis=0)
    store(gain_part, gains_out)
    each(line_end, 9, 5, 4, 7, 6)
    settle(stores)


def finish_kernel(
    new_in,
    media_in,
    latent_in,
    line_in,
    up_in,
    down_in,
    gains_in,
    new_out,
    media_out,
    latent_out,
    query_out,
    key_out,
    value_out,
    out_out,
    up_out,
    down_out,
    gains_out,
    new_room,
    media_room,
    latent_room,
    down_room,
    line_room,
    up_room,
    gains_room,
    squares,
    up_wide,
    gains_own,
    in_sems,
    out_sems,
):
    f32 = jnp.float32
    rooms = [line_room, media_room, down_room, up_room, new_room, latent_room, gains_room]
    sources = [line_in, media_in, down_in, up_in, new_in, latent_in, gains_in]
    arrivals = [
        pltpu.make_async_copy(src, dst, in_sems.at[n])
        for n, (src, dst) in enumerate(zip(sources, rooms))
    ]
    for copy in arrivals:
        copy.start()
    leaving = []

    def leave(src, dst):
        copy = pltpu.make_async_copy(src, dst, out_sems.at[len(leaving)])
        copy.start()
        leaving.append(copy)

    arrivals[0].wait()
    for n, cols in enumerate(spans(4)):
        squares[0, :, cols] = line_room[9, n].astype(f32)
        squares[1, :, cols] = jnp.sum(line_room[2 * n + 1].astype(f32), axis=0)
        squares[2, :, cols] = jnp.sum(line_room[2 * n].astype(f32), axis=0)
        squares[3, :, cols] = line_room[8, n].astype(f32)
    for n, dst in enumerate((query_out, key_out, value_out, out_out)):
        leave(squares.at[n], dst)
    arrivals[1].wait()
    leave(media_room, media_out)
    arrivals[2].wait()
    leave(down_room, down_out)
    arrivals[3].wait()
    features = up_in.shape[2]
    for n in range(4):
        up_wide[:, n * features : (n + 1) * features] = up_room[n].astype(f32)
    leave(up_wide, up_out)
    arrivals[4].wait()
    leave(new_room, new_out)
    arrivals[5].wait()
    leave(latent_room, latent_out)
    arrivals[6].wait()
    share = query_out.shape[0]
    start = lax.axis_index("dp") * share
    base = pl.multiple_of((start // 128) * 128, 128)
    window = gains_room[:, pl.ds(base, 256)]
    gains_own[...] = pltpu.roll(window, (256 - start % 128) % 256, 1)
    leave(gains_own, gains_out)
    settle(leaving)


def layer(operands, own_rows, own_lat, features):
    bf16, f32 = jnp.bfloat16, jnp.float32
    count = own_rows + own_lat
    lat_rows = 4 * own_lat
    share = features // 32
    vmem = pl.BlockSpec(memory_space=pltpu.VMEM)
    smem = pl.BlockSpec(memory_space=pltpu.SMEM)
    anyway = pl.BlockSpec(memory_space=pl.ANY)

    def array(kind, *shape):
        return jax.ShapeDtypeStruct(shape, kind)

    def room(kind, *shape):
        return pltpu.VMEM(shape, kind)

    def dma(*shape):
        return pltpu.SemaphoreType.DMA(shape)

    outs = (
        array(bf16, own_lat, features),
        array(bf16, own_rows, features),
        array(bf16, own_lat, features),
        array(bf16, 10, 4, share, SPAN),
        array(bf16, 4, share, features),
        array(f32, 4 * share, features),
        array(f32, 8, features),
    )
    scratch = dict(
        gains=room(f32, 8, features),
        w_a=room(bf16, features, features),
        w_b=room(bf16, features, features),
        w_c=room(bf16, features, features),
        rows=room(bf16, count, features),
        keys=room(bf16, count, features),
        values=room(bf16, count, features),
        queries=room(bf16, lat_rows, features),
        stats=room(f32, 8, 256),
        valid=room(f32, count, 128),
        lat_normed=room(bf16, lat_rows, features),
        lat_all=room(bf16, 4, own_lat, features),
        cot_all=room(bf16, 4, own_lat, features),
        att_all=room(bf16, lat_rows, features),
        part_send=room(bf16, 4, own_lat, features),
        part_recv=room(bf16, 4, own_lat, features),
        stat_send=room(f32, 4, 2, own_lat, 128),
        stat_recv=room(f32, 4, 2, own_lat, 128),
        attended_f=room(f32, own_lat, features),
        log_total=room(f32, own_lat, 128),
        mid_all=room(f32, lat_rows, features),
        act_grad=room(f32, lat_rows, features),
        act_all=room(bf16, lat_rows, features),
        pre_all=room(bf16, lat_rows, features),
        ffn_all=room(bf16, lat_rows, features),
        fig_f=room(f32, 4, own_lat, features),
        fig_send=room(bf16, 4, own_lat, features),
        fig_recv=room(bf16, 4, own_lat, features),
        new_f=room(f32, 4, own_lat, features),
        new_send=room(bf16, 4, own_lat, features),
        new_recv=room(bf16, 4, own_lat, features),
        mid_grad_own=room(f32, own_lat, features),
        rhs_all=room(bf16, 1024, features),
        lhs_send=room(bf16, 8, 4 * share, 128),
        lhs_recv=room(bf16, 4 * share, 1024),
        og_all=room(bf16, 4, 4, own_lat, SPAN),
        st_all=room(f32, 4, 2, own_lat, 128),
        branch_send=room(bf16, 4, own_lat, SPAN),
        branch_parts=room(bf16, 4, own_lat, SPAN),
        small_out=room(bf16, 2, own_lat, features),
        down_part=room(f32, 4 * share, features),
        up_part=room(bf16, 4, share, features),
        up_recv=room(bf16, 4, share, features),
        rows_t=room(bf16, 2, features // 2, count),
        lat_t=room(bf16, 2, features // 2, lat_rows),
        att_t=room(bf16, 2, features // 2, lat_rows),
        key_grad=room(bf16, count, features),
        value_grad=room(bf16, count, features),
        rows_grad=room(f32, count, features),
        query_parts=room(f32, 4, lat_rows, SPAN),
        query_send=room(bf16, 4, lat_rows, SPAN),
        query_recv=room(bf16, 4, lat_rows, SPAN),
        back_send=room(bf16, 4, own_lat, SPAN),
        back_recv=room(bf16, 4, own_lat, SPAN),
        pair_send=room(bf16, 6, 768, SPAN),
        pair_recv=room(bf16, 6, 768, SPAN),
        own=room(bf16, 10, 2, 2, 192, SPAN),
        one_recv=room(bf16, 10, 2, 192, SPAN),
        two_recv=room(bf16, 10, 192, SPAN),
        line_recv=room(bf16, 10, 4, share, SPAN),
        gain_part=room(f32, 8, features),
        gain_recv=room(f32, 4, 8, SPAN),
        gain_sum=room(f32, 4, 8, SPAN),
        gain_all=room(f32, 8, 8, SPAN),
        load_sems=dma(12),
        store_sems=dma(16),
        line_sems=dma(2, 20, 3),
        spread_sems=dma(2, 3, 7),
        block_sems=dma(2, 7),
        pair_sems=dma(2, 10),
        one_sems=dma(2, 10),
        two_sems=dma(2, 10),
        last_sems=dma(2, 10, 3),
    )
    staged = pl.pallas_call(
        layer_kernel,
        out_shape=outs,
        in_specs=[vmem] * 4 + [smem] + [anyway] * 9,
        out_specs=(anyway,) * len(outs),
        scratch_shapes=tuple(scratch.values()),
        compiler_params=pltpu.CompilerParams(
            collective_id=0, has_side_effects=True, vmem_limit_bytes=63 * 1024 * 1024
        ),
    )(*operands)
    square = array(f32, share, features)
    return pl.pallas_call(
        finish_kernel,
        out_shape=outs[:3]
        + (square,) * 4
        + (array(f32, share, 4 * features), outs[5], array(f32, 8, 256)),
        in_specs=[anyway] * 7,
        out_specs=(anyway,) * 10,
        scratch_shapes=[
            room(bf16, own_lat, features),
            room(bf16, own_rows, features),
            room(bf16, own_lat, features),
            room(f32, 4 * share, features),
            room(bf16, 10, 4, share, SPAN),
            room(bf16, 4, share, features),
            room(f32, 8, features),
            room(f32, 4, share, features),
            room(f32, share, 4 * features),
            room(f32, 8, 256),
            dma(7),
            dma(10),
        ],
        compiler_params=pltpu.CompilerParams(vmem_limit_bytes=63 * 1024 * 1024),
    )(*staged)


def spread_body(
    media,
    latents,
    frame_counts,
    media_mask,
    media_gain,
    latent_gain,
    ffn_gain,
    w_query,
    w_key,
    w_value,
    w_out,
    w_up,
    w_down,
    cotangent,
):
    _, own_rows, features = media.shape
    own_lat = latents.shape[1]
    seq_parts = lax.axis_size("seq")
    seq_index = lax.axis_index("seq")
    device_count = seq_parts * lax.axis_size("dp")
    both = ("seq", "dp")
    heads = features // HEAD_DIM
    score_scale = HEAD_DIM ** (-0.5)
    bf16 = jnp.bfloat16

    media, latents, cotangent = media[0], latents[0], cotangent[0]
    own_mask = lax.dynamic_slice_in_dim(media_mask[0], seq_index * own_rows, own_rows, 0)
    row_frame = (seq_index * own_rows + jnp.arange(own_rows, dtype=jnp.int32)) // PATCH
    own_valid = (own_mask > 0) & (row_frame < frame_counts[0])
    valid = jnp.concatenate([own_valid, jnp.ones((own_lat,), jnp.bool_)])[None, None, :]

    all_cotangent = lax.all_gather(cotangent, both, axis=0, tiled=True)

    latents_f = latents.astype(jnp.float32)
    latent_unit, latent_inv = normalize(latents_f)
    latent_normed = (latent_unit * latent_gain).astype(bf16)
    own_queries = (dot(latent_normed, w_query) * score_scale).astype(bf16)
    queries = lax.all_gather(own_queries, "seq", axis=0, tiled=True)

    media_unit, media_inv = normalize(media.astype(jnp.float32))
    media_normed = (media_unit * media_gain).astype(bf16)
    rows = jnp.concatenate([media_normed, latent_normed], axis=0)
    keys = dot(rows, w_key).astype(bf16)
    values = dot(rows, w_value).astype(bf16)

    scores = jnp.where(valid, head_products(queries, keys), MASKED_SCORE)
    largest = jnp.max(scores, axis=-1)
    expo = jnp.where(valid, jnp.exp(scores - largest[..., None]), 0.0)
    total = jnp.sum(expo, axis=-1)
    part = weighted(expo.astype(bf16), values)
    packed = jnp.concatenate([part, largest.T, total.T], axis=1)
    packed = lax.all_to_all(packed, "seq", split_axis=0, concat_axis=0, tiled=True)
    packed = packed.reshape(seq_parts, own_lat, -1)
    parts = packed[..., :features]
    maxima = packed[..., features : features + heads]
    totals = packed[..., features + heads :]
    top = jnp.max(maxima, axis=0)
    factor = jnp.exp(maxima - top)
    denominator = jnp.sum(factor * totals, axis=0)
    log_total = top + jnp.log(denominator)
    share = jnp.repeat(factor / denominator, HEAD_DIM, axis=-1)
    attended_f = jnp.sum(parts * share, axis=0)
    attended = attended_f.astype(bf16)

    mid = latents_f + dot(attended, w_out)
    mid_unit, mid_inv = normalize(mid)
    ffn_in = (mid_unit * ffn_gain).astype(bf16)
    pre = dot(ffn_in, w_up)
    act = gelu_exact(pre).astype(bf16)
    new_latents = (mid + dot(act, w_down)).astype(bf16)
    act_grad = dot_t(cotangent, w_down)
    pre_grad = jax.vjp(gelu_exact, pre)[1](act_grad)[0].astype(bf16)
    all_pre_grad = lax.all_gather(pre_grad, both, axis=0, tiled=True)
    ffn_in_grad = dot_t(pre_grad, w_up)
    mid_back, grad_ffn_gain = norm_back(ffn_in_grad, ffn_gain, mid_unit, mid_inv)
    mid_grad = cotangent.astype(jnp.float32) + mid_back
    branch_grad = mid_grad.astype(bf16)
    all_branch = lax.all_gather(branch_grad, both, axis=0, tiled=True)
    attended_grad = dot_t(branch_grad, w_out).astype(bf16)
    own_delta = jnp.sum(
        split_heads(attended_f * attended_grad.astype(jnp.float32)), axis=-1
    )
    out_grad = lax.all_gather(attended_grad, "seq", axis=0, tiled=True)
    stats = lax.all_gather(
        jnp.concatenate([log_total, own_delta], axis=1), "seq", axis=0, tiled=True
    )
    lse = stats[:, :heads].T[..., None]
    delta = stats[:, heads:].T[..., None]

    exact = jnp.where(valid, jnp.exp(scores - lse), 0.0)
    score_grad = (exact * (head_products(out_grad, values) - delta)).astype(bf16)
    value_grad = transposed(exact.astype(bf16), out_grad).astype(bf16)
    key_grad = transposed(score_grad, queries).astype(bf16)
    query_part = weighted(score_grad, keys)
    query_grad = lax.psum_scatter(
        query_part, "seq", scatter_dimension=0, tiled=True
    ).astype(bf16)
    all_query_grad = lax.all_gather(query_grad, both, axis=0, tiled=True)
    part_value = outer_sum(rows, value_grad).astype(bf16)
    part_key = outer_sum(rows, key_grad).astype(bf16)
    sum_value = lax.psum_scatter(part_value, both, scatter_dimension=0, tiled=True)
    sum_key = lax.psum_scatter(part_key, both, scatter_dimension=0, tiled=True)

    rows_grad = dot_t(key_grad, w_key) + dot_t(value_grad, w_value)
    media_back, grad_media_gain = norm_back(
        rows_grad[:own_rows], media_gain, media_unit, media_inv
    )
    media_grad = media_back.astype(bf16)
    latent_normed_grad = rows_grad[own_rows:] + dot_t(query_grad, w_query) * score_scale
    latent_back, grad_latent_gain = norm_back(
        latent_normed_grad, latent_gain, latent_unit, latent_inv
    )
    latent_grad = (mid_grad + latent_back).astype(bf16)

    def by_owner(tensor):
        return tensor.reshape(tensor.shape[0], device_count, -1)

    sent = jnp.concatenate(
        [by_owner(latent_normed), by_owner(attended), by_owner(ffn_in), by_owner(act)], axis=2
    )
    got = lax.all_to_all(sent, both, split_axis=1, concat_axis=0, tiled=True)
    got = got.reshape(-1, got.shape[-1])
    block = features // device_count
    grad_query = outer_sum(got[:, :block], all_query_grad) * score_scale
    grad_out = outer_sum(got[:, block : 2 * block], all_branch)
    grad_up = outer_sum(got[:, 2 * block : 3 * block], all_pre_grad)
    grad_down = outer_sum(got[:, 3 * block :], all_cotangent)

    gains = jnp.stack([grad_media_gain, grad_latent_gain, grad_ffn_gain])
    gains = by_owner(gains).transpose(1, 0, 2).reshape(device_count, -1)
    gains = lax.all_to_all(gains, both, split_axis=0, concat_axis=0, tiled=True)
    gains = jnp.sum(gains.reshape(device_count, 3, -1), axis=0)
    return (
        new_latents[None],
        media_grad[None],
        latent_grad[None],
        grad_query,
        sum_key.astype(jnp.float32),
        sum_value.astype(jnp.float32),
        grad_out,
        grad_up,
        grad_down,
        gains[0],
        gains[1],
        gains[2],
    )


def body(
    media,
    latents,
    frame_counts,
    media_mask,
    media_gain,
    latent_gain,
    ffn_gain,
    w_query,
    w_key,
    w_value,
    w_out,
    w_up,
    w_down,
    cotangent,
):
    _, own_rows, features = media.shape
    own_lat = latents.shape[1]
    seq_parts, dp_parts = lax.axis_size("seq"), lax.axis_size("dp")
    if (seq_parts, dp_parts, own_lat, features) != (4, 8, 16, 4 * SPAN):
        return spread_body(
            media,
            latents,
            frame_counts,
            media_mask,
            media_gain,
            latent_gain,
            ffn_gain,
            w_query,
            w_key,
            w_value,
            w_out,
            w_up,
            w_down,
            cotangent,
        )
    (
        new_latents,
        media_grad,
        latent_grad,
        grad_query,
        grad_key,
        grad_value,
        grad_out,
        grad_up,
        grad_down,
        gains,
    ) = layer(
        (
            media[0],
            latents[0],
            cotangent[0],
            media_mask,
            frame_counts,
            media_gain,
            latent_gain,
            ffn_gain,
            w_query,
            w_key,
            w_value,
            w_out,
            w_up,
            w_down,
        ),
        own_rows,
        own_lat,
        features,
    )
    share = grad_query.shape[0]
    return (
        new_latents[None],
        media_grad[None],
        latent_grad[None],
        grad_query,
        grad_key,
        grad_value,
        grad_out,
        grad_up,
        grad_down,
        gains[0, :share],
        gains[1, :share],
        gains[2, :share],
    )


def solution(mesh):
    return jax.shard_map(
        body,
        mesh=mesh,
        in_specs=(
            P("dp", "seq", None),
            P("dp", "seq", None),
            P("dp"),
            P("dp", None),
            P(),
            P(),
            P(),
            P(),
            P(),
            P(),
            P(),
            P(),
            P(),
            P("dp", "seq", None),
        ),
        out_specs=(
            P("dp", "seq", None),
            P("dp", "seq", None),
            P("dp", "seq", None),
            P(("seq", "dp"), None),
            P(("seq", "dp"), None),
            P(("seq", "dp"), None),
            P(("seq", "dp"), None),
            P(("seq", "dp"), None),
            P(("seq", "dp"), None),
            P(("seq", "dp")),
            P(("seq", "dp")),
            P(("seq", "dp")),
        ),
        check_vma=False,
    )
```

```python
import jax
import jax.numpy as jnp
from jax import lax
from jax.experimental import pallas as pl
from jax.experimental.pallas import tpu as pltpu
from jax.sharding import PartitionSpec as P

HEAD_DIM = 96
PATCH = 256


MASKED_SCORE = -1e30


def normalize(tensor):
    centered = tensor - jnp.mean(tensor, axis=-1, keepdims=True)
    inv = lax.rsqrt(jnp.mean(centered * centered, axis=-1, keepdims=True) + 1e-05)
    return centered * inv, inv


def norm_back(grad, gain_vec, unit, inv):
    scaled = grad * gain_vec
    inner = jnp.mean(scaled * unit, axis=-1, keepdims=True)
    input_grad = inv * (scaled - jnp.mean(scaled, axis=-1, keepdims=True) - unit * inner)
    return input_grad, jnp.sum(grad * unit, axis=0)


def gelu_exact(tensor):
    return jax.nn.gelu(tensor, approximate=False)


def dot(left_op, right_op):
    return jnp.dot(left_op, right_op, preferred_element_type=jnp.float32)


def dot_t(left_op, right_op):
    return lax.dot_general(
        left_op, right_op, (((1,), (1,)), ((), ())), preferred_element_type=jnp.float32
    )


def outer_sum(left_op, right_op):
    return lax.dot_general(
        left_op, right_op, (((0,), (0,)), ((), ())), preferred_element_type=jnp.float32
    )


def split_heads(tensor):
    return tensor.reshape(tensor.shape[0], -1, HEAD_DIM)


def head_products(left_op, right_op):
    return jnp.einsum(
        "qhd,khd->hqk",
        split_heads(left_op),
        split_heads(right_op),
        preferred_element_type=jnp.float32,
    )


def weighted(weights_tab, rows):
    result = jnp.einsum(
        "hqk,khd->qhd", weights_tab, split_heads(rows), preferred_element_type=jnp.float32
    )
    return result.reshape(result.shape[0], -1)


def transposed(weights_tab, rows):
    result = jnp.einsum(
        "hqk,qhd->khd", weights_tab, split_heads(rows), preferred_element_type=jnp.float32
    )
    return result.reshape(result.shape[0], -1)


MESH = pl.DeviceIdType.MESH
GROUP = 4
SPAN = GROUP * HEAD_DIM


def norm_parts(block):
    block = block.astype(jnp.float32)
    centered = block - jnp.mean(block, axis=-1, keepdims=True)
    inv = lax.rsqrt(jnp.mean(centered * centered, axis=-1, keepdims=True) + 1e-05)
    return centered * inv, inv


def input_grad(grad, gain, unit, inv):
    scaled = grad * gain
    inner = jnp.mean(scaled * unit, axis=-1, keepdims=True)
    return inv * (scaled - jnp.mean(scaled, axis=-1, keepdims=True) - unit * inner)


def head_masks(count):
    lane = lax.broadcasted_iota(jnp.int32, (count, SPAN), 1)
    return [(lane >= h * HEAD_DIM) & (lane < (h + 1) * HEAD_DIM) for h in range(GROUP)]


def stacked(tensor, masks):
    return jnp.concatenate(
        [jnp.where(mask, tensor, jnp.zeros_like(tensor)) for mask in masks], axis=0
    )


def copy_to(src, dst, sems, index, device):
    return pltpu.make_async_remote_copy(
        src_ref=src,
        dst_ref=dst,
        send_sem=sems.at[(0,) + index],
        recv_sem=sems.at[(1,) + index],
        device_id=device,
        device_id_type=MESH,
    )


def spans(count):
    return [slice(n * SPAN, (n + 1) * SPAN) for n in range(count)]


def halves(features):
    return [slice(0, features // 2), slice(features // 2, features)]


def settle(copies):
    for copy in copies:
        copy.wait()


def place_transposed(dest, tile, column):
    for piece in range(8):
        row = column + 16 * piece
        block, off = row // 48, row % 48
        bz, by, bx, bc = block // 8, (block // 4) % 2, (block // 2) % 2, block % 2
        at = bx * 384 + by * 192 + bz * 48 + off
        dest[bc, at : at + 16, :] = tile[16 * piece : 16 * piece + 16, :]


def layer_kernel(
    media_in,
    latents_in,
    cotangent_in,
    mask_in,
    frames_ref,
    media_gain_ref,
    latent_gain_ref,
    ffn_gain_ref,
    w_query_ref,
    w_key_ref,
    w_value_ref,
    w_out_ref,
    w_up_ref,
    w_down_ref,
    new_latents_out,
    media_grad_out,
    latent_grad_out,
    line_out,
    up_out,
    down_out,
    gains_out,
    media_ref,
    latents_ref,
    cotangent_ref,
    mask_ref,
    gains,
    w_a,
    w_b,
    w_c,
    rows,
    keys,
    values,
    queries,
    stats,
    valid,
    lat_normed,
    lat_all,
    cot_all,
    att_all,
    part_send,
    part_recv,
    stat_send,
    stat_recv,
    attended_f,
    log_total,
    mid_all,
    act_grad,
    act_all,
    pre_all,
    ffn_all,
    fig_f,
    fig_send,
    fig_recv,
    new_f,
    new_send,
    new_recv,
    mid_grad_own,
    rhs_all,
    lhs_send,
    lhs_recv,
    og_all,
    st_all,
    branch_send,
    branch_parts,
    small_out,
    down_part,
    up_part,
    up_recv,
    rows_t,
    lat_lhs,
    lat_got,
    rhs_branch,
    rhs_query,
    place_send,
    key_grad,
    value_grad,
    rows_grad,
    query_parts,
    query_send,
    query_recv,
    back_send,
    back_recv,
    pair_send,
    pair_recv,
    own,
    one_recv,
    two_recv,
    line_recv,
    gain_part,
    gain_recv,
    gain_sum,
    gain_all,
    load_sems,
    store_sems,
    line_sems,
    spread_sems,
    block_sems,
    pair_sems,
    one_sems,
    two_sems,
    last_sems,
):
    bf16, f32 = jnp.bfloat16, jnp.float32
    z = lax.axis_index("seq")
    d = lax.axis_index("dp")
    y, x, c = d // 4, (d // 2) % 2, d % 2
    own_lat = latents_ref.shape[0]
    own_rows, features = media_ref.shape
    groups = features // SPAN
    scale = HEAD_DIM ** (-0.5)
    pair = d + 1 - 2 * c
    x_peer = d + 2 * (1 - 2 * x)
    y_peer = d + 4 * (1 - 2 * y)
    xy_peer = 4 * (1 - y) + 2 * (1 - x) + c
    peers = [(z + k) % 4 for k in (1, 2, 3)]
    others = [(d + k) % 8 for k in range(1, 8)]

    quarter = pl.ds(pl.multiple_of(z * features, 128), features)

    def load(src, dst, number):
        copy = pltpu.make_async_copy(src, dst, load_sems.at[number])
        copy.start()
        return copy

    early = [
        load(media_in, media_ref, 12),
        load(latents_in, latents_ref, 13),
        load(cotangent_in, cotangent_ref, 14),
        load(mask_in, mask_ref, 15),
        load(media_gain_ref, gains.at[0], 0),
        load(latent_gain_ref, gains.at[1], 1),
        load(ffn_gain_ref, gains.at[2], 2),
    ]
    load_a = load(w_key_ref, w_a, 3)
    load_b = load(w_value_ref, w_b, 4)
    load_c = load(w_query_ref, w_c, 5)

    stores = []

    def store(src, dst):
        copy = pltpu.make_async_copy(src, dst, store_sems.at[len(stores)])
        copy.start()
        stores.append(copy)

    barrier = pltpu.get_barrier_semaphore()
    for device in [(p, d) for p in peers] + [(z, p) for p in others]:
        pl.semaphore_signal(barrier, inc=1, device_id=device, device_id_type=MESH)

    lines = []

    def to_line(src_of, dst):
        number = len(lines)
        lines.append(number)
        copies = [
            copy_to(src_of(p), dst, line_sems, (number, k), (p, d)) for k, p in enumerate(peers)
        ]
        for copy in copies:
            copy.start()
        return copies

    settle(early)
    frame = (z * own_rows + lax.broadcasted_iota(jnp.int32, (1, own_rows), 1)) // PATCH
    own_mask = mask_ref[:, pl.ds(pl.multiple_of(z * own_rows, 128), own_rows)]
    kept = jnp.where((own_mask > 0) & (frame < frames_ref[0]), 1.0, 0.0)
    valid[0:own_rows, :] = jnp.broadcast_to(kept, (128, own_rows)).T
    valid[own_rows:, :] = jnp.ones((own_lat, 128), f32)
    keep_row = jnp.concatenate([kept, jnp.ones((1, own_lat), f32)], axis=1) > 0.0

    media_gain, latent_gain, ffn_gain = gains[0:1, :], gains[1:2, :], gains[2:3, :]

    def norm_step(n, carry):
        at = pl.ds(pl.multiple_of(n * 64, 64), 64)
        unit, _ = norm_parts(media_ref[at, :])
        rows[at, :] = (unit * gains[0:1, :]).astype(bf16)
        return carry

    lax.fori_loop(0, own_rows // 64, norm_step, 0)
    pl.semaphore_wait(barrier, 10)
    lat_all[z] = latents_ref[...]
    cot_all[z] = cotangent_ref[...]
    lat_flight = to_line(lambda p: lat_all.at[z], lat_all.at[z])

    unit, _ = norm_parts(latents_ref[...])
    rows[own_rows:, :] = (unit * latent_gain).astype(bf16)

    load_a.wait()
    load_b.wait()

    def project_step(n, carry):
        at = pl.ds(pl.multiple_of(n * 2 * SPAN, 2 * SPAN), 2 * SPAN)
        keys[:, at] = dot(rows[...], w_a[:, at]).astype(bf16)
        values[:, at] = dot(rows[...], w_b[:, at]).astype(bf16)
        return carry

    lax.fori_loop(0, groups // 2, project_step, 0)
    load_b = load(w_down_ref.at[quarter], w_b, 6)
    load_a = load(w_up_ref.at[:, quarter], w_a, 7)

    settle(lat_flight)
    cot_flight = to_line(lambda p: cot_all.at[z], cot_all.at[z])
    unit, _ = norm_parts(lat_all[...].reshape(4 * own_lat, features))
    lat_normed[...] = (unit * latent_gain).astype(bf16)
    load_c.wait()
    for cols in halves(features):
        queries[:, cols] = (dot(lat_normed[...], w_c[:, cols]) * scale).astype(bf16)
    load_c = load(w_out_ref, w_c, 8)

    def to_plane(ref, at, number):
        copies = [
            copy_to(ref.at[at], ref.at[at], spread_sems, (number, k), (z, p))
            for k, p in enumerate((x_peer, y_peer, xy_peer, pair))
        ]
        for copy in copies:
            copy.start()
        return copies

    def to_pair(ref, low, number):
        copies = []
        for k, p in enumerate((x_peer, y_peer, xy_peer)):
            at = pl.ds(pl.multiple_of(p * 128 + low, 64), 64)
            copies.append(copy_to(ref.at[at], ref.at[at], spread_sems, (number, 4 + k), (z, pair)))
        for copy in copies:
            copy.start()
        return copies

    blank = jnp.zeros((64, 128), f32)

    def place_blocks(dest, source, side, spread=True):
        for j in range(features // 128):
            tile = source[:, 128 * j : 128 * j + 128].astype(f32)
            tile = jnp.concatenate([blank, tile] if side else [tile, blank], axis=0)
            tile = tile.T.astype(bf16)
            for piece in range(8):
                row = 128 * j + 16 * piece
                if spread:
                    block, off = row // 48, row % 48
                    owner, at = block % 8, (block // 8) * 48 + off
                else:
                    owner, at = row // 192, row % 192
                part = tile[16 * piece : 16 * piece + 16, :]
                if side:
                    dest[owner, at : at + 16, :] += part
                else:
                    dest[owner, at : at + 16, :] = part

    def spread_blocks(source, dest, number):
        slot = pl.ds(pl.multiple_of(d * 128, 128), 128)
        copies = [
            copy_to(source.at[p], dest.at[:, slot], block_sems, (number, k), (z, p))
            for k, p in enumerate(others)
        ]
        for copy in copies:
            copy.start()
        dest[:, slot] = source[d]
        return copies

    def sides(ref):
        lane = lax.broadcasted_iota(jnp.int32, ref.shape, 1) % 128
        left = ref[...]
        none = jnp.zeros_like(left)
        return jnp.where(lane < 64, left, none), jnp.where(lane >= 64, left, none)

    masks = head_masks(4 * own_lat)
    lane = lax.broadcasted_iota(jnp.int32, (4 * own_lat, 128), 1)
    top_tile = jnp.zeros((4 * own_lat, 128), f32)
    sum_tile = jnp.ones((4 * own_lat, 128), f32)
    part_flight = []
    for g, cols in enumerate(spans(groups)):
        scores = dot_t(stacked(queries[:, cols], masks), keys[:, cols])
        scores = jnp.where(keep_row, scores, MASKED_SCORE)
        largest = jnp.max(scores, axis=-1, keepdims=True)
        expo = jnp.where(keep_row, jnp.exp(scores - largest), 0.0)
        total = jnp.sum(expo, axis=-1, keepdims=True)
        part = dot(expo.astype(bf16), values[:, cols])
        mixed = jnp.zeros((64, SPAN), f32)
        for h in range(GROUP):
            at = slice(64 * h, 64 * h + 64)
            mixed = mixed + jnp.where(masks[h], part[at], 0.0)
            top_tile = jnp.where(lane == GROUP * g + h, largest[at], top_tile)
            sum_tile = jnp.where(lane == GROUP * g + h, total[at], sum_tile)
        part_send[:, :, cols] = mixed.astype(bf16).reshape(4, own_lat, SPAN)
        if g % 2 == 1:
            wide = halves(features)[g // 2]
            part_flight += to_line(
                lambda p: part_send.at[p, :, wide], part_recv.at[z, :, wide]
            )
    stat_send[:, 0] = top_tile.reshape(4, own_lat, 128)
    stat_send[:, 1] = sum_tile.reshape(4, own_lat, 128)
    stat_flight = to_line(lambda p: stat_send.at[p], stat_recv.at[z])
    part_recv[z] = part_send[z]
    stat_recv[z] = stat_send[z]

    settle(cot_flight)
    own_cot = pl.ds(pl.multiple_of(d * 128, 128), 64)
    own_pre = pl.ds(pl.multiple_of(d * 128 + 64, 64), 64)
    rhs_all[own_cot, :] = cot_all[...].reshape(4 * own_lat, features)

    cot_plane = to_plane(rhs_all, own_cot, 0)
    load_b.wait()
    for cols in halves(features):
        act_grad[:, cols] = dot_t(cot_all[...].reshape(64, features), w_b[cols, :])
    for j in range(features // 128):
        place_transposed(
            rows_t, rows[:, 128 * j : 128 * j + 128].astype(f32).T.astype(bf16), 128 * j
        )

    settle(stat_flight)
    tops = stat_recv[:, 0]
    top = jnp.max(tops, axis=0)
    factor = jnp.exp(tops - top[None])
    denominator = jnp.sum(factor * stat_recv[:, 1], axis=0)
    log_total[...] = top + jnp.log(denominator)
    share = factor / denominator[None]
    settle(part_flight)
    own_masks = head_masks(own_lat)
    own_at = pl.ds(pl.multiple_of(z * own_lat, 16), own_lat)
    att_own = att_all.at[own_at]
    att_flight = []
    for g, cols in enumerate(spans(groups)):
        merged = jnp.zeros((own_lat, SPAN), f32)
        for j in range(4):
            spread = jnp.zeros((own_lat, SPAN), f32)
            for h in range(GROUP):
                n = GROUP * g + h
                spread = jnp.where(own_masks[h], share[j, :, n : n + 1], spread)
            merged = merged + spread * part_recv[j, :, cols].astype(f32)
        attended_f[:, cols] = merged
        att_own[:, cols] = merged.astype(bf16)
        if g % 2 == 1:
            wide = halves(features)[g // 2]
            att_flight.append(to_line(lambda p: att_own.at[:, wide], att_own.at[:, wide]))

    settle(cot_plane)
    cot_pair = to_pair(rhs_all, 0, 0)
    place_blocks(lat_lhs, lat_normed, 0)
    for n in range(8):
        rhs_branch[128 * n : 128 * n + 64, :] = jnp.zeros((64, SPAN), bf16)
        rhs_query[128 * n + 64 : 128 * n + 128, :] = jnp.zeros((64, SPAN), bf16)
    load_c.wait()
    load_a.wait()

    mid_all[...] = lat_all[...].reshape(64, features).astype(f32)
    for flight, deep in zip(att_flight, halves(features)):
        settle(flight)
        for cols in halves(features):
            mid_all[:, cols] += dot(att_all[:, deep], w_c[deep, cols])
    unit, _ = norm_parts(mid_all[...])
    ffn_all[...] = (unit * ffn_gain).astype(bf16)

    for cols in halves(features):
        pre = dot(ffn_all[...], w_a[:, cols])
        cdf = 0.5 * (1.0 + lax.erf(pre * (0.5**0.5)))
        act_all[:, cols] = (pre * cdf).astype(bf16)
        density = jnp.exp(-0.5 * pre * pre) * (0.5 / jnp.pi) ** 0.5
        pre_all[:, cols] = (act_grad[:, cols] * (cdf + pre * density)).astype(bf16)
    fig_flight = []
    for wide in halves(features):
        part = dot_t(pre_all[...], w_a[wide, :])
        fig_f[:, :, wide] = part.reshape(4, own_lat, 2 * SPAN)
        fig_send[:, :, wide] = part.astype(bf16).reshape(4, own_lat, 2 * SPAN)
        fig_flight += to_line(lambda p: fig_send.at[p, :, wide], fig_recv.at[z, :, wide])
    load_a = load(w_key_ref, w_a, 9)
    rhs_all[own_pre, :] = pre_all[...]
    pre_plane = to_plane(rhs_all, own_pre, 1)
    for cols in halves(features):
        part = dot(act_all[...], w_b[:, cols])
        new_f[:, :, cols] = part.reshape(4, own_lat, 2 * SPAN)
        new_send[:, :, cols] = part.astype(bf16).reshape(4, own_lat, 2 * SPAN)
    flights = {}
    flights["new"] = to_line(lambda p: new_send.at[p], new_recv.at[z])
    load_b = load(w_value_ref, w_b, 10)
    place_blocks(lat_lhs, att_all, 1)
    lat_blocks = spread_blocks(lat_lhs, lat_got, 1)

    settle(fig_flight)
    fig = fig_f[z]
    for p in peers:
        fig = fig + fig_recv[p].astype(f32)
    mid = mid_all[own_at, :]
    unit, inv = norm_parts(mid)
    gain_part[...] = jnp.zeros_like(gain_part)
    gain_part[2:3, :] = jnp.sum(fig * unit, axis=0, keepdims=True)
    mid_grad = cotangent_ref[...].astype(f32) + input_grad(fig, ffn_gain, unit, inv)
    mid_grad_own[...] = mid_grad
    branch_grad = mid_grad.astype(bf16)
    for n, cols in enumerate(spans(groups)):
        branch_send[n] = branch_grad[:, cols]
    branch_parts[z] = branch_send[z]
    own_lane = lax.broadcasted_iota(jnp.int32, (own_lat, 128), 1)
    delta = jnp.zeros((own_lat, 128), f32)
    grads = [dot_t(branch_grad, w_c[wide, :]).astype(bf16) for wide in halves(features)]
    for g, cols in enumerate(spans(groups)):
        grad = grads[g // 2][:, g % 2 * SPAN : g % 2 * SPAN + SPAN]
        og_all[g, z] = grad
        product = grad.astype(f32) * attended_f[:, cols]
        for h in range(GROUP):
            summed = jnp.sum(jnp.where(own_masks[h], product, 0.0), axis=-1, keepdims=True)
            delta = jnp.where(own_lane == GROUP * g + h, summed, delta)
    st_all[z, 0] = log_total[...]
    st_all[z, 1] = delta
    st_flight = to_line(lambda p: st_all.at[z], st_all.at[z])
    branch_flight = to_line(lambda p: branch_send.at[p], branch_parts.at[z])
    og_flight = [to_line(lambda p: og_all.at[g, z], og_all.at[g, z]) for g in range(groups)]
    load_c = load(w_query_ref, w_c, 11)

    slots = {ch: ch % 6 for ch in range(2 * groups)}

    def weigh(g):
        cols = spans(groups)[g]
        right = jnp.concatenate([value_grad[:, cols], key_grad[:, cols]], axis=1)
        chunks = (2 * g, 2 * g + 1)
        for half in range(2):
            at = slice(half * 384, (half + 1) * 384)
            part = dot(rows_t[1 - c, at, :], right).astype(bf16)
            for n, ch in enumerate(chunks):
                pair_send[slots[ch], at, :] = part[:, n * SPAN : (n + 1) * SPAN]
        for ch in chunks:
            slot = slots[ch]
            copy = copy_to(pair_send.at[slot], pair_recv.at[slot], pair_sems, (ch,), (z, pair))
            copy.start()
            flights["pair", ch] = copy
        for half in range(2):
            at = slice(half * 384, (half + 1) * 384)
            part = dot(rows_t[c, at, :], right).astype(bf16)
            for n, ch in enumerate(chunks):
                own[ch, half] = part[:, n * SPAN : (n + 1) * SPAN].reshape(2, 192, SPAN)

    def add_to(view, block):
        view[...] = (view[...].astype(f32) + block.astype(f32)).astype(bf16)

    def pair_sum(ch):
        flights["pair", ch].wait()
        for bx in range(2):
            for by in range(2):
                at = bx * 384 + by * 192
                add_to(own.at[ch, bx, by], pair_recv[slots[ch], at : at + 192, :])
        if ch % 2 == 0:
            theirs, device = own.at[ch, 1 - x], x_peer
        else:
            theirs, device = own.at[ch, :, 1 - y], y_peer
        copy = copy_to(theirs, one_recv.at[ch], one_sems, (ch,), (z, device))
        copy.start()
        flights["one", ch] = copy

    def one_sum(ch):
        flights["one", ch].wait()
        for n in range(2):
            add_to(own.at[ch, x, n] if ch % 2 == 0 else own.at[ch, n, y], one_recv[ch, n])
        if ch % 2 == 0:
            theirs, device = own.at[ch, x, 1 - y], y_peer
        else:
            theirs, device = own.at[ch, 1 - x, y], x_peer
        copy = copy_to(theirs, two_recv.at[ch], two_sems, (ch,), (z, device))
        copy.start()
        flights["two", ch] = copy

    def two_sum(ch):
        flights["two", ch].wait()
        add_to(own.at[ch, x, y], two_recv[ch])
        copies = [
            copy_to(
                own.at[ch, x, y, pl.ds(pl.multiple_of(p * 48, 16), 48)],
                line_recv.at[ch, z],
                last_sems,
                (ch, k),
                (p, d),
            )
            for k, p in enumerate(peers)
        ]
        for copy in copies:
            copy.start()
        flights["line", ch] = copies
        line_recv[ch, z] = own[ch, x, y, pl.ds(pl.multiple_of(z * 48, 16), 48), :]

    def line_end(ch):
        settle(flights["line", ch])
        store(line_recv.at[ch], line_out.at[ch])

    def each(step, *chunks):
        for ch in chunks:
            step(ch)

    place_blocks(lhs_send, act_all, 0, spread=False)
    place_blocks(lhs_send, ffn_all, 1)
    lhs_flight = spread_blocks(lhs_send, lhs_recv, 0)

    settle(st_flight)
    lane = lax.broadcasted_iota(jnp.int32, (64, 256), 1)
    row = lax.broadcasted_iota(jnp.int32, (64, 256), 0)
    for kind in range(2):
        tile = st_all[:, kind].reshape(64, 128)
        for g in range(groups):
            wide = jnp.zeros((64, 256), f32)
            for h in range(GROUP):
                n = GROUP * g + h
                wide = jnp.where(lane == row + 64 * h, tile[:, n : n + 1], wide)
            at = kind * groups + g
            stats[at : at + 1, :] = jnp.sum(wide, axis=0, keepdims=True)

    def attend_back(g):
        cols = spans(groups)[g]
        settle(og_flight[g])
        q_stack = stacked(queries[:, cols], masks)
        o_stack = stacked(og_all[g].reshape(64, SPAN), masks)
        scores = dot_t(keys[:, cols], q_stack)
        keep = valid[:, 0:1] > 0.0
        exact = jnp.where(keep, jnp.exp(scores - stats[g : g + 1, :]), 0.0)
        prob_grad = dot_t(values[:, cols], o_stack)
        score_grad = (exact * (prob_grad - stats[4 + g : 5 + g, :])).astype(bf16)
        value_grad[:, cols] = dot(exact.astype(bf16), o_stack).astype(bf16)
        key_grad[:, cols] = dot(score_grad, q_stack).astype(bf16)
        q_part = outer_sum(score_grad, keys[:, cols])
        q_sum = jnp.zeros((64, SPAN), f32)
        for h in range(GROUP):
            q_sum = q_sum + jnp.where(masks[h], q_part[64 * h : 64 * h + 64], 0.0)
        query_parts[g] = q_sum
        query_send[g] = q_sum.astype(bf16)

    def forward_pre(_):
        settle(cot_pair)
        settle(pre_plane)
        flights["pre"] = to_pair(rhs_all, 64, 1)

    def new_rows(_):
        settle(flights["new"])
        new = mid_all[own_at, :] + new_f[z]
        for p in peers:
            new = new + new_recv[p].astype(f32)
        small_out[0] = new.astype(bf16)
        store(small_out.at[0], new_latents_out)

    def query_leave(_):
        flights["query"] = to_line(lambda p: query_send.at[p], query_recv.at[z])

    own_top = pl.ds(pl.multiple_of(d * 128, 128), 64)
    own_low = pl.ds(pl.multiple_of(d * 128 + 64, 64), 64)

    def branch_spread(_):
        settle(branch_flight)
        rhs_branch[own_low, :] = branch_parts[...].reshape(64, SPAN)
        flights["branch"] = to_plane(rhs_branch, own_low, 3)

    def branch_pair(_):
        settle(flights["branch"])
        flights["branch"] = to_pair(rhs_branch, 64, 3)

    def place(ch, part):
        place_send[ch - 8] = part.astype(bf16).reshape(4, 48, SPAN)
        flights["line", ch] = [
            copy_to(place_send.at[ch - 8, p], line_recv.at[ch, z], last_sems, (ch, k), (p, d))
            for k, p in enumerate(peers)
        ]
        for copy in flights["line", ch]:
            copy.start()
        line_recv[ch, z] = place_send[ch - 8, z]

    def branch_weigh(_):
        settle(lat_blocks)
        settle(flights["branch"])
        place(8, dot(lat_got[...], rhs_branch[...]))

    def query_spread(_):
        settle(flights["query"])
        total = query_parts[z]
        for p in peers:
            total = total + query_recv[p].astype(f32)
        total = total.astype(bf16)
        back_send[...] = total.reshape(4, own_lat, SPAN)
        back_recv[z] = back_send[z]
        flights["back"] = to_line(lambda p: back_send.at[p], back_recv.at[z])
        rhs_query[own_top, :] = total
        flights["rows"] = to_plane(rhs_query, own_top, 4)

    def query_pair(_):
        settle(flights["rows"])
        flights["rows"] = to_pair(rhs_query, 0, 4)

    def query_weigh(_):
        settle(flights["rows"])
        place(9, scale * dot(lat_got[...], rhs_query[...]))

    def up_down(_):
        settle(lhs_flight)
        settle(flights["pre"])
        act_left, ffn_left = sides(lhs_recv)
        for cols in halves(features):
            part = dot(ffn_left, rhs_all[:, cols])
            up_part[:, :, cols] = part.astype(bf16).reshape(4, 48, 2 * SPAN)
        flights["up"] = to_line(lambda p: up_part.at[p], up_recv.at[z])
        up_recv[z] = up_part[z]
        for cols in halves(features):
            down_part[:, cols] = dot(act_left, rhs_all[:, cols])
        store(down_part, down_out)

    def back_step(n, carry):
        at = pl.ds(pl.multiple_of(n * 2 * SPAN, 2 * SPAN), 2 * SPAN)
        rows_grad[:, at] = dot_t(key_grad[...], w_a[at, :]) + dot_t(value_grad[...], w_b[at, :])
        return carry

    def back_half(n):
        if n == 0:
            load_a.wait()
            load_b.wait()
        lax.fori_loop(n, n + 1, back_step, 0)

    def back_norm_step(n, total):
        at = pl.ds(pl.multiple_of(n * 64, 64), 64)
        unit, inv = norm_parts(media_ref[at, :])
        grad = rows_grad[at, :]
        rows[at, :] = input_grad(grad, gains[0:1, :], unit, inv).astype(bf16)
        return total + jnp.sum(grad * unit, axis=0, keepdims=True)

    def back_norm(_):
        gain_part[0:1, :] = lax.fori_loop(
            0, own_rows // 64, back_norm_step, jnp.zeros((1, features), f32)
        )
        store(rows.at[pl.ds(0, own_rows)], media_grad_out)

    def latent_rows(_):
        settle(flights["back"])
        load_c.wait()
        lat_grad = rows_grad[own_rows:, :]
        for n, cols in enumerate(spans(groups)):
            lat_grad = lat_grad + scale * dot_t(back_recv[n], w_c[:, cols])
        unit, inv = norm_parts(latents_ref[...])
        grad = input_grad(lat_grad, latent_gain, unit, inv)
        small_out[1] = (mid_grad_own[...] + grad).astype(bf16)
        store(small_out.at[1], latent_grad_out)
        gain_part[1:2, :] = jnp.sum(lat_grad * unit, axis=0, keepdims=True)
        for n, cols in enumerate(spans(groups)):
            gain_sum[n] = gain_part[:, cols]
        flights["gain"] = to_line(lambda p: gain_sum.at[p], gain_recv.at[z])

    def up_end(_):
        settle(flights["up"])
        store(up_recv, up_out)

    def gain_middle(_):
        settle(flights["gain"])
        total = gain_sum[z]
        for p in peers:
            total = total + gain_recv[p]
        gain_all[d] = total
        flights["spread"] = [
            copy_to(gain_all.at[d], gain_all.at[d], spread_sems, (2, k), (z, p))
            for k, p in enumerate(others)
        ]
        for item in flights["spread"]:
            item.start()

    def gain_end(_):
        settle(flights["spread"])
        gain_part[:, 0:SPAN] = jnp.sum(gain_all[...], axis=0)
        store(gain_part, gains_out)

    branch_spread(0)
    forward_pre(0)
    attend_back(0)
    weigh(0)
    up_down(0)
    pair_sum(0)
    attend_back(1)
    pair_sum(1)
    weigh(1)
    attend_back(2)
    attend_back(3)
    query_leave(0)
    pair_sum(2)
    branch_pair(0)
    pair_sum(3)
    branch_weigh(0)
    weigh(2)
    one_sum(1)
    weigh(3)
    one_sum(0)
    back_half(0)
    one_sum(3)
    one_sum(2)
    pair_sum(5)
    pair_sum(4)
    query_spread(0)
    two_sum(1)
    two_sum(0)
    back_half(1)
    back_norm(0)
    pair_sum(6)
    two_sum(2)
    one_sum(4)
    two_sum(3)
    new_rows(0)
    one_sum(5)
    line_end(1)
    line_end(0)
    query_pair(0)
    pair_sum(7)
    query_weigh(0)
    latent_rows(0)
    line_end(8)
    two_sum(4)
    line_end(3)
    one_sum(6)
    gain_middle(0)
    two_sum(5)
    one_sum(7)
    two_sum(6)
    two_sum(7)
    gain_end(0)
    line_end(7)
    up_end(0)
    line_end(2)
    line_end(4)
    line_end(6)
    line_end(9)
    line_end(5)
    settle(stores)


def finish_kernel(
    new_in,
    media_in,
    latent_in,
    line_in,
    up_in,
    down_in,
    gains_in,
    new_out,
    media_out,
    latent_out,
    query_out,
    key_out,
    value_out,
    out_out,
    up_out,
    down_out,
    media_gain_out,
    latent_gain_out,
    ffn_gain_out,
    new_room,
    media_room,
    latent_room,
    down_room,
    line_room,
    up_room,
    gains_room,
    squares,
    up_wide,
    in_sems,
    out_sems,
):
    f32 = jnp.float32
    rooms = [line_room, media_room, down_room, up_room, new_room, latent_room, gains_room]
    sources = [line_in, media_in, down_in, up_in, new_in, latent_in, gains_in]
    arrivals = [
        pltpu.make_async_copy(src, dst, in_sems.at[n])
        for n, (src, dst) in enumerate(zip(sources, rooms))
    ]
    for copy in arrivals:
        copy.start()
    leaving = []

    def leave(src, dst):
        copy = pltpu.make_async_copy(src, dst, out_sems.at[len(leaving)])
        copy.start()
        leaving.append(copy)

    arrivals[0].wait()
    for n, cols in enumerate(spans(4)):
        squares[0, :, cols] = line_room[9, n].astype(f32)
        squares[1, :, cols] = jnp.sum(line_room[2 * n + 1].astype(f32), axis=0)
        squares[2, :, cols] = jnp.sum(line_room[2 * n].astype(f32), axis=0)
        squares[3, :, cols] = line_room[8, n].astype(f32)
    for n, dst in enumerate((query_out, key_out, value_out, out_out)):
        leave(squares.at[n], dst)
    arrivals[1].wait()
    leave(media_room, media_out)
    arrivals[2].wait()
    leave(down_room, down_out)
    arrivals[3].wait()
    features = up_in.shape[2]
    for n in range(4):
        up_wide[:, n * features : (n + 1) * features] = up_room[n].astype(f32)
    leave(up_wide, up_out)
    arrivals[4].wait()
    leave(new_room, new_out)
    arrivals[5].wait()
    leave(latent_room, latent_out)
    arrivals[6].wait()
    share = query_out.shape[0]
    start = lax.axis_index("dp") * share
    base = pl.multiple_of((start // 128) * 128, 128)
    window = gains_room[:, pl.ds(base, 256)]
    window = pltpu.roll(window, (256 - start % 128) % 256, 1)
    media_gain_out[...] = window[0, :share]
    latent_gain_out[...] = window[1, :share]
    ffn_gain_out[...] = window[2, :share]
    settle(leaving)


def layer(operands, own_rows, own_lat, features):
    bf16, f32 = jnp.bfloat16, jnp.float32
    count = own_rows + own_lat
    lat_rows = 4 * own_lat
    share = features // 32
    vmem = pl.BlockSpec(memory_space=pltpu.VMEM)
    smem = pl.BlockSpec(memory_space=pltpu.SMEM)
    anyway = pl.BlockSpec(memory_space=pl.ANY)

    def array(kind, *shape):
        return jax.ShapeDtypeStruct(shape, kind)

    def room(kind, *shape):
        return pltpu.VMEM(shape, kind)

    def dma(*shape):
        return pltpu.SemaphoreType.DMA(shape)

    outs = (
        array(bf16, own_lat, features),
        array(bf16, own_rows, features),
        array(bf16, own_lat, features),
        array(bf16, 10, 4, share, SPAN),
        array(bf16, 4, share, features),
        array(f32, 4 * share, features),
        array(f32, 8, features),
    )
    scratch = dict(
        media_ref=room(bf16, own_rows, features),
        latents_ref=room(bf16, own_lat, features),
        cotangent_ref=room(bf16, own_lat, features),
        mask_ref=room(jnp.int32, 1, 4 * own_rows),
        gains=room(f32, 8, features),
        w_a=room(bf16, features, features),
        w_b=room(bf16, features, features),
        w_c=room(bf16, features, features),
        rows=room(bf16, count, features),
        keys=room(bf16, count, features),
        values=room(bf16, count, features),
        queries=room(bf16, lat_rows, features),
        stats=room(f32, 8, 256),
        valid=room(f32, count, 128),
        lat_normed=room(bf16, lat_rows, features),
        lat_all=room(bf16, 4, own_lat, features),
        cot_all=room(bf16, 4, own_lat, features),
        att_all=room(bf16, lat_rows, features),
        part_send=room(bf16, 4, own_lat, features),
        part_recv=room(bf16, 4, own_lat, features),
        stat_send=room(f32, 4, 2, own_lat, 128),
        stat_recv=room(f32, 4, 2, own_lat, 128),
        attended_f=room(f32, own_lat, features),
        log_total=room(f32, own_lat, 128),
        mid_all=room(f32, lat_rows, features),
        act_grad=room(f32, lat_rows, features),
        act_all=room(bf16, lat_rows, features),
        pre_all=room(bf16, lat_rows, features),
        ffn_all=room(bf16, lat_rows, features),
        fig_f=room(f32, 4, own_lat, features),
        fig_send=room(bf16, 4, own_lat, features),
        fig_recv=room(bf16, 4, own_lat, features),
        new_f=room(f32, 4, own_lat, features),
        new_send=room(bf16, 4, own_lat, features),
        new_recv=room(bf16, 4, own_lat, features),
        mid_grad_own=room(f32, own_lat, features),
        rhs_all=room(bf16, 1024, features),
        lhs_send=room(bf16, 8, 4 * share, 128),
        lhs_recv=room(bf16, 4 * share, 1024),
        og_all=room(bf16, 4, 4, own_lat, SPAN),
        st_all=room(f32, 4, 2, own_lat, 128),
        branch_send=room(bf16, 4, own_lat, SPAN),
        branch_parts=room(bf16, 4, own_lat, SPAN),
        small_out=room(bf16, 2, own_lat, features),
        down_part=room(f32, 4 * share, features),
        up_part=room(bf16, 4, share, features),
        up_recv=room(bf16, 4, share, features),
        rows_t=room(bf16, 2, features // 2, count),
        lat_lhs=room(bf16, 8, 4 * share, 128),
        lat_got=room(bf16, 4 * share, 1024),
        rhs_branch=room(bf16, 1024, SPAN),
        rhs_query=room(bf16, 1024, SPAN),
        place_send=room(bf16, 2, 4, share, SPAN),
        key_grad=room(bf16, count, features),
        value_grad=room(bf16, count, features),
        rows_grad=room(f32, count, features),
        query_parts=room(f32, 4, lat_rows, SPAN),
        query_send=room(bf16, 4, lat_rows, SPAN),
        query_recv=room(bf16, 4, lat_rows, SPAN),
        back_send=room(bf16, 4, own_lat, SPAN),
        back_recv=room(bf16, 4, own_lat, SPAN),
        pair_send=room(bf16, 6, 768, SPAN),
        pair_recv=room(bf16, 6, 768, SPAN),
        own=room(bf16, 8, 2, 2, 192, SPAN),
        one_recv=room(bf16, 8, 2, 192, SPAN),
        two_recv=room(bf16, 8, 192, SPAN),
        line_recv=room(bf16, 10, 4, share, SPAN),
        gain_part=room(f32, 8, features),
        gain_recv=room(f32, 4, 8, SPAN),
        gain_sum=room(f32, 4, 8, SPAN),
        gain_all=room(f32, 8, 8, SPAN),
        load_sems=dma(16),
        store_sems=dma(16),
        line_sems=dma(2, 20, 3),
        spread_sems=dma(2, 5, 7),
        block_sems=dma(2, 2, 7),
        pair_sems=dma(2, 8),
        one_sems=dma(2, 8),
        two_sems=dma(2, 8),
        last_sems=dma(2, 10, 3),
    )
    staged = pl.pallas_call(
        layer_kernel,
        out_shape=outs,
        in_specs=[anyway] * 4 + [smem] + [anyway] * 9,
        out_specs=(anyway,) * len(outs),
        scratch_shapes=tuple(scratch.values()),
        compiler_params=pltpu.CompilerParams(
            collective_id=0, has_side_effects=True, vmem_limit_bytes=63 * 1024 * 1024
        ),
    )(*operands)
    square = array(f32, share, features)
    return pl.pallas_call(
        finish_kernel,
        out_shape=outs[:3]
        + (square,) * 4
        + (array(f32, share, 4 * features), outs[5])
        + (array(f32, share),) * 3,
        in_specs=[anyway] * 7,
        out_specs=(anyway,) * 9 + (vmem,) * 3,
        scratch_shapes=[
            room(bf16, own_lat, features),
            room(bf16, own_rows, features),
            room(bf16, own_lat, features),
            room(f32, 4 * share, features),
            room(bf16, 10, 4, share, SPAN),
            room(bf16, 4, share, features),
            room(f32, 8, features),
            room(f32, 4, share, features),
            room(f32, share, 4 * features),
            dma(7),
            dma(9),
        ],
        compiler_params=pltpu.CompilerParams(vmem_limit_bytes=63 * 1024 * 1024),
    )(*staged)


def spread_body(
    media,
    latents,
    frame_counts,
    media_mask,
    media_gain,
    latent_gain,
    ffn_gain,
    w_query,
    w_key,
    w_value,
    w_out,
    w_up,
    w_down,
    cotangent,
):
    _, own_rows, features = media.shape
    own_lat = latents.shape[1]
    seq_parts = lax.axis_size("seq")
    seq_index = lax.axis_index("seq")
    device_count = seq_parts * lax.axis_size("dp")
    both = ("seq", "dp")
    heads = features // HEAD_DIM
    score_scale = HEAD_DIM ** (-0.5)
    bf16 = jnp.bfloat16

    media, latents, cotangent = media[0], latents[0], cotangent[0]
    own_mask = lax.dynamic_slice_in_dim(media_mask[0], seq_index * own_rows, own_rows, 0)
    row_frame = (seq_index * own_rows + jnp.arange(own_rows, dtype=jnp.int32)) // PATCH
    own_valid = (own_mask > 0) & (row_frame < frame_counts[0])
    valid = jnp.concatenate([own_valid, jnp.ones((own_lat,), jnp.bool_)])[None, None, :]

    all_cotangent = lax.all_gather(cotangent, both, axis=0, tiled=True)

    latents_f = latents.astype(jnp.float32)
    latent_unit, latent_inv = normalize(latents_f)
    latent_normed = (latent_unit * latent_gain).astype(bf16)
    own_queries = (dot(latent_normed, w_query) * score_scale).astype(bf16)
    queries = lax.all_gather(own_queries, "seq", axis=0, tiled=True)

    media_unit, media_inv = normalize(media.astype(jnp.float32))
    media_normed = (media_unit * media_gain).astype(bf16)
    rows = jnp.concatenate([media_normed, latent_normed], axis=0)
    keys = dot(rows, w_key).astype(bf16)
    values = dot(rows, w_value).astype(bf16)

    scores = jnp.where(valid, head_products(queries, keys), MASKED_SCORE)
    largest = jnp.max(scores, axis=-1)
    expo = jnp.where(valid, jnp.exp(scores - largest[..., None]), 0.0)
    total = jnp.sum(expo, axis=-1)
    part = weighted(expo.astype(bf16), values)
    packed = jnp.concatenate([part, largest.T, total.T], axis=1)
    packed = lax.all_to_all(packed, "seq", split_axis=0, concat_axis=0, tiled=True)
    packed = packed.reshape(seq_parts, own_lat, -1)
    parts = packed[..., :features]
    maxima = packed[..., features : features + heads]
    totals = packed[..., features + heads :]
    top = jnp.max(maxima, axis=0)
    factor = jnp.exp(maxima - top)
    denominator = jnp.sum(factor * totals, axis=0)
    log_total = top + jnp.log(denominator)
    share = jnp.repeat(factor / denominator, HEAD_DIM, axis=-1)
    attended_f = jnp.sum(parts * share, axis=0)
    attended = attended_f.astype(bf16)

    mid = latents_f + dot(attended, w_out)
    mid_unit, mid_inv = normalize(mid)
    ffn_in = (mid_unit * ffn_gain).astype(bf16)
    pre = dot(ffn_in, w_up)
    act = gelu_exact(pre).astype(bf16)
    new_latents = (mid + dot(act, w_down)).astype(bf16)
    act_grad = dot_t(cotangent, w_down)
    pre_grad = jax.vjp(gelu_exact, pre)[1](act_grad)[0].astype(bf16)
    all_pre_grad = lax.all_gather(pre_grad, both, axis=0, tiled=True)
    ffn_in_grad = dot_t(pre_grad, w_up)
    mid_back, grad_ffn_gain = norm_back(ffn_in_grad, ffn_gain, mid_unit, mid_inv)
    mid_grad = cotangent.astype(jnp.float32) + mid_back
    branch_grad = mid_grad.astype(bf16)
    all_branch = lax.all_gather(branch_grad, both, axis=0, tiled=True)
    attended_grad = dot_t(branch_grad, w_out).astype(bf16)
    own_delta = jnp.sum(
        split_heads(attended_f * attended_grad.astype(jnp.float32)), axis=-1
    )
    out_grad = lax.all_gather(attended_grad, "seq", axis=0, tiled=True)
    stats = lax.all_gather(
        jnp.concatenate([log_total, own_delta], axis=1), "seq", axis=0, tiled=True
    )
    lse = stats[:, :heads].T[..., None]
    delta = stats[:, heads:].T[..., None]

    exact = jnp.where(valid, jnp.exp(scores - lse), 0.0)
    score_grad = (exact * (head_products(out_grad, values) - delta)).astype(bf16)
    value_grad = transposed(exact.astype(bf16), out_grad).astype(bf16)
    key_grad = transposed(score_grad, queries).astype(bf16)
    query_part = weighted(score_grad, keys)
    query_grad = lax.psum_scatter(
        query_part, "seq", scatter_dimension=0, tiled=True
    ).astype(bf16)
    all_query_grad = lax.all_gather(query_grad, both, axis=0, tiled=True)
    part_value = outer_sum(rows, value_grad).astype(bf16)
    part_key = outer_sum(rows, key_grad).astype(bf16)
    sum_value = lax.psum_scatter(part_value, both, scatter_dimension=0, tiled=True)
    sum_key = lax.psum_scatter(part_key, both, scatter_dimension=0, tiled=True)

    rows_grad = dot_t(key_grad, w_key) + dot_t(value_grad, w_value)
    media_back, grad_media_gain = norm_back(
        rows_grad[:own_rows], media_gain, media_unit, media_inv
    )
    media_grad = media_back.astype(bf16)
    latent_normed_grad = rows_grad[own_rows:] + dot_t(query_grad, w_query) * score_scale
    latent_back, grad_latent_gain = norm_back(
        latent_normed_grad, latent_gain, latent_unit, latent_inv
    )
    latent_grad = (mid_grad + latent_back).astype(bf16)

    def by_owner(tensor):
        return tensor.reshape(tensor.shape[0], device_count, -1)

    sent = jnp.concatenate(
        [by_owner(latent_normed), by_owner(attended), by_owner(ffn_in), by_owner(act)], axis=2
    )
    got = lax.all_to_all(sent, both, split_axis=1, concat_axis=0, tiled=True)
    got = got.reshape(-1, got.shape[-1])
    block = features // device_count
    grad_query = outer_sum(got[:, :block], all_query_grad) * score_scale
    grad_out = outer_sum(got[:, block : 2 * block], all_branch)
    grad_up = outer_sum(got[:, 2 * block : 3 * block], all_pre_grad)
    grad_down = outer_sum(got[:, 3 * block :], all_cotangent)

    gains = jnp.stack([grad_media_gain, grad_latent_gain, grad_ffn_gain])
    gains = by_owner(gains).transpose(1, 0, 2).reshape(device_count, -1)
    gains = lax.all_to_all(gains, both, split_axis=0, concat_axis=0, tiled=True)
    gains = jnp.sum(gains.reshape(device_count, 3, -1), axis=0)
    return (
        new_latents[None],
        media_grad[None],
        latent_grad[None],
        grad_query,
        sum_key.astype(jnp.float32),
        sum_value.astype(jnp.float32),
        grad_out,
        grad_up,
        grad_down,
        gains[0],
        gains[1],
        gains[2],
    )


def body(
    media,
    latents,
    frame_counts,
    media_mask,
    media_gain,
    latent_gain,
    ffn_gain,
    w_query,
    w_key,
    w_value,
    w_out,
    w_up,
    w_down,
    cotangent,
):
    _, own_rows, features = media.shape
    own_lat = latents.shape[1]
    seq_parts, dp_parts = lax.axis_size("seq"), lax.axis_size("dp")
    if (seq_parts, dp_parts, own_lat, features) != (4, 8, 16, 4 * SPAN):
        return spread_body(
            media,
            latents,
            frame_counts,
            media_mask,
            media_gain,
            latent_gain,
            ffn_gain,
            w_query,
            w_key,
            w_value,
            w_out,
            w_up,
            w_down,
            cotangent,
        )
    (
        new_latents,
        media_grad,
        latent_grad,
        grad_query,
        grad_key,
        grad_value,
        grad_out,
        grad_up,
        grad_down,
        media_gain_grad,
        latent_gain_grad,
        ffn_gain_grad,
    ) = layer(
        (
            media[0],
            latents[0],
            cotangent[0],
            media_mask,
            frame_counts,
            media_gain,
            latent_gain,
            ffn_gain,
            w_query,
            w_key,
            w_value,
            w_out,
            w_up,
            w_down,
        ),
        own_rows,
        own_lat,
        features,
    )
    return (
        new_latents[None],
        media_grad[None],
        latent_grad[None],
        grad_query,
        grad_key,
        grad_value,
        grad_out,
        grad_up,
        grad_down,
        media_gain_grad,
        latent_gain_grad,
        ffn_gain_grad,
    )


def solution(mesh):
    return jax.shard_map(
        body,
        mesh=mesh,
        in_specs=(
            P("dp", "seq", None),
            P("dp", "seq", None),
            P("dp"),
            P("dp", None),
            P(),
            P(),
            P(),
            P(),
            P(),
            P(),
            P(),
            P(),
            P(),
            P("dp", "seq", None),
        ),
        out_specs=(
            P("dp", "seq", None),
            P("dp", "seq", None),
            P("dp", "seq", None),
            P(("seq", "dp"), None),
            P(("seq", "dp"), None),
            P(("seq", "dp"), None),
            P(("seq", "dp"), None),
            P(("seq", "dp"), None),
            P(("seq", "dp"), None),
            P(("seq", "dp")),
            P(("seq", "dp")),
            P(("seq", "dp")),
        ),
        check_vma=False,
    )
```

```python
import jax
import jax.numpy as jnp
from jax import lax
from jax.experimental import pallas as pl
from jax.experimental.pallas import tpu as pltpu
from jax.sharding import PartitionSpec as P

HEAD_DIM = 96
PATCH = 256


MASKED_SCORE = -1e30


def normalize(tensor):
    centered = tensor - jnp.mean(tensor, axis=-1, keepdims=True)
    inv = lax.rsqrt(jnp.mean(centered * centered, axis=-1, keepdims=True) + 1e-05)
    return centered * inv, inv


def norm_back(grad, gain_vec, unit, inv):
    scaled = grad * gain_vec
    inner = jnp.mean(scaled * unit, axis=-1, keepdims=True)
    input_grad = inv * (scaled - jnp.mean(scaled, axis=-1, keepdims=True) - unit * inner)
    return input_grad, jnp.sum(grad * unit, axis=0)


def gelu_exact(tensor):
    return jax.nn.gelu(tensor, approximate=False)


def dot(left_op, right_op):
    return jnp.dot(left_op, right_op, preferred_element_type=jnp.float32)


def dot_t(left_op, right_op):
    return lax.dot_general(
        left_op, right_op, (((1,), (1,)), ((), ())), preferred_element_type=jnp.float32
    )


def outer_sum(left_op, right_op):
    return lax.dot_general(
        left_op, right_op, (((0,), (0,)), ((), ())), preferred_element_type=jnp.float32
    )


def split_heads(tensor):
    return tensor.reshape(tensor.shape[0], -1, HEAD_DIM)


def head_products(left_op, right_op):
    return jnp.einsum(
        "qhd,khd->hqk",
        split_heads(left_op),
        split_heads(right_op),
        preferred_element_type=jnp.float32,
    )


def weighted(weights_tab, rows):
    result = jnp.einsum(
        "hqk,khd->qhd", weights_tab, split_heads(rows), preferred_element_type=jnp.float32
    )
    return result.reshape(result.shape[0], -1)


def transposed(weights_tab, rows):
    result = jnp.einsum(
        "hqk,qhd->khd", weights_tab, split_heads(rows), preferred_element_type=jnp.float32
    )
    return result.reshape(result.shape[0], -1)


MESH = pl.DeviceIdType.MESH
GROUP = 4
SPAN = GROUP * HEAD_DIM


def norm_parts(block):
    block = block.astype(jnp.float32)
    centered = block - jnp.mean(block, axis=-1, keepdims=True)
    inv = lax.rsqrt(jnp.mean(centered * centered, axis=-1, keepdims=True) + 1e-05)
    return centered * inv, inv


def input_grad(grad, gain, unit, inv):
    scaled = grad * gain
    inner = jnp.mean(scaled * unit, axis=-1, keepdims=True)
    return inv * (scaled - jnp.mean(scaled, axis=-1, keepdims=True) - unit * inner)


def head_masks(count):
    lane = lax.broadcasted_iota(jnp.int32, (count, SPAN), 1)
    return [(lane >= h * HEAD_DIM) & (lane < (h + 1) * HEAD_DIM) for h in range(GROUP)]


def stacked(tensor, masks):
    return jnp.concatenate(
        [jnp.where(mask, tensor, jnp.zeros_like(tensor)) for mask in masks], axis=0
    )


def copy_to(src, dst, sems, index, device):
    return pltpu.make_async_remote_copy(
        src_ref=src,
        dst_ref=dst,
        send_sem=sems.at[(0,) + index],
        recv_sem=sems.at[(1,) + index],
        device_id=device,
        device_id_type=MESH,
    )


def spans(count):
    return [slice(n * SPAN, (n + 1) * SPAN) for n in range(count)]


def halves(features):
    return [slice(0, features // 2), slice(features // 2, features)]


def settle(copies):
    for copy in copies:
        copy.wait()


def place_transposed(dest, tile, column):
    for piece in range(8):
        row = column + 16 * piece
        block, off = row // 48, row % 48
        bz, by, bx, bc = block // 8, (block // 4) % 2, (block // 2) % 2, block % 2
        at = bx * 384 + by * 192 + (bz % 2) * 96 + (bz // 2) * 48 + off
        dest[bc, at : at + 16, :] = tile[16 * piece : 16 * piece + 16, :]


def layer_kernel(
    media_in,
    latents_in,
    cotangent_in,
    mask_in,
    frames_ref,
    media_gain_ref,
    latent_gain_ref,
    ffn_gain_ref,
    w_query_ref,
    w_key_ref,
    w_value_ref,
    w_out_ref,
    w_up_ref,
    w_down_ref,
    new_latents_out,
    media_grad_out,
    latent_grad_out,
    line_out,
    place_out,
    up_out,
    down_out,
    gains_out,
    media_ref,
    latents_ref,
    cotangent_ref,
    mask_ref,
    gains,
    w_a,
    w_b,
    w_c,
    rows,
    keys,
    values,
    queries,
    stats,
    valid,
    lat_normed,
    lat_all,
    cot_all,
    att_all,
    part_send,
    part_recv,
    stat_send,
    stat_recv,
    attended_f,
    log_total,
    mid_all,
    act_grad,
    act_all,
    pre_all,
    ffn_all,
    fig_f,
    fig_send,
    fig_recv,
    new_f,
    new_send,
    new_recv,
    mid_grad_own,
    rhs_all,
    lhs_send,
    lhs_recv,
    og_all,
    st_all,
    branch_send,
    branch_parts,
    small_out,
    down_part,
    up_part,
    up_recv,
    rows_t,
    lat_lhs,
    lat_got,
    rhs_branch,
    rhs_query,
    place_send,
    place_recv,
    three_recv,
    key_grad,
    value_grad,
    rows_grad,
    query_parts,
    query_send,
    query_recv,
    back_send,
    back_recv,
    pair_send,
    pair_recv,
    own,
    one_recv,
    two_recv,
    line_recv,
    gain_part,
    gain_recv,
    gain_sum,
    gain_all,
    load_sems,
    store_sems,
    line_sems,
    spread_sems,
    block_sems,
    pair_sems,
    one_sems,
    two_sems,
    three_sems,
    last_sems,
):
    bf16, f32 = jnp.bfloat16, jnp.float32
    z = lax.axis_index("seq")
    d = lax.axis_index("dp")
    y, x, c = d // 4, (d // 2) % 2, d % 2
    own_lat = latents_ref.shape[0]
    own_rows, features = media_ref.shape
    groups = features // SPAN
    scale = HEAD_DIM ** (-0.5)
    pair = d + 1 - 2 * c
    x_peer = d + 2 * (1 - 2 * x)
    y_peer = d + 4 * (1 - 2 * y)
    xy_peer = 4 * (1 - y) + 2 * (1 - x) + c
    peers = [(z + k) % 4 for k in (1, 2, 3)]
    others = [(d + k) % 8 for k in range(1, 8)]

    quarter = pl.ds(pl.multiple_of(z * features, 128), features)

    def load(src, dst, number):
        copy = pltpu.make_async_copy(src, dst, load_sems.at[number])
        copy.start()
        return copy

    early = [
        load(media_in, media_ref, 12),
        load(latents_in, latents_ref, 13),
        load(cotangent_in, cotangent_ref, 14),
        load(mask_in, mask_ref, 15),
        load(media_gain_ref, gains.at[0], 0),
        load(latent_gain_ref, gains.at[1], 1),
        load(ffn_gain_ref, gains.at[2], 2),
    ]
    load_a = load(w_key_ref, w_a, 3)
    load_b = load(w_value_ref, w_b, 4)
    load_c = load(w_query_ref, w_c, 5)

    stores = []

    def store(src, dst):
        copy = pltpu.make_async_copy(src, dst, store_sems.at[len(stores)])
        copy.start()
        stores.append(copy)

    barrier = pltpu.get_barrier_semaphore()
    for device in [(p, d) for p in peers] + [(z, p) for p in others]:
        pl.semaphore_signal(barrier, inc=1, device_id=device, device_id_type=MESH)

    lines = []

    def to_line(src_of, dst):
        number = len(lines)
        lines.append(number)
        copies = [
            copy_to(src_of(p), dst, line_sems, (number, k), (p, d)) for k, p in enumerate(peers)
        ]
        for copy in copies:
            copy.start()
        return copies

    settle(early)
    frame = (z * own_rows + lax.broadcasted_iota(jnp.int32, (1, own_rows), 1)) // PATCH
    own_mask = mask_ref[:, pl.ds(pl.multiple_of(z * own_rows, 128), own_rows)]
    kept = jnp.where((own_mask > 0) & (frame < frames_ref[0]), 1.0, 0.0)
    valid[0:own_rows, :] = jnp.broadcast_to(kept, (128, own_rows)).T
    valid[own_rows:, :] = jnp.ones((own_lat, 128), f32)
    keep_row = jnp.concatenate([kept, jnp.ones((1, own_lat), f32)], axis=1) > 0.0

    media_gain, latent_gain, ffn_gain = gains[0:1, :], gains[1:2, :], gains[2:3, :]

    def norm_step(n, carry):
        at = pl.ds(pl.multiple_of(n * 64, 64), 64)
        unit, _ = norm_parts(media_ref[at, :])
        rows[at, :] = (unit * gains[0:1, :]).astype(bf16)
        return carry

    lax.fori_loop(0, own_rows // 64, norm_step, 0)
    pl.semaphore_wait(barrier, 10)
    lat_all[z] = latents_ref[...]
    cot_all[z] = cotangent_ref[...]
    lat_flight = to_line(lambda p: lat_all.at[z], lat_all.at[z])

    unit, _ = norm_parts(latents_ref[...])
    rows[own_rows:, :] = (unit * latent_gain).astype(bf16)

    load_a.wait()
    load_b.wait()

    def project_step(n, carry):
        at = pl.ds(pl.multiple_of(n * 2 * SPAN, 2 * SPAN), 2 * SPAN)
        keys[:, at] = dot(rows[...], w_a[:, at]).astype(bf16)
        values[:, at] = dot(rows[...], w_b[:, at]).astype(bf16)
        return carry

    lax.fori_loop(0, groups // 2, project_step, 0)
    load_b = load(w_down_ref.at[quarter], w_b, 6)
    load_a = load(w_up_ref.at[:, quarter], w_a, 7)

    settle(lat_flight)
    cot_flight = to_line(lambda p: cot_all.at[z], cot_all.at[z])
    unit, _ = norm_parts(lat_all[...].reshape(4 * own_lat, features))
    lat_normed[...] = (unit * latent_gain).astype(bf16)
    load_c.wait()
    for cols in halves(features):
        queries[:, cols] = (dot(lat_normed[...], w_c[:, cols]) * scale).astype(bf16)
    load_c = load(w_out_ref, w_c, 8)

    def to_plane(ref, at, number):
        copies = [
            copy_to(ref.at[at], ref.at[at], spread_sems, (number, k), (z, p))
            for k, p in enumerate((x_peer, y_peer, xy_peer, pair))
        ]
        for copy in copies:
            copy.start()
        return copies

    def to_pair(ref, low, number):
        copies = []
        for k, p in enumerate((x_peer, y_peer, xy_peer)):
            at = pl.ds(pl.multiple_of(p * 128 + low, 64), 64)
            copies.append(copy_to(ref.at[at], ref.at[at], spread_sems, (number, 4 + k), (z, pair)))
        for copy in copies:
            copy.start()
        return copies

    blank = jnp.zeros((64, 128), f32)

    def place_blocks(dest, source, side, spread=True):
        for j in range(features // 128):
            tile = source[:, 128 * j : 128 * j + 128].astype(f32)
            tile = jnp.concatenate([blank, tile] if side else [tile, blank], axis=0)
            tile = tile.T.astype(bf16)
            for piece in range(8):
                row = 128 * j + 16 * piece
                if spread:
                    block, off = row // 48, row % 48
                    owner, at = block % 8, (block // 8) * 48 + off
                else:
                    owner, at = row // 192, row % 192
                part = tile[16 * piece : 16 * piece + 16, :]
                if side:
                    dest[owner, at : at + 16, :] += part
                else:
                    dest[owner, at : at + 16, :] = part

    def spread_blocks(source, dest, number):
        slot = pl.ds(pl.multiple_of(d * 128, 128), 128)
        copies = [
            copy_to(source.at[p], dest.at[:, slot], block_sems, (number, k), (z, p))
            for k, p in enumerate(others)
        ]
        for copy in copies:
            copy.start()
        dest[:, slot] = source[d]
        return copies

    def sides(ref):
        lane = lax.broadcasted_iota(jnp.int32, ref.shape, 1) % 128
        left = ref[...]
        none = jnp.zeros_like(left)
        return jnp.where(lane < 64, left, none), jnp.where(lane >= 64, left, none)

    masks = head_masks(4 * own_lat)
    lane = lax.broadcasted_iota(jnp.int32, (4 * own_lat, 128), 1)
    top_tile = jnp.zeros((4 * own_lat, 128), f32)
    sum_tile = jnp.ones((4 * own_lat, 128), f32)
    part_flight = []
    for g, cols in enumerate(spans(groups)):
        scores = dot_t(stacked(queries[:, cols], masks), keys[:, cols])
        scores = jnp.where(keep_row, scores, MASKED_SCORE)
        largest = jnp.max(scores, axis=-1, keepdims=True)
        expo = jnp.where(keep_row, jnp.exp(scores - largest), 0.0)
        total = jnp.sum(expo, axis=-1, keepdims=True)
        part = dot(expo.astype(bf16), values[:, cols])
        mixed = jnp.zeros((64, SPAN), f32)
        for h in range(GROUP):
            at = slice(64 * h, 64 * h + 64)
            mixed = mixed + jnp.where(masks[h], part[at], 0.0)
            top_tile = jnp.where(lane == GROUP * g + h, largest[at], top_tile)
            sum_tile = jnp.where(lane == GROUP * g + h, total[at], sum_tile)
        part_send[:, :, cols] = mixed.astype(bf16).reshape(4, own_lat, SPAN)
        if g % 2 == 1:
            wide = halves(features)[g // 2]
            part_flight += to_line(
                lambda p: part_send.at[p, :, wide], part_recv.at[z, :, wide]
            )
    stat_send[:, 0] = top_tile.reshape(4, own_lat, 128)
    stat_send[:, 1] = sum_tile.reshape(4, own_lat, 128)
    stat_flight = to_line(lambda p: stat_send.at[p], stat_recv.at[z])
    part_recv[z] = part_send[z]
    stat_recv[z] = stat_send[z]

    settle(cot_flight)
    own_cot = pl.ds(pl.multiple_of(d * 128, 128), 64)
    own_pre = pl.ds(pl.multiple_of(d * 128 + 64, 64), 64)
    rhs_all[own_cot, :] = cot_all[...].reshape(4 * own_lat, features)

    cot_plane = to_plane(rhs_all, own_cot, 0)
    load_b.wait()
    for cols in halves(features):
        act_grad[:, cols] = dot_t(cot_all[...].reshape(64, features), w_b[cols, :])
    for j in range(features // 128):
        place_transposed(
            rows_t, rows[:, 128 * j : 128 * j + 128].astype(f32).T.astype(bf16), 128 * j
        )

    settle(stat_flight)
    tops = stat_recv[:, 0]
    top = jnp.max(tops, axis=0)
    factor = jnp.exp(tops - top[None])
    denominator = jnp.sum(factor * stat_recv[:, 1], axis=0)
    log_total[...] = top + jnp.log(denominator)
    share = factor / denominator[None]
    settle(part_flight)
    own_masks = head_masks(own_lat)
    own_at = pl.ds(pl.multiple_of(z * own_lat, 16), own_lat)
    att_own = att_all.at[own_at]
    att_flight = []
    for g, cols in enumerate(spans(groups)):
        merged = jnp.zeros((own_lat, SPAN), f32)
        for j in range(4):
            spread = jnp.zeros((own_lat, SPAN), f32)
            for h in range(GROUP):
                n = GROUP * g + h
                spread = jnp.where(own_masks[h], share[j, :, n : n + 1], spread)
            merged = merged + spread * part_recv[j, :, cols].astype(f32)
        attended_f[:, cols] = merged
        att_own[:, cols] = merged.astype(bf16)
        if g % 2 == 1:
            wide = halves(features)[g // 2]
            att_flight.append(to_line(lambda p: att_own.at[:, wide], att_own.at[:, wide]))

    settle(cot_plane)
    cot_pair = to_pair(rhs_all, 0, 0)
    place_blocks(lat_lhs, lat_normed, 0)
    for n in range(8):
        rhs_branch[128 * n : 128 * n + 64, :] = jnp.zeros((64, SPAN), bf16)
        rhs_query[128 * n + 64 : 128 * n + 128, :] = jnp.zeros((64, SPAN), bf16)
    load_c.wait()
    load_a.wait()

    mid_all[...] = lat_all[...].reshape(64, features).astype(f32)
    for flight, deep in zip(att_flight, halves(features)):
        settle(flight)
        for cols in halves(features):
            mid_all[:, cols] += dot(att_all[:, deep], w_c[deep, cols])
    place_blocks(lat_lhs, att_all, 1)
    lat_blocks = spread_blocks(lat_lhs, lat_got, 1)
    unit, _ = norm_parts(mid_all[...])
    ffn_all[...] = (unit * ffn_gain).astype(bf16)

    for cols in halves(features):
        pre = dot(ffn_all[...], w_a[:, cols])
        cdf = 0.5 * (1.0 + lax.erf(pre * (0.5**0.5)))
        act_all[:, cols] = (pre * cdf).astype(bf16)
        density = jnp.exp(-0.5 * pre * pre) * (0.5 / jnp.pi) ** 0.5
        pre_all[:, cols] = (act_grad[:, cols] * (cdf + pre * density)).astype(bf16)
    fig_flight = []
    for wide in halves(features):
        part = dot_t(pre_all[...], w_a[wide, :])
        fig_f[:, :, wide] = part.reshape(4, own_lat, 2 * SPAN)
        fig_send[:, :, wide] = part.astype(bf16).reshape(4, own_lat, 2 * SPAN)
        fig_flight += to_line(lambda p: fig_send.at[p, :, wide], fig_recv.at[z, :, wide])
    load_a = load(w_key_ref, w_a, 9)
    rhs_all[own_pre, :] = pre_all[...]
    pre_plane = to_plane(rhs_all, own_pre, 1)
    for cols in halves(features):
        part = dot(act_all[...], w_b[:, cols])
        new_f[:, :, cols] = part.reshape(4, own_lat, 2 * SPAN)
        new_send[:, :, cols] = part.astype(bf16).reshape(4, own_lat, 2 * SPAN)
    flights = {}
    flights["new"] = to_line(lambda p: new_send.at[p], new_recv.at[z])
    load_b = load(w_value_ref, w_b, 10)

    settle(fig_flight)
    fig = fig_f[z]
    for p in peers:
        fig = fig + fig_recv[p].astype(f32)
    mid = mid_all[own_at, :]
    unit, inv = norm_parts(mid)
    gain_part[...] = jnp.zeros_like(gain_part)
    gain_part[2:3, :] = jnp.sum(fig * unit, axis=0, keepdims=True)
    mid_grad = cotangent_ref[...].astype(f32) + input_grad(fig, ffn_gain, unit, inv)
    mid_grad_own[...] = mid_grad
    branch_grad = mid_grad.astype(bf16)
    for n, cols in enumerate(spans(groups)):
        branch_send[n] = branch_grad[:, cols]
    branch_parts[z] = branch_send[z]
    own_lane = lax.broadcasted_iota(jnp.int32, (own_lat, 128), 1)
    delta = jnp.zeros((own_lat, 128), f32)
    grads = [dot_t(branch_grad, w_c[wide, :]).astype(bf16) for wide in halves(features)]
    for g, cols in enumerate(spans(groups)):
        grad = grads[g // 2][:, g % 2 * SPAN : g % 2 * SPAN + SPAN]
        og_all[g, z] = grad
        product = grad.astype(f32) * attended_f[:, cols]
        for h in range(GROUP):
            summed = jnp.sum(jnp.where(own_masks[h], product, 0.0), axis=-1, keepdims=True)
            delta = jnp.where(own_lane == GROUP * g + h, summed, delta)
    st_all[z, 0] = log_total[...]
    st_all[z, 1] = delta
    st_flight = to_line(lambda p: st_all.at[z], st_all.at[z])
    load_c = load(w_query_ref, w_c, 11)

    slots = {ch: ch % 6 for ch in range(2 * groups)}

    def weigh(g):
        cols = spans(groups)[g]
        right = jnp.concatenate([value_grad[:, cols], key_grad[:, cols]], axis=1)
        chunks = (2 * g, 2 * g + 1)
        for half in range(2):
            at = slice(half * 384, (half + 1) * 384)
            part = dot(rows_t[1 - c, at, :], right).astype(bf16)
            for n, ch in enumerate(chunks):
                pair_send[slots[ch], at, :] = part[:, n * SPAN : (n + 1) * SPAN]
        for ch in chunks:
            slot = slots[ch]
            copy = copy_to(pair_send.at[slot], pair_recv.at[slot], pair_sems, (ch,), (z, pair))
            copy.start()
            flights["pair", ch] = copy
        for half in range(2):
            at = slice(half * 384, (half + 1) * 384)
            part = dot(rows_t[c, at, :], right).astype(bf16)
            for n, ch in enumerate(chunks):
                own[ch, half] = part[:, n * SPAN : (n + 1) * SPAN].reshape(2, 192, SPAN)

    def add_to(view, block):
        view[...] = (view[...].astype(f32) + block.astype(f32)).astype(bf16)

    def pair_sum(ch):
        flights["pair", ch].wait()
        for bx in range(2):
            for by in range(2):
                at = bx * 384 + by * 192
                add_to(own.at[ch, bx, by], pair_recv[slots[ch], at : at + 192, :])
        if ch % 2 == 0:
            theirs, device = own.at[ch, 1 - x], x_peer
        else:
            theirs, device = own.at[ch, :, 1 - y], y_peer
        copy = copy_to(theirs, one_recv.at[ch], one_sems, (ch,), (z, device))
        copy.start()
        flights["one", ch] = copy

    def one_sum(ch):
        flights["one", ch].wait()
        for n in range(2):
            add_to(own.at[ch, x, n] if ch % 2 == 0 else own.at[ch, n, y], one_recv[ch, n])
        if ch % 2 == 0:
            theirs, device = own.at[ch, x, 1 - y], y_peer
        else:
            theirs, device = own.at[ch, 1 - x, y], x_peer
        copy = copy_to(theirs, two_recv.at[ch], two_sems, (ch,), (z, device))
        copy.start()
        flights["two", ch] = copy

    odd, high = z % 2, z // 2

    def line_rows(at, count):
        return pl.ds(pl.multiple_of(at, 16), count)

    def two_sum(ch):
        flights["two", ch].wait()
        add_to(own.at[ch, x, y], two_recv[ch])
        copy = copy_to(
            own.at[ch, x, y, line_rows((1 - odd) * 96, 96)],
            three_recv.at[ch],
            three_sems,
            (ch,),
            (z + 1 - 2 * odd, d),
        )
        copy.start()
        flights["three", ch] = copy

    def three_sum(ch):
        flights["three", ch].wait()
        add_to(own.at[ch, x, y, line_rows(odd * 96, 96)], three_recv[ch])
        copy = copy_to(
            own.at[ch, x, y, line_rows(odd * 96 + (1 - high) * 48, 48)],
            line_recv.at[ch, 1],
            last_sems,
            (ch,),
            ((z + 2) % 4, d),
        )
        copy.start()
        flights["line", ch] = copy
        line_recv[ch, 0] = own[ch, x, y, line_rows(odd * 96 + high * 48, 48), :]

    def line_end(ch):
        flights["line", ch].wait()
        store(line_recv.at[ch], line_out.at[ch])

    def rows_leave(g):
        flights["rows", g] = to_line(lambda p: og_all.at[g, z], og_all.at[g, z])

    def branch_leave(_):
        flights["parts"] = to_line(lambda p: branch_send.at[p], branch_parts.at[z])

    def blocks_leave(_):
        place_blocks(lhs_send, act_all, 0, spread=False)
        place_blocks(lhs_send, ffn_all, 1)
        flights["blocks"] = spread_blocks(lhs_send, lhs_recv, 0)

    def spread_stats(_):
        settle(st_flight)
        lane = lax.broadcasted_iota(jnp.int32, (64, 256), 1)
        row = lax.broadcasted_iota(jnp.int32, (64, 256), 0)
        for kind in range(2):
            tile = st_all[:, kind].reshape(64, 128)
            for g in range(groups):
                wide = jnp.zeros((64, 256), f32)
                for h in range(GROUP):
                    n = GROUP * g + h
                    wide = jnp.where(lane == row + 64 * h, tile[:, n : n + 1], wide)
                at = kind * groups + g
                stats[at : at + 1, :] = jnp.sum(wide, axis=0, keepdims=True)

    def attend_back(g):
        cols = spans(groups)[g]
        settle(flights["rows", g])
        q_stack = stacked(queries[:, cols], masks)
        o_stack = stacked(og_all[g].reshape(64, SPAN), masks)
        scores = dot_t(keys[:, cols], q_stack)
        keep = valid[:, 0:1] > 0.0
        exact = jnp.where(keep, jnp.exp(scores - stats[g : g + 1, :]), 0.0)
        prob_grad = dot_t(values[:, cols], o_stack)
        score_grad = (exact * (prob_grad - stats[4 + g : 5 + g, :])).astype(bf16)
        value_grad[:, cols] = dot(exact.astype(bf16), o_stack).astype(bf16)
        key_grad[:, cols] = dot(score_grad, q_stack).astype(bf16)
        q_part = outer_sum(score_grad, keys[:, cols])
        q_sum = jnp.zeros((64, SPAN), f32)
        for h in range(GROUP):
            q_sum = q_sum + jnp.where(masks[h], q_part[64 * h : 64 * h + 64], 0.0)
        query_parts[g] = q_sum
        query_send[g] = q_sum.astype(bf16)

    def forward_pre(_):
        settle(cot_pair)
        settle(pre_plane)
        settle(lat_blocks)
        flights["pre"] = to_pair(rhs_all, 64, 1)

    def new_rows(_):
        settle(flights["new"])
        new = mid_all[own_at, :] + new_f[z]
        for p in peers:
            new = new + new_recv[p].astype(f32)
        small_out[0] = new.astype(bf16)
        store(small_out.at[0], new_latents_out)

    def query_leave(_):
        flights["query"] = to_line(lambda p: query_send.at[p], query_recv.at[z])

    own_top = pl.ds(pl.multiple_of(d * 128, 128), 64)
    own_low = pl.ds(pl.multiple_of(d * 128 + 64, 64), 64)

    def branch_spread(_):
        settle(flights["parts"])
        rhs_branch[own_low, :] = branch_parts[...].reshape(64, SPAN)
        flights["branch"] = to_plane(rhs_branch, own_low, 3)

    def branch_pair(_):
        settle(flights["branch"])
        flights["branch"] = to_pair(rhs_branch, 64, 3)

    def place(n, part):
        place_send[n] = part.astype(bf16).reshape(4, 48, SPAN)
        flights["place", n] = to_line(lambda p: place_send.at[n, p], place_recv.at[n, z])
        place_recv[n, z] = place_send[n, z]

    def place_end(n):
        settle(flights["place", n])
        store(place_recv.at[n], place_out.at[n])

    def branch_weigh(_):
        settle(flights["branch"])
        place(0, dot(lat_got[...], rhs_branch[...]))

    def query_spread(_):
        settle(flights["query"])
        total = query_parts[z]
        for p in peers:
            total = total + query_recv[p].astype(f32)
        total = total.astype(bf16)
        back_send[...] = total.reshape(4, own_lat, SPAN)
        back_recv[z] = back_send[z]
        flights["back"] = to_line(lambda p: back_send.at[p], back_recv.at[z])
        rhs_query[own_top, :] = total
        flights["rows"] = to_plane(rhs_query, own_top, 4)

    def query_pair(_):
        settle(flights["rows"])
        flights["rows"] = to_pair(rhs_query, 0, 4)

    def query_weigh(_):
        settle(flights["rows"])
        place(1, scale * dot(lat_got[...], rhs_query[...]))

    def up_down(_):
        settle(flights["blocks"])
        settle(flights["pre"])
        act_left, ffn_left = sides(lhs_recv)
        for cols in halves(features):
            part = dot(ffn_left, rhs_all[:, cols])
            up_part[:, :, cols] = part.astype(bf16).reshape(4, 48, 2 * SPAN)
        flights["up"] = to_line(lambda p: up_part.at[p], up_recv.at[z])
        up_recv[z] = up_part[z]
        for cols in halves(features):
            down_part[:, cols] = dot(act_left, rhs_all[:, cols])
        store(down_part, down_out)

    def back_step(n, carry):
        at = pl.ds(pl.multiple_of(n * 2 * SPAN, 2 * SPAN), 2 * SPAN)
        rows_grad[:, at] = dot_t(key_grad[...], w_a[at, :]) + dot_t(value_grad[...], w_b[at, :])
        return carry

    def back_half(n):
        if n == 0:
            load_a.wait()
            load_b.wait()
        lax.fori_loop(n, n + 1, back_step, 0)

    def back_norm_step(n, total):
        at = pl.ds(pl.multiple_of(n * 64, 64), 64)
        unit, inv = norm_parts(media_ref[at, :])
        grad = rows_grad[at, :]
        rows[at, :] = input_grad(grad, gains[0:1, :], unit, inv).astype(bf16)
        return total + jnp.sum(grad * unit, axis=0, keepdims=True)

    def back_norm(_):
        gain_part[0:1, :] = lax.fori_loop(
            0, own_rows // 64, back_norm_step, jnp.zeros((1, features), f32)
        )
        store(rows.at[pl.ds(0, own_rows)], media_grad_out)

    def latent_rows(_):
        settle(flights["back"])
        load_c.wait()
        lat_grad = rows_grad[own_rows:, :]
        for n, cols in enumerate(spans(groups)):
            lat_grad = lat_grad + scale * dot_t(back_recv[n], w_c[:, cols])
        unit, inv = norm_parts(latents_ref[...])
        grad = input_grad(lat_grad, latent_gain, unit, inv)
        small_out[1] = (mid_grad_own[...] + grad).astype(bf16)
        store(small_out.at[1], latent_grad_out)
        gain_part[1:2, :] = jnp.sum(lat_grad * unit, axis=0, keepdims=True)
        for n, cols in enumerate(spans(groups)):
            gain_sum[n] = gain_part[:, cols]
        flights["gain"] = to_line(lambda p: gain_sum.at[p], gain_recv.at[z])

    def up_end(_):
        settle(flights["up"])
        store(up_recv, up_out)

    def gain_middle(_):
        settle(flights["gain"])
        total = gain_sum[z]
        for p in peers:
            total = total + gain_recv[p]
        gain_all[d] = total
        flights["spread"] = [
            copy_to(gain_all.at[d], gain_all.at[d], spread_sems, (2, k), (z, p))
            for k, p in enumerate(others)
        ]
        for item in flights["spread"]:
            item.start()

    def gain_end(_):
        settle(flights["spread"])
        gain_part[:, 0:SPAN] = jnp.sum(gain_all[...], axis=0)
        store(gain_part, gains_out)

    blocks_leave(0)
    rows_leave(0)
    spread_stats(0)
    rows_leave(1)
    rows_leave(3)
    branch_leave(0)
    attend_back(0)
    weigh(0)
    branch_spread(0)
    attend_back(3)
    rows_leave(2)
    attend_back(1)
    pair_sum(1)
    pair_sum(0)
    weigh(1)
    attend_back(2)
    query_leave(0)
    pair_sum(3)
    forward_pre(0)
    pair_sum(2)
    weigh(2)
    weigh(3)
    query_spread(0)
    one_sum(0)
    up_down(0)
    pair_sum(5)
    pair_sum(4)
    back_half(0)
    one_sum(1)
    query_pair(0)
    back_half(1)
    one_sum(3)
    branch_pair(0)
    one_sum(2)
    two_sum(0)
    query_weigh(0)
    two_sum(1)
    pair_sum(7)
    one_sum(5)
    branch_weigh(0)
    three_sum(0)
    two_sum(3)
    pair_sum(6)
    back_norm(0)
    three_sum(1)
    two_sum(2)
    new_rows(0)
    one_sum(4)
    line_end(0)
    latent_rows(0)
    two_sum(5)
    one_sum(7)
    one_sum(6)
    three_sum(3)
    three_sum(2)
    two_sum(4)
    three_sum(5)
    two_sum(7)
    gain_middle(0)
    two_sum(6)
    line_end(2)
    up_end(0)
    line_end(3)
    three_sum(4)
    three_sum(7)
    line_end(1)
    three_sum(6)
    gain_end(0)
    line_end(5)
    place_end(0)
    place_end(1)
    line_end(4)
    line_end(7)
    line_end(6)
    settle(stores)


def finish_kernel(
    new_in,
    media_in,
    latent_in,
    line_in,
    place_in,
    up_in,
    down_in,
    gains_in,
    new_out,
    media_out,
    latent_out,
    query_out,
    key_out,
    value_out,
    out_out,
    up_out,
    down_out,
    media_gain_out,
    latent_gain_out,
    ffn_gain_out,
    new_room,
    media_room,
    latent_room,
    down_room,
    line_room,
    place_room,
    up_room,
    gains_room,
    squares,
    up_wide,
    in_sems,
    out_sems,
):
    f32 = jnp.float32
    rooms = [line_room, media_room, down_room, up_room, new_room, latent_room, gains_room]
    sources = [line_in, media_in, down_in, up_in, new_in, latent_in, gains_in]
    rooms.append(place_room)
    sources.append(place_in)
    arrivals = [
        pltpu.make_async_copy(src, dst, in_sems.at[n])
        for n, (src, dst) in enumerate(zip(sources, rooms))
    ]
    for copy in arrivals[:1] + arrivals[7:] + arrivals[1:7]:
        copy.start()
    leaving = []

    def leave(src, dst):
        copy = pltpu.make_async_copy(src, dst, out_sems.at[len(leaving)])
        copy.start()
        leaving.append(copy)

    arrivals[0].wait()
    arrivals[7].wait()
    for n, cols in enumerate(spans(4)):
        squares[0, :, cols] = place_room[1, n].astype(f32)
        squares[1, :, cols] = jnp.sum(line_room[2 * n + 1].astype(f32), axis=0)
        squares[2, :, cols] = jnp.sum(line_room[2 * n].astype(f32), axis=0)
        squares[3, :, cols] = place_room[0, n].astype(f32)
    for n, dst in enumerate((query_out, key_out, value_out, out_out)):
        leave(squares.at[n], dst)
    arrivals[1].wait()
    leave(media_room, media_out)
    arrivals[2].wait()
    leave(down_room, down_out)
    arrivals[3].wait()
    features = up_in.shape[2]
    for n in range(4):
        up_wide[:, n * features : (n + 1) * features] = up_room[n].astype(f32)
    leave(up_wide, up_out)
    arrivals[4].wait()
    leave(new_room, new_out)
    arrivals[5].wait()
    leave(latent_room, latent_out)
    arrivals[6].wait()
    share = query_out.shape[0]
    start = lax.axis_index("dp") * share
    base = pl.multiple_of((start // 128) * 128, 128)
    window = gains_room[:, pl.ds(base, 256)]
    window = pltpu.roll(window, (256 - start % 128) % 256, 1)
    media_gain_out[...] = window[0, :share]
    latent_gain_out[...] = window[1, :share]
    ffn_gain_out[...] = window[2, :share]
    settle(leaving)


def layer(operands, own_rows, own_lat, features):
    bf16, f32 = jnp.bfloat16, jnp.float32
    count = own_rows + own_lat
    lat_rows = 4 * own_lat
    share = features // 32
    vmem = pl.BlockSpec(memory_space=pltpu.VMEM)
    smem = pl.BlockSpec(memory_space=pltpu.SMEM)
    anyway = pl.BlockSpec(memory_space=pl.ANY)

    def array(kind, *shape):
        return jax.ShapeDtypeStruct(shape, kind)

    def room(kind, *shape):
        return pltpu.VMEM(shape, kind)

    def dma(*shape):
        return pltpu.SemaphoreType.DMA(shape)

    outs = (
        array(bf16, own_lat, features),
        array(bf16, own_rows, features),
        array(bf16, own_lat, features),
        array(bf16, 8, 2, share, SPAN),
        array(bf16, 2, 4, share, SPAN),
        array(bf16, 4, share, features),
        array(f32, 4 * share, features),
        array(f32, 8, features),
    )
    scratch = dict(
        media_ref=room(bf16, own_rows, features),
        latents_ref=room(bf16, own_lat, features),
        cotangent_ref=room(bf16, own_lat, features),
        mask_ref=room(jnp.int32, 1, 4 * own_rows),
        gains=room(f32, 8, features),
        w_a=room(bf16, features, features),
        w_b=room(bf16, features, features),
        w_c=room(bf16, features, features),
        rows=room(bf16, count, features),
        keys=room(bf16, count, features),
        values=room(bf16, count, features),
        queries=room(bf16, lat_rows, features),
        stats=room(f32, 8, 256),
        valid=room(f32, count, 128),
        lat_normed=room(bf16, lat_rows, features),
        lat_all=room(bf16, 4, own_lat, features),
        cot_all=room(bf16, 4, own_lat, features),
        att_all=room(bf16, lat_rows, features),
        part_send=room(bf16, 4, own_lat, features),
        part_recv=room(bf16, 4, own_lat, features),
        stat_send=room(f32, 4, 2, own_lat, 128),
        stat_recv=room(f32, 4, 2, own_lat, 128),
        attended_f=room(f32, own_lat, features),
        log_total=room(f32, own_lat, 128),
        mid_all=room(f32, lat_rows, features),
        act_grad=room(f32, lat_rows, features),
        act_all=room(bf16, lat_rows, features),
        pre_all=room(bf16, lat_rows, features),
        ffn_all=room(bf16, lat_rows, features),
        fig_f=room(f32, 4, own_lat, features),
        fig_send=room(bf16, 4, own_lat, features),
        fig_recv=room(bf16, 4, own_lat, features),
        new_f=room(f32, 4, own_lat, features),
        new_send=room(bf16, 4, own_lat, features),
        new_recv=room(bf16, 4, own_lat, features),
        mid_grad_own=room(f32, own_lat, features),
        rhs_all=room(bf16, 1024, features),
        lhs_send=room(bf16, 8, 4 * share, 128),
        lhs_recv=room(bf16, 4 * share, 1024),
        og_all=room(bf16, 4, 4, own_lat, SPAN),
        st_all=room(f32, 4, 2, own_lat, 128),
        branch_send=room(bf16, 4, own_lat, SPAN),
        branch_parts=room(bf16, 4, own_lat, SPAN),
        small_out=room(bf16, 2, own_lat, features),
        down_part=room(f32, 4 * share, features),
        up_part=room(bf16, 4, share, features),
        up_recv=room(bf16, 4, share, features),
        rows_t=room(bf16, 2, features // 2, count),
        lat_lhs=room(bf16, 8, 4 * share, 128),
        lat_got=room(bf16, 4 * share, 1024),
        rhs_branch=room(bf16, 1024, SPAN),
        rhs_query=room(bf16, 1024, SPAN),
        place_send=room(bf16, 2, 4, share, SPAN),
        place_recv=room(bf16, 2, 4, share, SPAN),
        three_recv=room(bf16, 8, 96, SPAN),
        key_grad=room(bf16, count, features),
        value_grad=room(bf16, count, features),
        rows_grad=room(f32, count, features),
        query_parts=room(f32, 4, lat_rows, SPAN),
        query_send=room(bf16, 4, lat_rows, SPAN),
        query_recv=room(bf16, 4, lat_rows, SPAN),
        back_send=room(bf16, 4, own_lat, SPAN),
        back_recv=room(bf16, 4, own_lat, SPAN),
        pair_send=room(bf16, 6, 768, SPAN),
        pair_recv=room(bf16, 6, 768, SPAN),
        own=room(bf16, 8, 2, 2, 192, SPAN),
        one_recv=room(bf16, 8, 2, 192, SPAN),
        two_recv=room(bf16, 8, 192, SPAN),
        line_recv=room(bf16, 8, 2, share, SPAN),
        gain_part=room(f32, 8, features),
        gain_recv=room(f32, 4, 8, SPAN),
        gain_sum=room(f32, 4, 8, SPAN),
        gain_all=room(f32, 8, 8, SPAN),
        load_sems=dma(16),
        store_sems=dma(16),
        line_sems=dma(2, 24, 3),
        spread_sems=dma(2, 5, 7),
        block_sems=dma(2, 2, 7),
        pair_sems=dma(2, 8),
        one_sems=dma(2, 8),
        two_sems=dma(2, 8),
        three_sems=dma(2, 8),
        last_sems=dma(2, 8),
    )
    staged = pl.pallas_call(
        layer_kernel,
        out_shape=outs,
        in_specs=[anyway] * 4 + [smem] + [anyway] * 9,
        out_specs=(anyway,) * len(outs),
        scratch_shapes=tuple(scratch.values()),
        compiler_params=pltpu.CompilerParams(
            collective_id=0, has_side_effects=True, vmem_limit_bytes=63 * 1024 * 1024
        ),
    )(*operands)
    square = array(f32, share, features)
    return pl.pallas_call(
        finish_kernel,
        out_shape=outs[:3]
        + (square,) * 4
        + (array(f32, share, 4 * features), outs[6])
        + (array(f32, share),) * 3,
        in_specs=[anyway] * 8,
        out_specs=(anyway,) * 9 + (vmem,) * 3,
        scratch_shapes=[
            room(bf16, own_lat, features),
            room(bf16, own_rows, features),
            room(bf16, own_lat, features),
            room(f32, 4 * share, features),
            room(bf16, 8, 2, share, SPAN),
            room(bf16, 2, 4, share, SPAN),
            room(bf16, 4, share, features),
            room(f32, 8, features),
            room(f32, 4, share, features),
            room(f32, share, 4 * features),
            dma(8),
            dma(9),
        ],
        compiler_params=pltpu.CompilerParams(vmem_limit_bytes=63 * 1024 * 1024),
    )(*staged)


def spread_body(
    media,
    latents,
    frame_counts,
    media_mask,
    media_gain,
    latent_gain,
    ffn_gain,
    w_query,
    w_key,
    w_value,
    w_out,
    w_up,
    w_down,
    cotangent,
):
    _, own_rows, features = media.shape
    own_lat = latents.shape[1]
    seq_parts = lax.axis_size("seq")
    seq_index = lax.axis_index("seq")
    device_count = seq_parts * lax.axis_size("dp")
    both = ("seq", "dp")
    heads = features // HEAD_DIM
    score_scale = HEAD_DIM ** (-0.5)
    bf16 = jnp.bfloat16

    media, latents, cotangent = media[0], latents[0], cotangent[0]
    own_mask = lax.dynamic_slice_in_dim(media_mask[0], seq_index * own_rows, own_rows, 0)
    row_frame = (seq_index * own_rows + jnp.arange(own_rows, dtype=jnp.int32)) // PATCH
    own_valid = (own_mask > 0) & (row_frame < frame_counts[0])
    valid = jnp.concatenate([own_valid, jnp.ones((own_lat,), jnp.bool_)])[None, None, :]

    all_cotangent = lax.all_gather(cotangent, both, axis=0, tiled=True)

    latents_f = latents.astype(jnp.float32)
    latent_unit, latent_inv = normalize(latents_f)
    latent_normed = (latent_unit * latent_gain).astype(bf16)
    own_queries = (dot(latent_normed, w_query) * score_scale).astype(bf16)
    queries = lax.all_gather(own_queries, "seq", axis=0, tiled=True)

    media_unit, media_inv = normalize(media.astype(jnp.float32))
    media_normed = (media_unit * media_gain).astype(bf16)
    rows = jnp.concatenate([media_normed, latent_normed], axis=0)
    keys = dot(rows, w_key).astype(bf16)
    values = dot(rows, w_value).astype(bf16)

    scores = jnp.where(valid, head_products(queries, keys), MASKED_SCORE)
    largest = jnp.max(scores, axis=-1)
    expo = jnp.where(valid, jnp.exp(scores - largest[..., None]), 0.0)
    total = jnp.sum(expo, axis=-1)
    part = weighted(expo.astype(bf16), values)
    packed = jnp.concatenate([part, largest.T, total.T], axis=1)
    packed = lax.all_to_all(packed, "seq", split_axis=0, concat_axis=0, tiled=True)
    packed = packed.reshape(seq_parts, own_lat, -1)
    parts = packed[..., :features]
    maxima = packed[..., features : features + heads]
    totals = packed[..., features + heads :]
    top = jnp.max(maxima, axis=0)
    factor = jnp.exp(maxima - top)
    denominator = jnp.sum(factor * totals, axis=0)
    log_total = top + jnp.log(denominator)
    share = jnp.repeat(factor / denominator, HEAD_DIM, axis=-1)
    attended_f = jnp.sum(parts * share, axis=0)
    attended = attended_f.astype(bf16)

    mid = latents_f + dot(attended, w_out)
    mid_unit, mid_inv = normalize(mid)
    ffn_in = (mid_unit * ffn_gain).astype(bf16)
    pre = dot(ffn_in, w_up)
    act = gelu_exact(pre).astype(bf16)
    new_latents = (mid + dot(act, w_down)).astype(bf16)
    act_grad = dot_t(cotangent, w_down)
    pre_grad = jax.vjp(gelu_exact, pre)[1](act_grad)[0].astype(bf16)
    all_pre_grad = lax.all_gather(pre_grad, both, axis=0, tiled=True)
    ffn_in_grad = dot_t(pre_grad, w_up)
    mid_back, grad_ffn_gain = norm_back(ffn_in_grad, ffn_gain, mid_unit, mid_inv)
    mid_grad = cotangent.astype(jnp.float32) + mid_back
    branch_grad = mid_grad.astype(bf16)
    all_branch = lax.all_gather(branch_grad, both, axis=0, tiled=True)
    attended_grad = dot_t(branch_grad, w_out).astype(bf16)
    own_delta = jnp.sum(
        split_heads(attended_f * attended_grad.astype(jnp.float32)), axis=-1
    )
    out_grad = lax.all_gather(attended_grad, "seq", axis=0, tiled=True)
    stats = lax.all_gather(
        jnp.concatenate([log_total, own_delta], axis=1), "seq", axis=0, tiled=True
    )
    lse = stats[:, :heads].T[..., None]
    delta = stats[:, heads:].T[..., None]

    exact = jnp.where(valid, jnp.exp(scores - lse), 0.0)
    score_grad = (exact * (head_products(out_grad, values) - delta)).astype(bf16)
    value_grad = transposed(exact.astype(bf16), out_grad).astype(bf16)
    key_grad = transposed(score_grad, queries).astype(bf16)
    query_part = weighted(score_grad, keys)
    query_grad = lax.psum_scatter(
        query_part, "seq", scatter_dimension=0, tiled=True
    ).astype(bf16)
    all_query_grad = lax.all_gather(query_grad, both, axis=0, tiled=True)
    part_value = outer_sum(rows, value_grad).astype(bf16)
    part_key = outer_sum(rows, key_grad).astype(bf16)
    sum_value = lax.psum_scatter(part_value, both, scatter_dimension=0, tiled=True)
    sum_key = lax.psum_scatter(part_key, both, scatter_dimension=0, tiled=True)

    rows_grad = dot_t(key_grad, w_key) + dot_t(value_grad, w_value)
    media_back, grad_media_gain = norm_back(
        rows_grad[:own_rows], media_gain, media_unit, media_inv
    )
    media_grad = media_back.astype(bf16)
    latent_normed_grad = rows_grad[own_rows:] + dot_t(query_grad, w_query) * score_scale
    latent_back, grad_latent_gain = norm_back(
        latent_normed_grad, latent_gain, latent_unit, latent_inv
    )
    latent_grad = (mid_grad + latent_back).astype(bf16)

    def by_owner(tensor):
        return tensor.reshape(tensor.shape[0], device_count, -1)

    sent = jnp.concatenate(
        [by_owner(latent_normed), by_owner(attended), by_owner(ffn_in), by_owner(act)], axis=2
    )
    got = lax.all_to_all(sent, both, split_axis=1, concat_axis=0, tiled=True)
    got = got.reshape(-1, got.shape[-1])
    block = features // device_count
    grad_query = outer_sum(got[:, :block], all_query_grad) * score_scale
    grad_out = outer_sum(got[:, block : 2 * block], all_branch)
    grad_up = outer_sum(got[:, 2 * block : 3 * block], all_pre_grad)
    grad_down = outer_sum(got[:, 3 * block :], all_cotangent)

    gains = jnp.stack([grad_media_gain, grad_latent_gain, grad_ffn_gain])
    gains = by_owner(gains).transpose(1, 0, 2).reshape(device_count, -1)
    gains = lax.all_to_all(gains, both, split_axis=0, concat_axis=0, tiled=True)
    gains = jnp.sum(gains.reshape(device_count, 3, -1), axis=0)
    return (
        new_latents[None],
        media_grad[None],
        latent_grad[None],
        grad_query,
        sum_key.astype(jnp.float32),
        sum_value.astype(jnp.float32),
        grad_out,
        grad_up,
        grad_down,
        gains[0],
        gains[1],
        gains[2],
    )


def body(
    media,
    latents,
    frame_counts,
    media_mask,
    media_gain,
    latent_gain,
    ffn_gain,
    w_query,
    w_key,
    w_value,
    w_out,
    w_up,
    w_down,
    cotangent,
):
    _, own_rows, features = media.shape
    own_lat = latents.shape[1]
    seq_parts, dp_parts = lax.axis_size("seq"), lax.axis_size("dp")
    if (seq_parts, dp_parts, own_lat, features) != (4, 8, 16, 4 * SPAN):
        return spread_body(
            media,
            latents,
            frame_counts,
            media_mask,
            media_gain,
            latent_gain,
            ffn_gain,
            w_query,
            w_key,
            w_value,
            w_out,
            w_up,
            w_down,
            cotangent,
        )
    (
        new_latents,
        media_grad,
        latent_grad,
        grad_query,
        grad_key,
        grad_value,
        grad_out,
        grad_up,
        grad_down,
        media_gain_grad,
        latent_gain_grad,
        ffn_gain_grad,
    ) = layer(
        (
            media[0],
            latents[0],
            cotangent[0],
            media_mask,
            frame_counts,
            media_gain,
            latent_gain,
            ffn_gain,
            w_query,
            w_key,
            w_value,
            w_out,
            w_up,
            w_down,
        ),
        own_rows,
        own_lat,
        features,
    )
    return (
        new_latents[None],
        media_grad[None],
        latent_grad[None],
        grad_query,
        grad_key,
        grad_value,
        grad_out,
        grad_up,
        grad_down,
        media_gain_grad,
        latent_gain_grad,
        ffn_gain_grad,
    )


def solution(mesh):
    return jax.shard_map(
        body,
        mesh=mesh,
        in_specs=(
            P("dp", "seq", None),
            P("dp", "seq", None),
            P("dp"),
            P("dp", None),
            P(),
            P(),
            P(),
            P(),
            P(),
            P(),
            P(),
            P(),
            P(),
            P("dp", "seq", None),
        ),
        out_specs=(
            P("dp", "seq", None),
            P("dp", "seq", None),
            P("dp", "seq", None),
            P(("seq", "dp"), None),
            P(("seq", "dp"), None),
            P(("seq", "dp"), None),
            P(("seq", "dp"), None),
            P(("seq", "dp"), None),
            P(("seq", "dp"), None),
            P(("seq", "dp")),
            P(("seq", "dp")),
            P(("seq", "dp")),
        ),
        check_vma=False,
    )
```

```python
import jax
import jax.numpy as jnp
from jax import lax
from jax.experimental import pallas as pl
from jax.experimental.pallas import tpu as pltpu
from jax.sharding import PartitionSpec as P

HEAD_DIM = 96
PATCH = 256


MASKED_SCORE = -1e30


def normalize(tensor):
    centered = tensor - jnp.mean(tensor, axis=-1, keepdims=True)
    inv = lax.rsqrt(jnp.mean(centered * centered, axis=-1, keepdims=True) + 1e-05)
    return centered * inv, inv


def norm_back(grad, gain_vec, unit, inv):
    scaled = grad * gain_vec
    inner = jnp.mean(scaled * unit, axis=-1, keepdims=True)
    input_grad = inv * (scaled - jnp.mean(scaled, axis=-1, keepdims=True) - unit * inner)
    return input_grad, jnp.sum(grad * unit, axis=0)


def gelu_exact(tensor):
    return jax.nn.gelu(tensor, approximate=False)


def dot(left_op, right_op):
    return jnp.dot(left_op, right_op, preferred_element_type=jnp.float32)


def dot_t(left_op, right_op):
    return lax.dot_general(
        left_op, right_op, (((1,), (1,)), ((), ())), preferred_element_type=jnp.float32
    )


def outer_sum(left_op, right_op):
    return lax.dot_general(
        left_op, right_op, (((0,), (0,)), ((), ())), preferred_element_type=jnp.float32
    )


def split_heads(tensor):
    return tensor.reshape(tensor.shape[0], -1, HEAD_DIM)


def head_products(left_op, right_op):
    return jnp.einsum(
        "qhd,khd->hqk",
        split_heads(left_op),
        split_heads(right_op),
        preferred_element_type=jnp.float32,
    )


def weighted(weights_tab, rows):
    result = jnp.einsum(
        "hqk,khd->qhd", weights_tab, split_heads(rows), preferred_element_type=jnp.float32
    )
    return result.reshape(result.shape[0], -1)


def transposed(weights_tab, rows):
    result = jnp.einsum(
        "hqk,qhd->khd", weights_tab, split_heads(rows), preferred_element_type=jnp.float32
    )
    return result.reshape(result.shape[0], -1)


MESH = pl.DeviceIdType.MESH
GROUP = 4
SPAN = GROUP * HEAD_DIM


def norm_parts(block):
    block = block.astype(jnp.float32)
    centered = block - jnp.mean(block, axis=-1, keepdims=True)
    inv = lax.rsqrt(jnp.mean(centered * centered, axis=-1, keepdims=True) + 1e-05)
    return centered * inv, inv


def input_grad(grad, gain, unit, inv):
    scaled = grad * gain
    inner = jnp.mean(scaled * unit, axis=-1, keepdims=True)
    return inv * (scaled - jnp.mean(scaled, axis=-1, keepdims=True) - unit * inner)


def head_masks(count):
    lane = lax.broadcasted_iota(jnp.int32, (count, SPAN), 1)
    return [(lane >= h * HEAD_DIM) & (lane < (h + 1) * HEAD_DIM) for h in range(GROUP)]


def stacked(tensor, masks):
    return jnp.concatenate(
        [jnp.where(mask, tensor, jnp.zeros_like(tensor)) for mask in masks], axis=0
    )


def copy_to(src, dst, sems, index, device):
    return pltpu.make_async_remote_copy(
        src_ref=src,
        dst_ref=dst,
        send_sem=sems.at[(0,) + index],
        recv_sem=sems.at[(1,) + index],
        device_id=device,
        device_id_type=MESH,
    )


def spans(count):
    return [slice(n * SPAN, (n + 1) * SPAN) for n in range(count)]


def halves(features):
    return [slice(0, features // 2), slice(features // 2, features)]


def settle(copies):
    for copy in copies:
        copy.wait()


def place_transposed(dest, tile, column):
    for piece in range(8):
        row = column + 16 * piece
        block, off = row // 48, row % 48
        bz, by, bx, bc = block // 8, (block // 4) % 2, (block // 2) % 2, block % 2
        at = bx * 384 + by * 192 + (bz % 2) * 96 + (bz // 2) * 48 + off
        dest[bc, at : at + 16, :] = tile[16 * piece : 16 * piece + 16, :]


def layer_kernel(
    media_in,
    latents_in,
    cotangent_in,
    mask_in,
    frames_ref,
    media_gain_ref,
    latent_gain_ref,
    ffn_gain_ref,
    w_query_ref,
    w_key_ref,
    w_value_ref,
    w_out_ref,
    w_up_ref,
    w_down_ref,
    new_latents_out,
    media_grad_out,
    latent_grad_out,
    line_out,
    place_out,
    up_out,
    down_out,
    gains_out,
    media_ref,
    latents_ref,
    cotangent_ref,
    mask_ref,
    gains,
    w_a,
    w_b,
    w_c,
    rows,
    keys,
    values,
    queries,
    stats,
    valid,
    lat_normed,
    lat_all,
    cot_all,
    att_all,
    part_send,
    part_recv,
    stat_send,
    stat_recv,
    attended_f,
    log_total,
    mid_all,
    act_grad,
    act_all,
    pre_all,
    ffn_all,
    fig_f,
    fig_send,
    fig_recv,
    new_f,
    new_send,
    new_recv,
    mid_grad_own,
    rhs_all,
    lhs_send,
    lhs_recv,
    og_all,
    st_all,
    branch_send,
    branch_parts,
    small_out,
    down_part,
    up_part,
    up_recv,
    rows_t,
    lat_lhs,
    lat_got,
    rhs_branch,
    rhs_query,
    place_send,
    place_recv,
    three_recv,
    key_grad,
    value_grad,
    rows_grad,
    query_parts,
    query_send,
    query_recv,
    back_send,
    back_recv,
    pair_send,
    pair_recv,
    own,
    one_recv,
    two_recv,
    line_recv,
    gain_part,
    gain_recv,
    gain_sum,
    gain_all,
    load_sems,
    store_sems,
    line_sems,
    spread_sems,
    block_sems,
    pair_sems,
    one_sems,
    two_sems,
    three_sems,
    last_sems,
):
    bf16, f32 = jnp.bfloat16, jnp.float32
    z = lax.axis_index("seq")
    d = lax.axis_index("dp")
    y, x, c = d // 4, (d // 2) % 2, d % 2
    own_lat = latents_ref.shape[0]
    own_rows, features = media_ref.shape
    groups = features // SPAN
    scale = HEAD_DIM ** (-0.5)
    pair = d + 1 - 2 * c
    x_peer = d + 2 * (1 - 2 * x)
    y_peer = d + 4 * (1 - 2 * y)
    xy_peer = 4 * (1 - y) + 2 * (1 - x) + c
    peers = [(z + k) % 4 for k in (1, 2, 3)]
    others = [(d + k) % 8 for k in range(1, 8)]

    quarter = pl.ds(pl.multiple_of(z * features, 128), features)

    def load(src, dst, number):
        copy = pltpu.make_async_copy(src, dst, load_sems.at[number])
        copy.start()
        return copy

    early = [
        load(media_in, media_ref, 12),
        load(latents_in, latents_ref, 13),
        load(cotangent_in, cotangent_ref, 14),
        load(mask_in, mask_ref, 15),
        load(media_gain_ref, gains.at[0], 0),
        load(latent_gain_ref, gains.at[1], 1),
        load(ffn_gain_ref, gains.at[2], 2),
    ]
    load_a = load(w_key_ref, w_a, 3)
    load_b = load(w_value_ref, w_b, 4)
    load_c = load(w_query_ref, w_c, 5)

    stores = []

    def store(src, dst):
        copy = pltpu.make_async_copy(src, dst, store_sems.at[len(stores)])
        copy.start()
        stores.append(copy)

    barrier = pltpu.get_barrier_semaphore()
    for device in [(p, d) for p in peers] + [(z, p) for p in others]:
        pl.semaphore_signal(barrier, inc=1, device_id=device, device_id_type=MESH)

    lines = []

    def to_line(src_of, dst):
        number = len(lines)
        lines.append(number)
        copies = [
            copy_to(src_of(p), dst, line_sems, (number, k), (p, d)) for k, p in enumerate(peers)
        ]
        for copy in copies:
            copy.start()
        return copies

    settle(early)
    frame = (z * own_rows + lax.broadcasted_iota(jnp.int32, (1, own_rows), 1)) // PATCH
    own_mask = mask_ref[:, pl.ds(pl.multiple_of(z * own_rows, 128), own_rows)]
    kept = jnp.where((own_mask > 0) & (frame < frames_ref[0]), 1.0, 0.0)
    valid[0:own_rows, :] = jnp.broadcast_to(kept, (128, own_rows)).T
    valid[own_rows:, :] = jnp.ones((own_lat, 128), f32)
    keep_row = jnp.concatenate([kept, jnp.ones((1, own_lat), f32)], axis=1) > 0.0

    media_gain, latent_gain, ffn_gain = gains[0:1, :], gains[1:2, :], gains[2:3, :]

    def norm_step(n, carry):
        at = pl.ds(pl.multiple_of(n * 64, 64), 64)
        unit, _ = norm_parts(media_ref[at, :])
        rows[at, :] = (unit * gains[0:1, :]).astype(bf16)
        return carry

    lax.fori_loop(0, own_rows // 64, norm_step, 0)
    pl.semaphore_wait(barrier, 10)
    lat_all[z] = latents_ref[...]
    cot_all[z] = cotangent_ref[...]
    lat_flight = to_line(lambda p: lat_all.at[z], lat_all.at[z])

    unit, _ = norm_parts(latents_ref[...])
    rows[own_rows:, :] = (unit * latent_gain).astype(bf16)

    load_a.wait()
    load_b.wait()

    def project_step(n, carry):
        at = pl.ds(pl.multiple_of(n * 2 * SPAN, 2 * SPAN), 2 * SPAN)
        keys[:, at] = dot(rows[...], w_a[:, at]).astype(bf16)
        values[:, at] = dot(rows[...], w_b[:, at]).astype(bf16)
        return carry

    lax.fori_loop(0, groups // 2, project_step, 0)
    load_b = load(w_down_ref.at[quarter], w_b, 6)
    load_a = load(w_up_ref.at[:, quarter], w_a, 7)

    settle(lat_flight)
    cot_flight = to_line(lambda p: cot_all.at[z], cot_all.at[z])
    unit, _ = norm_parts(lat_all[...].reshape(4 * own_lat, features))
    lat_normed[...] = (unit * latent_gain).astype(bf16)
    load_c.wait()
    for cols in halves(features):
        queries[:, cols] = (dot(lat_normed[...], w_c[:, cols]) * scale).astype(bf16)
    load_c = load(w_out_ref, w_c, 8)

    def to_plane(ref, at, number):
        copies = [
            copy_to(ref.at[at], ref.at[at], spread_sems, (number, k), (z, p))
            for k, p in enumerate((x_peer, y_peer, xy_peer, pair))
        ]
        for copy in copies:
            copy.start()
        return copies

    def to_pair(ref, low, number):
        copies = []
        for k, p in enumerate((x_peer, y_peer, xy_peer)):
            at = pl.ds(pl.multiple_of(p * 128 + low, 64), 64)
            copies.append(copy_to(ref.at[at], ref.at[at], spread_sems, (number, 4 + k), (z, pair)))
        for copy in copies:
            copy.start()
        return copies

    blank = jnp.zeros((64, 128), f32)

    def place_blocks(dest, source, side, spread=True):
        for j in range(features // 128):
            tile = source[:, 128 * j : 128 * j + 128].astype(f32)
            tile = jnp.concatenate([blank, tile] if side else [tile, blank], axis=0)
            tile = tile.T.astype(bf16)
            for piece in range(8):
                row = 128 * j + 16 * piece
                if spread:
                    block, off = row // 48, row % 48
                    owner, at = block % 8, (block // 8) * 48 + off
                else:
                    owner, at = row // 192, row % 192
                part = tile[16 * piece : 16 * piece + 16, :]
                if side:
                    dest[owner, at : at + 16, :] += part
                else:
                    dest[owner, at : at + 16, :] = part

    def spread_blocks(source, dest, number):
        slot = pl.ds(pl.multiple_of(d * 128, 128), 128)
        copies = [
            copy_to(source.at[p], dest.at[:, slot], block_sems, (number, k), (z, p))
            for k, p in enumerate(others)
        ]
        for copy in copies:
            copy.start()
        dest[:, slot] = source[d]
        return copies

    def sides(ref):
        lane = lax.broadcasted_iota(jnp.int32, ref.shape, 1) % 128
        left = ref[...]
        none = jnp.zeros_like(left)
        return jnp.where(lane < 64, left, none), jnp.where(lane >= 64, left, none)

    masks = head_masks(4 * own_lat)
    lane = lax.broadcasted_iota(jnp.int32, (4 * own_lat, 128), 1)
    top_tile = jnp.zeros((4 * own_lat, 128), f32)
    sum_tile = jnp.ones((4 * own_lat, 128), f32)
    part_flight = []
    for g, cols in enumerate(spans(groups)):
        scores = dot_t(stacked(queries[:, cols], masks), keys[:, cols])
        scores = jnp.where(keep_row, scores, MASKED_SCORE)
        largest = jnp.max(scores, axis=-1, keepdims=True)
        expo = jnp.where(keep_row, jnp.exp(scores - largest), 0.0)
        total = jnp.sum(expo, axis=-1, keepdims=True)
        part = dot(expo.astype(bf16), values[:, cols])
        mixed = jnp.zeros((64, SPAN), f32)
        for h in range(GROUP):
            at = slice(64 * h, 64 * h + 64)
            mixed = mixed + jnp.where(masks[h], part[at], 0.0)
            top_tile = jnp.where(lane == GROUP * g + h, largest[at], top_tile)
            sum_tile = jnp.where(lane == GROUP * g + h, total[at], sum_tile)
        part_send[:, :, cols] = mixed.astype(bf16).reshape(4, own_lat, SPAN)
        if g % 2 == 1:
            wide = halves(features)[g // 2]
            part_flight += to_line(
                lambda p: part_send.at[p, :, wide], part_recv.at[z, :, wide]
            )
    stat_send[:, 0] = top_tile.reshape(4, own_lat, 128)
    stat_send[:, 1] = sum_tile.reshape(4, own_lat, 128)
    stat_flight = to_line(lambda p: stat_send.at[p], stat_recv.at[z])
    part_recv[z] = part_send[z]
    stat_recv[z] = stat_send[z]

    settle(cot_flight)
    own_cot = pl.ds(pl.multiple_of(d * 128, 128), 64)
    own_pre = pl.ds(pl.multiple_of(d * 128 + 64, 64), 64)
    rhs_all[own_cot, :] = cot_all[...].reshape(4 * own_lat, features)

    cot_plane = to_plane(rhs_all, own_cot, 0)
    load_b.wait()
    for cols in halves(features):
        act_grad[:, cols] = dot_t(cot_all[...].reshape(64, features), w_b[cols, :])
    for j in range(features // 128):
        place_transposed(
            rows_t, rows[:, 128 * j : 128 * j + 128].astype(f32).T.astype(bf16), 128 * j
        )

    settle(stat_flight)
    tops = stat_recv[:, 0]
    top = jnp.max(tops, axis=0)
    factor = jnp.exp(tops - top[None])
    denominator = jnp.sum(factor * stat_recv[:, 1], axis=0)
    log_total[...] = top + jnp.log(denominator)
    share = factor / denominator[None]
    settle(part_flight)
    own_masks = head_masks(own_lat)
    own_at = pl.ds(pl.multiple_of(z * own_lat, 16), own_lat)
    att_own = att_all.at[own_at]
    att_flight = []
    for g, cols in enumerate(spans(groups)):
        merged = jnp.zeros((own_lat, SPAN), f32)
        for j in range(4):
            spread = jnp.zeros((own_lat, SPAN), f32)
            for h in range(GROUP):
                n = GROUP * g + h
                spread = jnp.where(own_masks[h], share[j, :, n : n + 1], spread)
            merged = merged + spread * part_recv[j, :, cols].astype(f32)
        attended_f[:, cols] = merged
        att_own[:, cols] = merged.astype(bf16)
        if g % 2 == 1:
            wide = halves(features)[g // 2]
            att_flight.append(to_line(lambda p: att_own.at[:, wide], att_own.at[:, wide]))

    settle(cot_plane)
    cot_pair = to_pair(rhs_all, 0, 0)
    place_blocks(lat_lhs, lat_normed, 0)
    for n in range(8):
        rhs_branch[128 * n : 128 * n + 64, :] = jnp.zeros((64, SPAN), bf16)
        rhs_query[128 * n + 64 : 128 * n + 128, :] = jnp.zeros((64, SPAN), bf16)
    load_c.wait()
    load_a.wait()

    mid_all[...] = lat_all[...].reshape(64, features).astype(f32)
    for flight, deep in zip(att_flight, halves(features)):
        settle(flight)
        for cols in halves(features):
            mid_all[:, cols] += dot(att_all[:, deep], w_c[deep, cols])
    place_blocks(lat_lhs, att_all, 1)
    lat_blocks = spread_blocks(lat_lhs, lat_got, 1)
    unit, _ = norm_parts(mid_all[...])
    ffn_all[...] = (unit * ffn_gain).astype(bf16)

    for cols in halves(features):
        pre = dot(ffn_all[...], w_a[:, cols])
        cdf = 0.5 * (1.0 + lax.erf(pre * (0.5**0.5)))
        act_all[:, cols] = (pre * cdf).astype(bf16)
        density = jnp.exp(-0.5 * pre * pre) * (0.5 / jnp.pi) ** 0.5
        pre_all[:, cols] = (act_grad[:, cols] * (cdf + pre * density)).astype(bf16)
    fig_flight = []
    for wide in halves(features):
        part = dot_t(pre_all[...], w_a[wide, :])
        fig_f[:, :, wide] = part.reshape(4, own_lat, 2 * SPAN)
        fig_send[:, :, wide] = part.astype(bf16).reshape(4, own_lat, 2 * SPAN)
        fig_flight += to_line(lambda p: fig_send.at[p, :, wide], fig_recv.at[z, :, wide])
    load_a = load(w_key_ref, w_a, 9)
    rhs_all[own_pre, :] = pre_all[...]
    pre_plane = to_plane(rhs_all, own_pre, 1)
    for cols in halves(features):
        part = dot(act_all[...], w_b[:, cols])
        new_f[:, :, cols] = part.reshape(4, own_lat, 2 * SPAN)
        new_send[:, :, cols] = part.astype(bf16).reshape(4, own_lat, 2 * SPAN)
    flights = {}
    load_b = load(w_value_ref, w_b, 10)

    settle(fig_flight)
    flights["new"] = to_line(lambda p: new_send.at[p], new_recv.at[z])
    fig = fig_f[z]
    for p in peers:
        fig = fig + fig_recv[p].astype(f32)
    mid = mid_all[own_at, :]
    unit, inv = norm_parts(mid)
    gain_part[...] = jnp.zeros_like(gain_part)
    gain_part[2:3, :] = jnp.sum(fig * unit, axis=0, keepdims=True)
    mid_grad = cotangent_ref[...].astype(f32) + input_grad(fig, ffn_gain, unit, inv)
    mid_grad_own[...] = mid_grad
    branch_grad = mid_grad.astype(bf16)
    for n, cols in enumerate(spans(groups)):
        branch_send[n] = branch_grad[:, cols]
    branch_parts[z] = branch_send[z]
    own_lane = lax.broadcasted_iota(jnp.int32, (own_lat, 128), 1)
    delta = jnp.zeros((own_lat, 128), f32)
    grads = [dot_t(branch_grad, w_c[wide, :]).astype(bf16) for wide in halves(features)]
    for g, cols in enumerate(spans(groups)):
        grad = grads[g // 2][:, g % 2 * SPAN : g % 2 * SPAN + SPAN]
        og_all[g, z] = grad
        product = grad.astype(f32) * attended_f[:, cols]
        for h in range(GROUP):
            summed = jnp.sum(jnp.where(own_masks[h], product, 0.0), axis=-1, keepdims=True)
            delta = jnp.where(own_lane == GROUP * g + h, summed, delta)
    st_all[z, 0] = log_total[...]
    st_all[z, 1] = delta
    st_flight = to_line(lambda p: st_all.at[z], st_all.at[z])
    load_c = load(w_query_ref, w_c, 11)

    slots = {ch: ch % 6 for ch in range(2 * groups)}

    def weigh(g):
        cols = spans(groups)[g]
        right = jnp.concatenate([value_grad[:, cols], key_grad[:, cols]], axis=1)
        chunks = (2 * g, 2 * g + 1)
        for half in range(2):
            at = slice(half * 384, (half + 1) * 384)
            part = dot(rows_t[1 - c, at, :], right).astype(bf16)
            for n, ch in enumerate(chunks):
                pair_send[slots[ch], at, :] = part[:, n * SPAN : (n + 1) * SPAN]
        for ch in chunks:
            slot = slots[ch]
            copy = copy_to(pair_send.at[slot], pair_recv.at[slot], pair_sems, (ch,), (z, pair))
            copy.start()
            flights["pair", ch] = copy
        for half in range(2):
            at = slice(half * 384, (half + 1) * 384)
            part = dot(rows_t[c, at, :], right).astype(bf16)
            for n, ch in enumerate(chunks):
                own[ch, half] = part[:, n * SPAN : (n + 1) * SPAN].reshape(2, 192, SPAN)

    def add_to(view, block):
        view[...] = (view[...].astype(f32) + block.astype(f32)).astype(bf16)

    def pair_sum(ch):
        flights["pair", ch].wait()
        for bx in range(2):
            for by in range(2):
                at = bx * 384 + by * 192
                add_to(own.at[ch, bx, by], pair_recv[slots[ch], at : at + 192, :])
        if ch % 2 == 0:
            theirs, device = own.at[ch, 1 - x], x_peer
        else:
            theirs, device = own.at[ch, :, 1 - y], y_peer
        copy = copy_to(theirs, one_recv.at[ch], one_sems, (ch,), (z, device))
        copy.start()
        flights["one", ch] = copy

    def one_sum(ch):
        flights["one", ch].wait()
        for n in range(2):
            add_to(own.at[ch, x, n] if ch % 2 == 0 else own.at[ch, n, y], one_recv[ch, n])
        if ch % 2 == 0:
            theirs, device = own.at[ch, x, 1 - y], y_peer
        else:
            theirs, device = own.at[ch, 1 - x, y], x_peer
        copy = copy_to(theirs, two_recv.at[ch], two_sems, (ch,), (z, device))
        copy.start()
        flights["two", ch] = copy

    odd, high = z % 2, z // 2

    def line_rows(at, count):
        return pl.ds(pl.multiple_of(at, 16), count)

    def two_sum(ch):
        flights["two", ch].wait()
        add_to(own.at[ch, x, y], two_recv[ch])
        copy = copy_to(
            own.at[ch, x, y, line_rows((1 - odd) * 96, 96)],
            three_recv.at[ch],
            three_sems,
            (ch,),
            (z + 1 - 2 * odd, d),
        )
        copy.start()
        flights["three", ch] = copy

    def three_sum(ch):
        flights["three", ch].wait()
        add_to(own.at[ch, x, y, line_rows(odd * 96, 96)], three_recv[ch])
        copy = copy_to(
            own.at[ch, x, y, line_rows(odd * 96 + (1 - high) * 48, 48)],
            line_recv.at[ch, 1],
            last_sems,
            (ch,),
            ((z + 2) % 4, d),
        )
        copy.start()
        flights["line", ch] = copy
        line_recv[ch, 0] = own[ch, x, y, line_rows(odd * 96 + high * 48, 48), :]

    def line_end(ch):
        flights["line", ch].wait()
        store(line_recv.at[ch], line_out.at[ch])

    def rows_leave(g):
        flights["rows", g] = to_line(lambda p: og_all.at[g, z], og_all.at[g, z])

    def branch_leave(_):
        flights["parts"] = to_line(lambda p: branch_send.at[p], branch_parts.at[z])

    def blocks_leave(_):
        place_blocks(lhs_send, act_all, 0, spread=False)
        place_blocks(lhs_send, ffn_all, 1)
        flights["blocks"] = spread_blocks(lhs_send, lhs_recv, 0)

    def spread_stats(_):
        settle(st_flight)
        lane = lax.broadcasted_iota(jnp.int32, (64, 256), 1)
        row = lax.broadcasted_iota(jnp.int32, (64, 256), 0)
        for kind in range(2):
            tile = st_all[:, kind].reshape(64, 128)
            for g in range(groups):
                wide = jnp.zeros((64, 256), f32)
                for h in range(GROUP):
                    n = GROUP * g + h
                    wide = jnp.where(lane == row + 64 * h, tile[:, n : n + 1], wide)
                at = kind * groups + g
                stats[at : at + 1, :] = jnp.sum(wide, axis=0, keepdims=True)

    def attend_back(g):
        cols = spans(groups)[g]
        q_stack = stacked(queries[:, cols], masks)
        scores = dot_t(keys[:, cols], q_stack)
        keep = valid[:, 0:1] > 0.0
        exact = jnp.where(keep, jnp.exp(scores - stats[g : g + 1, :]), 0.0)
        settle(flights["rows", g])
        o_stack = stacked(og_all[g].reshape(64, SPAN), masks)
        prob_grad = dot_t(values[:, cols], o_stack)
        score_grad = (exact * (prob_grad - stats[4 + g : 5 + g, :])).astype(bf16)
        value_grad[:, cols] = dot(exact.astype(bf16), o_stack).astype(bf16)
        key_grad[:, cols] = dot(score_grad, q_stack).astype(bf16)
        q_part = outer_sum(score_grad, keys[:, cols])
        q_sum = jnp.zeros((64, SPAN), f32)
        for h in range(GROUP):
            q_sum = q_sum + jnp.where(masks[h], q_part[64 * h : 64 * h + 64], 0.0)
        query_parts[g] = q_sum
        query_send[g] = q_sum.astype(bf16)

    def forward_pre(_):
        settle(cot_pair)
        settle(pre_plane)
        settle(lat_blocks)
        flights["pre"] = to_pair(rhs_all, 64, 1)

    def new_rows(_):
        settle(flights["new"])
        new = mid_all[own_at, :] + new_f[z]
        for p in peers:
            new = new + new_recv[p].astype(f32)
        small_out[0] = new.astype(bf16)
        store(small_out.at[0], new_latents_out)

    def query_leave(_):
        flights["query"] = to_line(lambda p: query_send.at[p], query_recv.at[z])

    own_top = pl.ds(pl.multiple_of(d * 128, 128), 64)
    own_low = pl.ds(pl.multiple_of(d * 128 + 64, 64), 64)

    def branch_spread(_):
        settle(flights["parts"])
        rhs_branch[own_low, :] = branch_parts[...].reshape(64, SPAN)
        flights["branch"] = to_plane(rhs_branch, own_low, 3)

    def branch_pair(_):
        settle(flights["branch"])
        flights["branch"] = to_pair(rhs_branch, 64, 3)

    def place(n, part):
        place_send[n] = part.astype(bf16).reshape(4, 48, SPAN)
        flights["place", n] = to_line(lambda p: place_send.at[n, p], place_recv.at[n, z])
        place_recv[n, z] = place_send[n, z]

    def place_end(n):
        settle(flights["place", n])
        store(place_recv.at[n], place_out.at[n])

    def branch_weigh(_):
        settle(flights["branch"])
        place(0, dot(lat_got[...], rhs_branch[...]))

    def query_spread(_):
        settle(flights["query"])
        total = query_parts[z]
        for p in peers:
            total = total + query_recv[p].astype(f32)
        total = total.astype(bf16)
        back_send[...] = total.reshape(4, own_lat, SPAN)
        back_recv[z] = back_send[z]
        flights["back"] = to_line(lambda p: back_send.at[p], back_recv.at[z])
        rhs_query[own_top, :] = total
        flights["rows"] = to_plane(rhs_query, own_top, 4)

    def query_pair(_):
        settle(flights["rows"])
        flights["rows"] = to_pair(rhs_query, 0, 4)

    def query_weigh(_):
        settle(flights["rows"])
        place(1, scale * dot(lat_got[...], rhs_query[...]))

    def up_down(_):
        settle(flights["blocks"])
        settle(flights["pre"])
        act_left, ffn_left = sides(lhs_recv)
        for cols in halves(features):
            part = dot(ffn_left, rhs_all[:, cols])
            up_part[:, :, cols] = part.astype(bf16).reshape(4, 48, 2 * SPAN)
        flights["up"] = to_line(lambda p: up_part.at[p], up_recv.at[z])
        up_recv[z] = up_part[z]
        for cols in halves(features):
            down_part[:, cols] = dot(act_left, rhs_all[:, cols])
        store(down_part, down_out)

    def back_step(n, carry):
        at = pl.ds(pl.multiple_of(n * 2 * SPAN, 2 * SPAN), 2 * SPAN)
        rows_grad[:, at] = dot_t(key_grad[...], w_a[at, :]) + dot_t(value_grad[...], w_b[at, :])
        return carry

    def back_half(n):
        if n == 0:
            load_a.wait()
            load_b.wait()
        lax.fori_loop(n, n + 1, back_step, 0)

    def back_norm_step(n, total):
        at = pl.ds(pl.multiple_of(n * 64, 64), 64)
        unit, inv = norm_parts(media_ref[at, :])
        grad = rows_grad[at, :]
        rows[at, :] = input_grad(grad, gains[0:1, :], unit, inv).astype(bf16)
        return total + jnp.sum(grad * unit, axis=0, keepdims=True)

    def back_norm(_):
        gain_part[0:1, :] = lax.fori_loop(
            0, own_rows // 64, back_norm_step, jnp.zeros((1, features), f32)
        )
        store(rows.at[pl.ds(0, own_rows)], media_grad_out)

    def latent_rows(_):
        settle(flights["back"])
        load_c.wait()
        lat_grad = rows_grad[own_rows:, :]
        for n, cols in enumerate(spans(groups)):
            lat_grad = lat_grad + scale * dot_t(back_recv[n], w_c[:, cols])
        unit, inv = norm_parts(latents_ref[...])
        grad = input_grad(lat_grad, latent_gain, unit, inv)
        small_out[1] = (mid_grad_own[...] + grad).astype(bf16)
        store(small_out.at[1], latent_grad_out)
        gain_part[1:2, :] = jnp.sum(lat_grad * unit, axis=0, keepdims=True)
        for n, cols in enumerate(spans(groups)):
            gain_sum[n] = gain_part[:, cols]
        flights["gain"] = to_line(lambda p: gain_sum.at[p], gain_recv.at[z])

    def up_end(_):
        settle(flights["up"])
        store(up_recv, up_out)

    def gain_middle(_):
        settle(flights["gain"])
        total = gain_sum[z]
        for p in peers:
            total = total + gain_recv[p]
        gain_all[d] = total
        flights["spread"] = [
            copy_to(gain_all.at[d], gain_all.at[d], spread_sems, (2, k), (z, p))
            for k, p in enumerate(others)
        ]
        for item in flights["spread"]:
            item.start()

    def gain_end(_):
        settle(flights["spread"])
        gain_part[:, 0:SPAN] = jnp.sum(gain_all[...], axis=0)
        store(gain_part, gains_out)

    blocks_leave(0)
    rows_leave(0)
    spread_stats(0)
    rows_leave(1)
    rows_leave(3)
    branch_leave(0)
    attend_back(0)
    weigh(0)
    branch_spread(0)
    attend_back(3)
    rows_leave(2)
    attend_back(1)
    pair_sum(1)
    pair_sum(0)
    weigh(1)
    attend_back(2)
    query_leave(0)
    pair_sum(3)
    forward_pre(0)
    pair_sum(2)
    weigh(2)
    weigh(3)
    query_spread(0)
    one_sum(0)
    up_down(0)
    pair_sum(5)
    pair_sum(4)
    back_half(0)
    one_sum(1)
    query_pair(0)
    back_half(1)
    one_sum(3)
    branch_pair(0)
    one_sum(2)
    two_sum(0)
    query_weigh(0)
    two_sum(1)
    pair_sum(7)
    one_sum(5)
    branch_weigh(0)
    three_sum(0)
    two_sum(3)
    pair_sum(6)
    back_norm(0)
    three_sum(1)
    two_sum(2)
    new_rows(0)
    one_sum(4)
    line_end(0)
    latent_rows(0)
    two_sum(5)
    one_sum(7)
    one_sum(6)
    three_sum(3)
    three_sum(2)
    two_sum(4)
    three_sum(5)
    two_sum(7)
    gain_middle(0)
    two_sum(6)
    line_end(2)
    up_end(0)
    line_end(3)
    three_sum(4)
    three_sum(7)
    line_end(1)
    three_sum(6)
    gain_end(0)
    line_end(5)
    place_end(0)
    place_end(1)
    line_end(4)
    line_end(7)
    line_end(6)
    settle(stores)


def finish_kernel(
    new_in,
    media_in,
    latent_in,
    line_in,
    place_in,
    up_in,
    down_in,
    gains_in,
    new_out,
    media_out,
    latent_out,
    query_out,
    key_out,
    value_out,
    out_out,
    up_out,
    down_out,
    media_gain_out,
    latent_gain_out,
    ffn_gain_out,
    new_room,
    media_room,
    latent_room,
    down_room,
    line_room,
    place_room,
    up_room,
    gains_room,
    squares,
    up_wide,
    in_sems,
    out_sems,
):
    f32 = jnp.float32
    rooms = [line_room, media_room, down_room, up_room, new_room, latent_room, gains_room]
    sources = [line_in, media_in, down_in, up_in, new_in, latent_in, gains_in]
    rooms.append(place_room)
    sources.append(place_in)
    arrivals = [
        pltpu.make_async_copy(src, dst, in_sems.at[n])
        for n, (src, dst) in enumerate(zip(sources, rooms))
    ]
    for copy in arrivals[1:3] + arrivals[:1] + arrivals[7:] + arrivals[3:7]:
        copy.start()
    leaving = []

    def leave(src, dst):
        copy = pltpu.make_async_copy(src, dst, out_sems.at[len(leaving)])
        copy.start()
        leaving.append(copy)

    arrivals[1].wait()
    leave(media_room, media_out)
    arrivals[2].wait()
    leave(down_room, down_out)
    arrivals[0].wait()
    arrivals[7].wait()
    for n, cols in enumerate(spans(4)):
        squares[0, :, cols] = place_room[1, n].astype(f32)
        squares[1, :, cols] = jnp.sum(line_room[2 * n + 1].astype(f32), axis=0)
        squares[2, :, cols] = jnp.sum(line_room[2 * n].astype(f32), axis=0)
        squares[3, :, cols] = place_room[0, n].astype(f32)
    for n, dst in enumerate((query_out, key_out, value_out, out_out)):
        leave(squares.at[n], dst)
    arrivals[3].wait()
    features = up_in.shape[2]
    for n in range(4):
        up_wide[:, n * features : (n + 1) * features] = up_room[n].astype(f32)
    leave(up_wide, up_out)
    arrivals[4].wait()
    leave(new_room, new_out)
    arrivals[5].wait()
    leave(latent_room, latent_out)
    arrivals[6].wait()
    share = query_out.shape[0]
    start = lax.axis_index("dp") * share
    base = pl.multiple_of((start // 128) * 128, 128)
    window = gains_room[:, pl.ds(base, 256)]
    window = pltpu.roll(window, (256 - start % 128) % 256, 1)
    media_gain_out[...] = window[0, :share]
    latent_gain_out[...] = window[1, :share]
    ffn_gain_out[...] = window[2, :share]
    settle(leaving)


def layer(operands, own_rows, own_lat, features):
    bf16, f32 = jnp.bfloat16, jnp.float32
    count = own_rows + own_lat
    lat_rows = 4 * own_lat
    share = features // 32
    vmem = pl.BlockSpec(memory_space=pltpu.VMEM)
    smem = pl.BlockSpec(memory_space=pltpu.SMEM)
    anyway = pl.BlockSpec(memory_space=pl.ANY)

    def array(kind, *shape):
        return jax.ShapeDtypeStruct(shape, kind)

    def room(kind, *shape):
        return pltpu.VMEM(shape, kind)

    def dma(*shape):
        return pltpu.SemaphoreType.DMA(shape)

    outs = (
        array(bf16, own_lat, features),
        array(bf16, own_rows, features),
        array(bf16, own_lat, features),
        array(bf16, 8, 2, share, SPAN),
        array(bf16, 2, 4, share, SPAN),
        array(bf16, 4, share, features),
        array(f32, 4 * share, features),
        array(f32, 8, features),
    )
    scratch = dict(
        media_ref=room(bf16, own_rows, features),
        latents_ref=room(bf16, own_lat, features),
        cotangent_ref=room(bf16, own_lat, features),
        mask_ref=room(jnp.int32, 1, 4 * own_rows),
        gains=room(f32, 8, features),
        w_a=room(bf16, features, features),
        w_b=room(bf16, features, features),
        w_c=room(bf16, features, features),
        rows=room(bf16, count, features),
        keys=room(bf16, count, features),
        values=room(bf16, count, features),
        queries=room(bf16, lat_rows, features),
        stats=room(f32, 8, 256),
        valid=room(f32, count, 128),
        lat_normed=room(bf16, lat_rows, features),
        lat_all=room(bf16, 4, own_lat, features),
        cot_all=room(bf16, 4, own_lat, features),
        att_all=room(bf16, lat_rows, features),
        part_send=room(bf16, 4, own_lat, features),
        part_recv=room(bf16, 4, own_lat, features),
        stat_send=room(f32, 4, 2, own_lat, 128),
        stat_recv=room(f32, 4, 2, own_lat, 128),
        attended_f=room(f32, own_lat, features),
        log_total=room(f32, own_lat, 128),
        mid_all=room(f32, lat_rows, features),
        act_grad=room(f32, lat_rows, features),
        act_all=room(bf16, lat_rows, features),
        pre_all=room(bf16, lat_rows, features),
        ffn_all=room(bf16, lat_rows, features),
        fig_f=room(f32, 4, own_lat, features),
        fig_send=room(bf16, 4, own_lat, features),
        fig_recv=room(bf16, 4, own_lat, features),
        new_f=room(f32, 4, own_lat, features),
        new_send=room(bf16, 4, own_lat, features),
        new_recv=room(bf16, 4, own_lat, features),
        mid_grad_own=room(f32, own_lat, features),
        rhs_all=room(bf16, 1024, features),
        lhs_send=room(bf16, 8, 4 * share, 128),
        lhs_recv=room(bf16, 4 * share, 1024),
        og_all=room(bf16, 4, 4, own_lat, SPAN),
        st_all=room(f32, 4, 2, own_lat, 128),
        branch_send=room(bf16, 4, own_lat, SPAN),
        branch_parts=room(bf16, 4, own_lat, SPAN),
        small_out=room(bf16, 2, own_lat, features),
        down_part=room(f32, 4 * share, features),
        up_part=room(bf16, 4, share, features),
        up_recv=room(bf16, 4, share, features),
        rows_t=room(bf16, 2, features // 2, count),
        lat_lhs=room(bf16, 8, 4 * share, 128),
        lat_got=room(bf16, 4 * share, 1024),
        rhs_branch=room(bf16, 1024, SPAN),
        rhs_query=room(bf16, 1024, SPAN),
        place_send=room(bf16, 2, 4, share, SPAN),
        place_recv=room(bf16, 2, 4, share, SPAN),
        three_recv=room(bf16, 8, 96, SPAN),
        key_grad=room(bf16, count, features),
        value_grad=room(bf16, count, features),
        rows_grad=room(f32, count, features),
        query_parts=room(f32, 4, lat_rows, SPAN),
        query_send=room(bf16, 4, lat_rows, SPAN),
        query_recv=room(bf16, 4, lat_rows, SPAN),
        back_send=room(bf16, 4, own_lat, SPAN),
        back_recv=room(bf16, 4, own_lat, SPAN),
        pair_send=room(bf16, 6, 768, SPAN),
        pair_recv=room(bf16, 6, 768, SPAN),
        own=room(bf16, 8, 2, 2, 192, SPAN),
        one_recv=room(bf16, 8, 2, 192, SPAN),
        two_recv=room(bf16, 8, 192, SPAN),
        line_recv=room(bf16, 8, 2, share, SPAN),
        gain_part=room(f32, 8, features),
        gain_recv=room(f32, 4, 8, SPAN),
        gain_sum=room(f32, 4, 8, SPAN),
        gain_all=room(f32, 8, 8, SPAN),
        load_sems=dma(16),
        store_sems=dma(16),
        line_sems=dma(2, 24, 3),
        spread_sems=dma(2, 5, 7),
        block_sems=dma(2, 2, 7),
        pair_sems=dma(2, 8),
        one_sems=dma(2, 8),
        two_sems=dma(2, 8),
        three_sems=dma(2, 8),
        last_sems=dma(2, 8),
    )
    staged = pl.pallas_call(
        layer_kernel,
        out_shape=outs,
        in_specs=[anyway] * 4 + [smem] + [anyway] * 9,
        out_specs=(anyway,) * len(outs),
        scratch_shapes=tuple(scratch.values()),
        compiler_params=pltpu.CompilerParams(
            collective_id=0, has_side_effects=True, vmem_limit_bytes=63 * 1024 * 1024
        ),
    )(*operands)
    square = array(f32, share, features)
    return pl.pallas_call(
        finish_kernel,
        out_shape=outs[:3]
        + (square,) * 4
        + (array(f32, share, 4 * features), outs[6])
        + (array(f32, share),) * 3,
        in_specs=[anyway] * 8,
        out_specs=(anyway,) * 9 + (vmem,) * 3,
        scratch_shapes=[
            room(bf16, own_lat, features),
            room(bf16, own_rows, features),
            room(bf16, own_lat, features),
            room(f32, 4 * share, features),
            room(bf16, 8, 2, share, SPAN),
            room(bf16, 2, 4, share, SPAN),
            room(bf16, 4, share, features),
            room(f32, 8, features),
            room(f32, 4, share, features),
            room(f32, share, 4 * features),
            dma(8),
            dma(9),
        ],
        compiler_params=pltpu.CompilerParams(vmem_limit_bytes=63 * 1024 * 1024),
    )(*staged)


def spread_body(
    media,
    latents,
    frame_counts,
    media_mask,
    media_gain,
    latent_gain,
    ffn_gain,
    w_query,
    w_key,
    w_value,
    w_out,
    w_up,
    w_down,
    cotangent,
):
    _, own_rows, features = media.shape
    own_lat = latents.shape[1]
    seq_parts = lax.axis_size("seq")
    seq_index = lax.axis_index("seq")
    device_count = seq_parts * lax.axis_size("dp")
    both = ("seq", "dp")
    heads = features // HEAD_DIM
    score_scale = HEAD_DIM ** (-0.5)
    bf16 = jnp.bfloat16

    media, latents, cotangent = media[0], latents[0], cotangent[0]
    own_mask = lax.dynamic_slice_in_dim(media_mask[0], seq_index * own_rows, own_rows, 0)
    row_frame = (seq_index * own_rows + jnp.arange(own_rows, dtype=jnp.int32)) // PATCH
    own_valid = (own_mask > 0) & (row_frame < frame_counts[0])
    valid = jnp.concatenate([own_valid, jnp.ones((own_lat,), jnp.bool_)])[None, None, :]

    all_cotangent = lax.all_gather(cotangent, both, axis=0, tiled=True)

    latents_f = latents.astype(jnp.float32)
    latent_unit, latent_inv = normalize(latents_f)
    latent_normed = (latent_unit * latent_gain).astype(bf16)
    own_queries = (dot(latent_normed, w_query) * score_scale).astype(bf16)
    queries = lax.all_gather(own_queries, "seq", axis=0, tiled=True)

    media_unit, media_inv = normalize(media.astype(jnp.float32))
    media_normed = (media_unit * media_gain).astype(bf16)
    rows = jnp.concatenate([media_normed, latent_normed], axis=0)
    keys = dot(rows, w_key).astype(bf16)
    values = dot(rows, w_value).astype(bf16)

    scores = jnp.where(valid, head_products(queries, keys), MASKED_SCORE)
    largest = jnp.max(scores, axis=-1)
    expo = jnp.where(valid, jnp.exp(scores - largest[..., None]), 0.0)
    total = jnp.sum(expo, axis=-1)
    part = weighted(expo.astype(bf16), values)
    packed = jnp.concatenate([part, largest.T, total.T], axis=1)
    packed = lax.all_to_all(packed, "seq", split_axis=0, concat_axis=0, tiled=True)
    packed = packed.reshape(seq_parts, own_lat, -1)
    parts = packed[..., :features]
    maxima = packed[..., features : features + heads]
    totals = packed[..., features + heads :]
    top = jnp.max(maxima, axis=0)
    factor = jnp.exp(maxima - top)
    denominator = jnp.sum(factor * totals, axis=0)
    log_total = top + jnp.log(denominator)
    share = jnp.repeat(factor / denominator, HEAD_DIM, axis=-1)
    attended_f = jnp.sum(parts * share, axis=0)
    attended = attended_f.astype(bf16)

    mid = latents_f + dot(attended, w_out)
    mid_unit, mid_inv = normalize(mid)
    ffn_in = (mid_unit * ffn_gain).astype(bf16)
    pre = dot(ffn_in, w_up)
    act = gelu_exact(pre).astype(bf16)
    new_latents = (mid + dot(act, w_down)).astype(bf16)
    act_grad = dot_t(cotangent, w_down)
    pre_grad = jax.vjp(gelu_exact, pre)[1](act_grad)[0].astype(bf16)
    all_pre_grad = lax.all_gather(pre_grad, both, axis=0, tiled=True)
    ffn_in_grad = dot_t(pre_grad, w_up)
    mid_back, grad_ffn_gain = norm_back(ffn_in_grad, ffn_gain, mid_unit, mid_inv)
    mid_grad = cotangent.astype(jnp.float32) + mid_back
    branch_grad = mid_grad.astype(bf16)
    all_branch = lax.all_gather(branch_grad, both, axis=0, tiled=True)
    attended_grad = dot_t(branch_grad, w_out).astype(bf16)
    own_delta = jnp.sum(
        split_heads(attended_f * attended_grad.astype(jnp.float32)), axis=-1
    )
    out_grad = lax.all_gather(attended_grad, "seq", axis=0, tiled=True)
    stats = lax.all_gather(
        jnp.concatenate([log_total, own_delta], axis=1), "seq", axis=0, tiled=True
    )
    lse = stats[:, :heads].T[..., None]
    delta = stats[:, heads:].T[..., None]

    exact = jnp.where(valid, jnp.exp(scores - lse), 0.0)
    score_grad = (exact * (head_products(out_grad, values) - delta)).astype(bf16)
    value_grad = transposed(exact.astype(bf16), out_grad).astype(bf16)
    key_grad = transposed(score_grad, queries).astype(bf16)
    query_part = weighted(score_grad, keys)
    query_grad = lax.psum_scatter(
        query_part, "seq", scatter_dimension=0, tiled=True
    ).astype(bf16)
    all_query_grad = lax.all_gather(query_grad, both, axis=0, tiled=True)
    part_value = outer_sum(rows, value_grad).astype(bf16)
    part_key = outer_sum(rows, key_grad).astype(bf16)
    sum_value = lax.psum_scatter(part_value, both, scatter_dimension=0, tiled=True)
    sum_key = lax.psum_scatter(part_key, both, scatter_dimension=0, tiled=True)

    rows_grad = dot_t(key_grad, w_key) + dot_t(value_grad, w_value)
    media_back, grad_media_gain = norm_back(
        rows_grad[:own_rows], media_gain, media_unit, media_inv
    )
    media_grad = media_back.astype(bf16)
    latent_normed_grad = rows_grad[own_rows:] + dot_t(query_grad, w_query) * score_scale
    latent_back, grad_latent_gain = norm_back(
        latent_normed_grad, latent_gain, latent_unit, latent_inv
    )
    latent_grad = (mid_grad + latent_back).astype(bf16)

    def by_owner(tensor):
        return tensor.reshape(tensor.shape[0], device_count, -1)

    sent = jnp.concatenate(
        [by_owner(latent_normed), by_owner(attended), by_owner(ffn_in), by_owner(act)], axis=2
    )
    got = lax.all_to_all(sent, both, split_axis=1, concat_axis=0, tiled=True)
    got = got.reshape(-1, got.shape[-1])
    block = features // device_count
    grad_query = outer_sum(got[:, :block], all_query_grad) * score_scale
    grad_out = outer_sum(got[:, block : 2 * block], all_branch)
    grad_up = outer_sum(got[:, 2 * block : 3 * block], all_pre_grad)
    grad_down = outer_sum(got[:, 3 * block :], all_cotangent)

    gains = jnp.stack([grad_media_gain, grad_latent_gain, grad_ffn_gain])
    gains = by_owner(gains).transpose(1, 0, 2).reshape(device_count, -1)
    gains = lax.all_to_all(gains, both, split_axis=0, concat_axis=0, tiled=True)
    gains = jnp.sum(gains.reshape(device_count, 3, -1), axis=0)
    return (
        new_latents[None],
        media_grad[None],
        latent_grad[None],
        grad_query,
        sum_key.astype(jnp.float32),
        sum_value.astype(jnp.float32),
        grad_out,
        grad_up,
        grad_down,
        gains[0],
        gains[1],
        gains[2],
    )


def body(
    media,
    latents,
    frame_counts,
    media_mask,
    media_gain,
    latent_gain,
    ffn_gain,
    w_query,
    w_key,
    w_value,
    w_out,
    w_up,
    w_down,
    cotangent,
):
    _, own_rows, features = media.shape
    own_lat = latents.shape[1]
    seq_parts, dp_parts = lax.axis_size("seq"), lax.axis_size("dp")
    if (seq_parts, dp_parts, own_lat, features) != (4, 8, 16, 4 * SPAN):
        return spread_body(
            media,
            latents,
            frame_counts,
            media_mask,
            media_gain,
            latent_gain,
            ffn_gain,
            w_query,
            w_key,
            w_value,
            w_out,
            w_up,
            w_down,
            cotangent,
        )
    (
        new_latents,
        media_grad,
        latent_grad,
        grad_query,
        grad_key,
        grad_value,
        grad_out,
        grad_up,
        grad_down,
        media_gain_grad,
        latent_gain_grad,
        ffn_gain_grad,
    ) = layer(
        (
            media[0],
            latents[0],
            cotangent[0],
            media_mask,
            frame_counts,
            media_gain,
            latent_gain,
            ffn_gain,
            w_query,
            w_key,
            w_value,
            w_out,
            w_up,
            w_down,
        ),
        own_rows,
        own_lat,
        features,
    )
    return (
        new_latents[None],
        media_grad[None],
        latent_grad[None],
        grad_query,
        grad_key,
        grad_value,
        grad_out,
        grad_up,
        grad_down,
        media_gain_grad,
        latent_gain_grad,
        ffn_gain_grad,
    )


def solution(mesh):
    return jax.shard_map(
        body,
        mesh=mesh,
        in_specs=(
            P("dp", "seq", None),
            P("dp", "seq", None),
            P("dp"),
            P("dp", None),
            P(),
            P(),
            P(),
            P(),
            P(),
            P(),
            P(),
            P(),
            P(),
            P("dp", "seq", None),
        ),
        out_specs=(
            P("dp", "seq", None),
            P("dp", "seq", None),
            P("dp", "seq", None),
            P(("seq", "dp"), None),
            P(("seq", "dp"), None),
            P(("seq", "dp"), None),
            P(("seq", "dp"), None),
            P(("seq", "dp"), None),
            P(("seq", "dp"), None),
            P(("seq", "dp")),
            P(("seq", "dp")),
            P(("seq", "dp")),
        ),
        check_vma=False,
    )
```
